32 devices in a mesh: seq: 4 (over z), dp: 8 (over y, x, core).
Axes of the slice: x: 2, y: 2, z: 4, core: 2. Of those that a mesh axis runs over, the one named last changes fastest.
Arguments:
- tokens: bfloat16 [16384, 512], P(('seq', 'dp')), may hold values from -6 to 6
- cotangent: bfloat16 [16384, 512], P(('seq', 'dp')), may hold values from -6 to 6
- deal: int32 [32, 8], P(('seq', 'dp')), may hold values from 0 to 7, each once within a row
- lengths: int32 [8, 3], P('dp'), may hold values from 1 to 1024, 2048 in all within a row
- buckets: int32 [1024], replicated, may hold values from 0 to 31, as said below
- ln1_gain: bfloat16 [512], P('dp'), may hold values from 0.5 to 1.5
- ln1_bias: bfloat16 [512], P('dp'), may hold values from -2 to 2
- w_qkv: bfloat16 [512, 1536], P('dp'), may hold values from -0.25 to 0.25
- w_out: bfloat16 [512, 512], P('dp'), may hold values from -0.75 to 0.75
- rel_bias: bfloat16 [32, 8], P('dp'), may hold values from -4 to 4
- ln2_gain: bfloat16 [512], P('dp'), may hold values from 0.5 to 1.5
- ln2_bias: bfloat16 [512], P('dp'), may hold values from -2 to 2
- w_up: bfloat16 [512, 2048], P('dp'), may hold values from -0.25 to 0.25
- w_down: bfloat16 [2048, 512], P('dp'), may hold values from -0.125 to 0.125
Outputs:
- output: bfloat16 [16384, 512], P(('seq', 'dp'))
- grad_tokens: bfloat16 [16384, 512], P(('seq', 'dp'))
- grad_ln1_gain: float32 [512], P('dp')
- grad_ln1_bias: float32 [512], P('dp')
- grad_w_qkv: float32 [512, 1536], P('dp')
- grad_w_out: float32 [512, 512], P('dp')
- grad_rel_bias: float32 [32, 8], P('dp')
- grad_ln2_gain: float32 [512], P('dp')
- grad_ln2_bias: float32 [512], P('dp')
- grad_w_up: float32 [512, 2048], P('dp')
- grad_w_down: float32 [2048, 512], P('dp')
The draws below stay inside these ranges and needn't reach their ends.
Inputs may be any that keep to these rules, and one draw needn't show every extreme that they name: `deal`: each row lists every group once. Each group's 3 lengths sum to 2048, and the longest of each group is exactly 1024. Never falling with the distance; buckets[0] = 0 and buckets[1023] = 31.
All inputs are finite; a program needn't handle non-finite values.
Results may differ from the reference program's by a relative error of at most 0.02.
Values may be sent and summed in bfloat16 or wider, within the bound.
A program may use at most 192 MiB of HBM per device.

```python
import math
import jax
import jax.numpy as jnp
import numpy as np
from jax import lax

D = 512
H = 8
HD = 64
FF = 2048
NBK = 32
SEQS = 3
TOK_DEV = 512
TOKENS = 16384
MAXLEN = 1024
N_SEQ = 4
N_DP = 8


def draw_buckets(key, part):
    stride = max(2, MAXLEN // (2 * NBK))
    coin_flips = jax.random.randint(key, (MAXLEN,), 0, stride)
    places = jnp.arange(MAXLEN, dtype=jnp.int32)
    step_up = jnp.where((coin_flips == 0) & (places > 0), 1, 0).astype(jnp.int32)
    levels = jnp.minimum(jnp.cumsum(step_up).astype(jnp.int32), NBK - 1)
    return jnp.where(places == MAXLEN - 1, NBK - 1, levels).astype(jnp.int32)


def block_scale(key, extent, cuts, low, largest):
    loudness, own = 1.0, jax.random.fold_in(key, 6)
    for position, shards_of in cuts:
        steps = jnp.exp(jax.random.uniform(jax.random.fold_in(own, position), (shards_of,), jnp.float32, low / len(cuts), largest / len(cuts)))
        loudness = loudness * jnp.repeat(steps, extent[position] // shards_of).reshape([-1 if axis == position else 1 for axis in range(len(extent))])
    return loudness


def split_up(count, total, most, slope):
    portions = [(1 << 20) // math.isqrt(rank ** slope) + 1 for rank in range(2, count + 1)]
    surplus, holding = total - most - (count - 1), [1] * (count - 1)
    while surplus > 0:
        movable = [i for i in range(count - 1) if holding[i] < most]
        pool, left = sum([portions[i] for i in movable]), surplus
        for i in movable:
            more = min(most - holding[i], max(1, left * portions[i] // pool), surplus)
            holding[i] = holding[i] + more
            surplus = surplus - more
    return np.array([most] + holding)


def uneven_parts(key, count, total, reach, lean):
    if count == 2:
        one = jax.random.randint(key, (), max(1, total - reach), min(reach, total - 1) + 1)
        return jnp.stack([one, total - one])
    tallies = jnp.asarray(split_up(count, total, reach, lean), jnp.int32)
    couples = (count - 1) // 2
    source_of, sink = tallies[1:1 + 2 * couples:2], tallies[2:2 + 2 * couples:2]
    margin = jnp.minimum(source_of - 1, reach - sink)
    moved = jax.random.randint(jax.random.fold_in(key, 1), (couples,), 0, 1 << 20) % (margin + 1)
    tallies = tallies.at[1:1 + 2 * couples:2].set(source_of - moved).at[2:2 + 2 * couples:2].set(sink + moved)
    return tallies[jax.random.permutation(jax.random.fold_in(key, 2), count)]


def scatter_about(own_key, extent, width, bound, shards=(), held_as=jnp.bfloat16):
    values = width * jax.random.normal(own_key, extent, jnp.float32)
    if shards:
        values = values * block_scale(own_key, extent, shards, -0.22, 0.18)
    return jnp.clip(values, -bound, bound).astype(held_as)


def setup_inputs(seed: int = 0) -> dict:
    key_of = jax.random.split(jax.random.key(seed), 15)
    return {
        "tokens": scatter_about(key_of[0], (TOKENS, D), 1.0, 6.0, ((0, 32),)),
        "cotangent": scatter_about(key_of[1], (TOKENS, D), 1.0, 6.0, ((0, 32),)),
        "deal": jax.vmap(lambda own: jax.random.permutation(own, N_DP))(jax.random.split(key_of[2], (N_SEQ * N_DP))).reshape((N_SEQ * N_DP, N_DP)).astype(jnp.int32),
        "lengths": jax.vmap(lambda own: uneven_parts(own, SEQS, TOK_DEV * N_SEQ, MAXLEN, 2))(jax.random.split(key_of[3], N_DP)).reshape((N_DP, SEQS)).astype(jnp.int32),
        "buckets": draw_buckets(jax.random.fold_in(key_of[14], 71), 0),
        "ln1_gain": jnp.clip(1.0 + 0.1 * jax.random.normal(key_of[5], (D,), jnp.float32), 0.5, 1.5).astype(jnp.bfloat16),
        "ln1_bias": scatter_about(key_of[6], (D,), 0.3, 2.0, ((0, 8),)),
        "w_qkv": scatter_about(key_of[7], (D, 3 * D), D ** -0.5, 0.25, ((0, 8),)),
        "w_out": scatter_about(key_of[8], (D, D), (D // 8) ** -0.5, 0.75, ((0, 8),)),
        "rel_bias": scatter_about(key_of[9], (NBK, H), 1.0, 4.0, ((0, 8),)),
        "ln2_gain": jnp.clip(1.0 + 0.1 * jax.random.normal(key_of[10], (D,), jnp.float32), 0.5, 1.5).astype(jnp.bfloat16),
        "ln2_bias": scatter_about(key_of[11], (D,), 0.3, 2.0, ((0, 8),)),
        "w_up": scatter_about(key_of[12], (D, FF), D ** -0.5, 0.25, ((0, 8),)),
        "w_down": scatter_about(key_of[13], (FF, D), FF ** -0.5, 0.125, ((0, 8),)),
    }


@jax.custom_vjp
def low(v):
    return lax.optimization_barrier(v.astype(jnp.bfloat16)).astype(jnp.float32)

@jax.custom_vjp
def low_back(v):
    return v

def low_keep(v):
    return (low(v), None)

def low_pass(kept, grad):
    return (grad,)

def back_keep(v):
    return (v, None)

def back_low(kept, grad):
    return (low(grad),)
low.defvjp(low_keep, low_pass)
low_back.defvjp(back_keep, back_low)
HIGHEST = lax.Precision.HIGHEST

def norm_rows(values, gain_vec, bias_vec):
    average = lax.optimization_barrier(jnp.mean(values, axis=-1, keepdims=True))
    centred = values - average
    variance = lax.optimization_barrier(jnp.mean(centred * centred, axis=-1, keepdims=True))
    return centred * lax.rsqrt(variance + 1e-05) * gain_vec + bias_vec

def gelu_exact(values):
    return jax.nn.gelu(values, approximate=False)

def segment_of(lengths_row, total_rows):
    ends_at = jnp.cumsum(lengths_row).astype(jnp.int32)
    places = jnp.arange(total_rows, dtype=jnp.int32)
    return lax.optimization_barrier(jnp.sum((places[:, None] >= ends_at[None, :]).astype(jnp.int32), axis=1)).astype(jnp.int32)

def inverse_of(deal_rows):
    slot_count = deal_rows.shape[-1]
    places = jnp.arange(slot_count, dtype=jnp.int32)
    matches = (deal_rows[..., :, None] == places).astype(jnp.int32)
    return lax.optimization_barrier(jnp.sum(matches * places[:, None], axis=-2)).astype(jnp.int32)

def layer_forward(tokens_in, params, seg_ids, buckets):
    gain_one, bias_one, w_qkv, w_out, rel_bias, gain_two, bias_two, w_up, w_down = params
    group_tok = tokens_in.shape[0]
    rows_blk = min(512, group_tok)
    score_scale = HD ** (-0.5)
    bias_table = jnp.take(rel_bias, buckets, axis=0).T
    normed = low(norm_rows(tokens_in, gain_one, bias_one))
    projected = jnp.dot(normed, w_qkv, precision=HIGHEST)
    projected = low_back(low(projected)).reshape(group_tok, 3, H, HD)
    queries = projected[:, 0]
    keys_all = projected[:, 1]
    values_all = projected[:, 2]
    places = jnp.arange(group_tok, dtype=jnp.int32)

    def attend(first_row):
        q_block = lax.dynamic_slice_in_dim(queries, first_row, rows_blk, 0)
        row_ids = first_row + jnp.arange(rows_blk, dtype=jnp.int32)
        distance = row_ids[:, None] - places[None, :]
        bucket_at = jnp.clip(distance, 0, MAXLEN - 1)
        row_seg = lax.dynamic_slice_in_dim(seg_ids, first_row, rows_blk, 0)
        allowed = (row_seg[:, None] == seg_ids[None, :]) & (distance >= 0)
        raw_dot = jnp.einsum('qhd,khd->hqk', q_block, keys_all, precision=HIGHEST) * score_scale
        shifted = low_back(raw_dot + jnp.take(bias_table, bucket_at, axis=1))
        masked = jnp.where(allowed[None], shifted, -1e+30)
        attn_prob = low(jax.nn.softmax(masked, axis=-1))
        return jnp.einsum('hqk,khd->qhd', attn_prob, values_all, precision=HIGHEST)
    starts = jnp.arange(group_tok // rows_blk, dtype=jnp.int32) * rows_blk
    attended = lax.map(jax.checkpoint(attend), starts).reshape(group_tok, D)
    attended = low_back(low(attended))
    branch = low_back(jnp.dot(attended, w_out, precision=HIGHEST))
    residual = tokens_in + branch
    normed_two = low(norm_rows(residual, gain_two, bias_two))
    pre_act = low_back(jnp.dot(normed_two, w_up, precision=HIGHEST))
    active = low(gelu_exact(pre_act))
    return residual + jnp.dot(active, w_down, precision=HIGHEST)

def reference(tokens, cotangent, deal, lengths, buckets, ln1_gain, ln1_bias, w_qkv, w_out, rel_bias, ln2_gain, ln2_bias, w_up, w_down):
    group_tok = TOK_DEV * N_SEQ
    block_len = TOK_DEV // N_DP
    deal_rows = deal.reshape(N_SEQ, N_DP, N_DP)
    inverse = inverse_of(deal_rows)
    full_shape = (N_SEQ, N_DP, N_DP, block_len, D)

    def to_groups(array):
        pieces = array.reshape(full_shape)
        picks = jnp.broadcast_to(inverse[:, :, :, None, None], full_shape)
        chosen = jnp.take_along_axis(pieces, picks, axis=2)
        return chosen.transpose(2, 0, 1, 3, 4).reshape(N_DP, group_tok, D)

    def from_groups(array):
        returned = array.reshape(N_DP, N_SEQ, N_DP, block_len, D).transpose(1, 2, 0, 3, 4)
        picks = jnp.broadcast_to(deal_rows[:, :, :, None, None], full_shape)
        restored = jnp.take_along_axis(returned, picks, axis=2)
        return restored.reshape(N_SEQ * N_DP * TOK_DEV, D)
    dealt_in = to_groups(tokens.astype(jnp.float32))
    dealt_grad = to_groups(cotangent.astype(jnp.float32))

    def group_segments(lengths_row):
        return segment_of(lengths_row, group_tok)
    seg_all = jax.vmap(group_segments)(lengths)
    params = tuple((weight_arg.astype(jnp.float32) for weight_arg in (ln1_gain, ln1_bias, w_qkv, w_out, rel_bias, ln2_gain, ln2_bias, w_up, w_down)))

    def one_group(running, inputs):
        group_in, group_grad, group_seg = inputs

        def run_layer(tokens_arg, params_arg):
            return layer_forward(tokens_arg, params_arg, group_seg, buckets)
        result, pullback = jax.vjp(run_layer, group_in, params)
        grad_in, grad_params = pullback(group_grad)
        summed = tuple((so_far + addend for so_far, addend in zip(running, grad_params)))
        return (summed, (result, grad_in))
    zeros_init = tuple((jnp.zeros_like(weight_arg) for weight_arg in params))
    weight_grads, outcome = lax.scan(one_group, zeros_init, (dealt_in, dealt_grad, seg_all))
    output = from_groups(outcome[0]).astype(jnp.bfloat16)
    grad_tokens = from_groups(outcome[1]).astype(jnp.bfloat16)
    return (output, grad_tokens, weight_grads[0], weight_grads[1], weight_grads[2], weight_grads[3], weight_grads[4], weight_grads[5], weight_grads[6], weight_grads[7], weight_grads[8])
```

```python
import functools

import jax
import jax.numpy as jnp
from jax import lax
from jax.experimental import pallas as pl
from jax.experimental.pallas import tpu as pltpu
from jax.sharding import PartitionSpec as P

H = 8
HD = 64
NBK = 32
QB = 256
PAIR = 2 * HD
BIG = -1e30
F32 = jnp.float32
BF16 = jnp.bfloat16
VMEM_LIMIT = 60 * 1024 * 1024

NT = (((1,), (1,)), ((), ()))
NN = (((1,), (0,)), ((), ()))


def dot_nt(a, b):
    return lax.dot_general(a, b, NT, preferred_element_type=F32)


def dot_nn(a, b):
    return lax.dot_general(a, b, NN, preferred_element_type=F32)


def norm_rows(values, gain_vec, bias_vec):
    average = jnp.mean(values, axis=-1, keepdims=True)
    centred = values - average
    variance = jnp.mean(centred * centred, axis=-1, keepdims=True)
    return centred * lax.rsqrt(variance + 1e-05) * gain_vec + bias_vec


def gelu_exact(values):
    return jax.nn.gelu(values, approximate=False)


def toeplitz(row, width):
    return pltpu.roll(jnp.broadcast_to(row, (QB, width)), 0, 1, stride=1, stride_axis=0)


def attention_fwd_kernel(base_ref, q_ref, qx_ref, k_ref, kx_ref, v_ref, att_ref, lse_ref, bias, kaug, vaug, scores):
    rows = q_ref.shape[0]
    width = base_ref.shape[-1]
    tiles = width // QB
    lane_q = lax.broadcasted_iota(jnp.int32, (QB, PAIR), 1) < HD
    lane_k = lax.broadcasted_iota(jnp.int32, k_ref.shape, 1) < HD
    for h in range(2):
        mine_k = lane_k if h == 0 else jnp.logical_not(lane_k)
        mine_q = lane_q if h == 0 else jnp.logical_not(lane_q)
        bias[...] = toeplitz(base_ref[0, h : h + 1, :], width)
        kaug[...] = jnp.where(mine_k, k_ref[...], kx_ref[...])
        vaug[...] = jnp.where(mine_k, v_ref[...], jnp.ones_like(v_ref))
        for b in range(rows // QB):
            here = pl.ds(b * QB, QB)
            q_aug = jnp.where(mine_q, q_ref[here, :], qx_ref[here, :])
            top = None
            for j in range(tiles):
                cols = pl.ds(j * QB, QB)
                s = dot_nt(q_aug, kaug[pl.ds((b + j) * QB, QB), :]) + bias[:, cols]
                scores[:, cols] = s
                most = jnp.maximum(s[:, :128], s[:, 128:])
                top = most if top is None else jnp.maximum(top, most)
            top = jnp.max(top, axis=1, keepdims=True)
            acc = jnp.zeros((QB, PAIR), F32)
            for j in range(tiles):
                p = jnp.exp(scores[:, pl.ds(j * QB, QB)] - top).astype(BF16)
                acc = acc + dot_nn(p, vaug[pl.ds((b + j) * QB, QB), :])
            att = acc / pltpu.roll(acc, HD, 1)
            lse = top + jnp.log(acc)
            if h == 0:
                att_ref[here, :] = att.astype(BF16)
                lse_ref[here, :] = lse
            else:
                att_ref[here, :] = jnp.where(mine_q, att.astype(BF16), att_ref[here, :])
                lse_ref[here, :] = jnp.where(mine_q, lse_ref[here, :], lse)


def attention_bwd_kernel(
    base_ref, q_ref, qx_ref, k_ref, kx_ref, v_ref, att_ref, lse_ref, do_ref,
    dq_ref, dk_ref, dv_ref, dd_ref,
    bias, kaug, vaug, qaug, doaug, dsum, dkt, dvt,
):
    rows = q_ref.shape[0]
    width = base_ref.shape[-1]
    tiles = width // QB
    lane_q = lax.broadcasted_iota(jnp.int32, (rows, PAIR), 1)
    extra = lax.rem(lane_q, HD)
    lane_k = lax.broadcasted_iota(jnp.int32, k_ref.shape, 1) < HD
    swap = (
        (lax.broadcasted_iota(jnp.int32, (PAIR, PAIR), 0) < HD)
        != (lax.broadcasted_iota(jnp.int32, (PAIR, PAIR), 1) < HD)
    ).astype(BF16)
    prod = do_ref[...].astype(F32) * att_ref[...].astype(F32)
    prod_hi = prod.astype(BF16)
    prod_lo = (prod - prod_hi.astype(F32)).astype(BF16)
    delta = -(dot_nn(prod_hi, swap) + dot_nn(prod_lo, swap))
    delta_hi = delta.astype(BF16).astype(F32)
    lse = -lse_ref[...]
    lse_hi = lse.astype(BF16).astype(F32)
    lse_mid = (lse - lse_hi).astype(BF16).astype(F32)
    lse_lo = lse - lse_hi - lse_mid
    q_extra = jnp.where(
        extra == HD - 3, lse_hi, jnp.where(extra == HD - 2, lse_mid, jnp.where(extra == HD - 1, lse_lo, qx_ref[...].astype(F32)))
    ).astype(BF16)
    do_extra = jnp.where(extra == 0, delta_hi, jnp.where(extra == 1, delta - delta_hi, 0.0)).astype(BF16)
    dkt[...] = jnp.zeros_like(dkt)
    dvt[...] = jnp.zeros_like(dvt)
    for h in range(2):
        mine_k = lane_k if h == 0 else jnp.logical_not(lane_k)
        mine_q = (lane_q < HD) if h == 0 else (lane_q >= HD)
        bias[...] = toeplitz(base_ref[0, h : h + 1, :], width)
        kaug[...] = jnp.where(mine_k, k_ref[...], kx_ref[...])
        vaug[...] = jnp.where(mine_k, v_ref[...], jnp.ones_like(v_ref))
        qaug[...] = jnp.where(mine_q, q_ref[...], q_extra)
        doaug[...] = jnp.where(mine_q, do_ref[...], do_extra)
        feat = pl.ds(h * HD, HD)
        for b in range(rows // QB):
            here = pl.ds(b * QB, QB)
            q_t = q_ref[here, :].astype(F32).T[h * HD : (h + 1) * HD].astype(BF16)
            do_t = do_ref[here, :].astype(F32).T[h * HD : (h + 1) * HD].astype(BF16)
            dq = jnp.zeros((QB, PAIR), F32)
            for j in range(tiles):
                cols = pl.ds(j * QB, QB)
                keys = pl.ds((b + j) * QB, QB)
                p = jnp.exp(dot_nt(qaug[here, :], kaug[keys, :]) + bias[:, cols])
                ds = p * dot_nt(doaug[here, :], vaug[keys, :])
                ds_low = ds.astype(BF16)
                dvt[feat, keys] += dot_nn(do_t, p.astype(BF16))
                dkt[feat, keys] += dot_nn(q_t, ds_low)
                dq = dq + dot_nn(ds_low, k_ref[keys, :])
                if b == 0:
                    dsum[:, cols] = ds
                else:
                    dsum[:, cols] += ds
            dq = (dq * (HD**-0.5)).astype(BF16)
            if h == 0:
                dq_ref[here, :] = dq
            else:
                dq_ref[here, :] = jnp.where(mine_q[:QB], dq, dq_ref[here, :])
        left, half = dsum[...], QB // 2
        while half:
            left = left[:half] + pltpu.roll(left[half:], width - half, 1)
            half //= 2
        dd_ref[0, h : h + 1, :] = left
    dk_ref[...] = dkt[...].T.astype(BF16)
    dv_ref[...] = dvt[...].T.astype(BF16)


def column_block(rows):
    return pl.BlockSpec((rows, PAIR), lambda i: (0, i))


def whole_block(rows):
    return pl.BlockSpec((rows, PAIR), lambda i: (0, 0))


def attention_fwd(base, q, qx, k, kx, v):
    rows, width, window = q.shape[0], base.shape[-1], k.shape[0]
    return pl.pallas_call(
        attention_fwd_kernel,
        grid=(H // 2,),
        in_specs=[
            pl.BlockSpec((1, 2, width), lambda i: (i, 0, 0)),
            column_block(rows),
            whole_block(rows),
            column_block(window),
            whole_block(window),
            column_block(window),
        ],
        out_specs=[column_block(rows), column_block(rows)],
        out_shape=[jax.ShapeDtypeStruct(q.shape, BF16), jax.ShapeDtypeStruct(q.shape, F32)],
        scratch_shapes=[
            pltpu.VMEM((QB, width), F32),
            pltpu.VMEM((window, PAIR), BF16),
            pltpu.VMEM((window, PAIR), BF16),
            pltpu.VMEM((QB, width), F32),
        ],
        compiler_params=pltpu.CompilerParams(vmem_limit_bytes=VMEM_LIMIT),
        name="attention_fwd",
    )(base, q, qx, k, kx, v)


def attention_bwd(base, q, qx, k, kx, v, att, lse, do):
    rows, width, window = q.shape[0], base.shape[-1], k.shape[0]
    return pl.pallas_call(
        attention_bwd_kernel,
        grid=(H // 2,),
        in_specs=[
            pl.BlockSpec((1, 2, width), lambda i: (i, 0, 0)),
            column_block(rows),
            whole_block(rows),
            column_block(window),
            whole_block(window),
            column_block(window),
            column_block(rows),
            column_block(rows),
            column_block(rows),
        ],
        out_specs=[
            column_block(rows),
            column_block(window),
            column_block(window),
            pl.BlockSpec((1, 2, width), lambda i: (i, 0, 0)),
        ],
        out_shape=[
            jax.ShapeDtypeStruct(q.shape, BF16),
            jax.ShapeDtypeStruct(k.shape, BF16),
            jax.ShapeDtypeStruct(k.shape, BF16),
            jax.ShapeDtypeStruct(base.shape, F32),
        ],
        scratch_shapes=[
            pltpu.VMEM((QB, width), F32),
            pltpu.VMEM((window, PAIR), BF16),
            pltpu.VMEM((window, PAIR), BF16),
            pltpu.VMEM((rows, PAIR), BF16),
            pltpu.VMEM((rows, PAIR), BF16),
            pltpu.VMEM((QB, width), F32),
            pltpu.VMEM((PAIR, window), F32),
            pltpu.VMEM((PAIR, window), F32),
        ],
        compiler_params=pltpu.CompilerParams(vmem_limit_bytes=VMEM_LIMIT),
        name="attention_bwd",
    )(base, q, qx, k, kx, v, att, lse, do)


def copy_kernel(deal_ref, *refs):
    count = len(refs) // 2
    for i in range(count):
        refs[count + i][...] = refs[i][...]


def to_slots(deal_row, arrays):
    groups, length, width = arrays[0].shape
    spec_in = pl.BlockSpec((1, length, width), lambda g, deal: (g, 0, 0))
    spec_out = pl.BlockSpec((1, length, width), lambda g, deal: (deal[g], 0, 0))
    return pl.pallas_call(
        copy_kernel,
        grid_spec=pltpu.PrefetchScalarGridSpec(
            num_scalar_prefetch=1, grid=(groups,), in_specs=[spec_in] * len(arrays), out_specs=[spec_out] * len(arrays)
        ),
        out_shape=[jax.ShapeDtypeStruct(a.shape, a.dtype) for a in arrays],
        name="to_slots",
    )(deal_row, *arrays)


def from_slots(deal_row, arrays):
    groups, length, width = arrays[0].shape
    spec_out = pl.BlockSpec((1, length, width), lambda g, deal: (g, 0, 0))
    spec_in = pl.BlockSpec((1, length, width), lambda g, deal: (deal[g], 0, 0))
    return pl.pallas_call(
        copy_kernel,
        grid_spec=pltpu.PrefetchScalarGridSpec(
            num_scalar_prefetch=1, grid=(groups,), in_specs=[spec_in] * len(arrays), out_specs=[spec_out] * len(arrays)
        ),
        out_shape=[jax.ShapeDtypeStruct(a.shape, a.dtype) for a in arrays],
        name="from_slots",
    )(deal_row, *arrays)


def swap_slots(values):
    return lax.all_to_all(values, "dp", split_axis=0, concat_axis=0, tiled=True)


def shards(
    tokens,
    cotangent,
    deal,
    lengths,
    buckets,
    ln1_gain,
    ln1_bias,
    w_qkv,
    w_out,
    rel_bias,
    ln2_gain,
    ln2_bias,
    w_up,
    w_down,
):
    groups = lax.axis_size("dp")
    splits = lax.axis_size("seq")
    tok_dev, width = tokens.shape
    block_len = tok_dev // groups
    maxlen = buckets.shape[0]
    back = -(-maxlen // tok_dev)
    window = (back + 1) * tok_dev
    span = back * tok_dev + QB
    chunk = lax.axis_index("seq")
    deal_row = deal[0]
    shard_rows = ln1_gain.shape[0]

    small = jnp.concatenate([ln1_gain, ln1_bias, ln2_gain, ln2_bias, rel_bias.reshape(-1)])
    wqkv_full = lax.all_gather(w_qkv, "dp", axis=0, tiled=True)
    small_full = lax.all_gather(small, "dp", axis=0, tiled=False)
    wout_full = lax.all_gather(w_out, "dp", axis=0, tiled=True)
    wup_full = lax.all_gather(w_up, "dp", axis=0, tiled=True)
    wdown_full = lax.all_gather(w_down, "dp", axis=0, tiled=True)
    gains = small_full[:, : 4 * shard_rows].reshape(groups, 4, shard_rows).transpose(1, 0, 2).reshape(4, width)
    gain_one, bias_one, gain_two, bias_two = (gains[i].astype(F32) for i in range(4))
    rel_full = small_full[:, 4 * shard_rows :].reshape(NBK, H)

    pieces = (groups, block_len, width)
    slot_in, slot_grad = to_slots(deal_row, [tokens.reshape(pieces), cotangent.reshape(pieces)])
    dealt = swap_slots(jnp.stack([slot_in, slot_grad], axis=1))
    x_rows = dealt[:, 0].reshape(tok_dev, width).astype(F32)
    grad_out = dealt[:, 1].reshape(tok_dev, width)

    ends, so_far = [], 0
    for c in range(lengths.shape[1]):
        so_far = so_far + lengths[0, c]
        ends.append(so_far)
    lane = lax.rem(jnp.arange(PAIR, dtype=jnp.int32), HD)[None, :]
    key_pos = (chunk - back) * tok_dev + jnp.arange(window, dtype=jnp.int32)
    key_seg = sum((key_pos >= e).astype(jnp.int32) for e in ends)
    key_seg = jnp.where(key_pos < 0, len(ends), key_seg)[:, None]
    query_seg = key_seg[back * tok_dev :]
    kx = jnp.where((lane == key_seg) | (lane >= HD - 3), 1.0, 0.0).astype(BF16)
    qx = jnp.where((lane <= len(ends)) & (lane != query_seg), BIG, 0.0).astype(BF16)
    offset = jnp.arange(span, dtype=jnp.int32)
    distance = back * tok_dev - offset
    in_reach = (distance >= 0) & (distance < maxlen)
    table_bucket = jnp.concatenate(
        [jnp.zeros((back * tok_dev + 1 - maxlen,), jnp.int32), buckets[::-1], jnp.zeros((QB - 1,), jnp.int32)]
    )
    one_hot = ((table_bucket[:, None] == jnp.arange(NBK, dtype=jnp.int32)[None, :]) & in_reach[:, None]).astype(F32)
    base = jnp.einsum("cb,bh->hc", one_hot, rel_full.astype(F32), precision=lax.Precision.HIGHEST)
    base = jnp.where(in_reach[None], base, BIG).reshape(H // 2, 2, span)

    normed, norm_one_back = jax.vjp(norm_rows, x_rows, gain_one, bias_one)
    normed_low = normed.astype(BF16)
    earlier = [
        lax.ppermute(normed_low, "seq", [(i, i + step) for i in range(splits - step)]) for step in range(back, 0, -1)
    ]
    scale = HD**-0.5
    own_qkv = jnp.dot(normed_low, wqkv_full, preferred_element_type=F32).astype(BF16)
    rows_before = jnp.concatenate(earlier, axis=0)
    kv_before = jnp.dot(rows_before, wqkv_full[:, width:], preferred_element_type=F32).astype(BF16)
    queries = own_qkv[:, :width] * jnp.asarray(scale, BF16)
    keys_all = jnp.concatenate([kv_before[:, :width], own_qkv[:, width : 2 * width]], axis=0)
    values_all = jnp.concatenate([kv_before[:, width:], own_qkv[:, 2 * width :]], axis=0)
    attended, lse = attention_fwd(base, queries, qx, keys_all, kx, values_all)
    residual = x_rows + jnp.dot(attended, wout_full, preferred_element_type=F32)
    normed_two, norm_two_back = jax.vjp(norm_rows, residual, gain_two, bias_two)
    normed_two_low = normed_two.astype(BF16)
    pre_act = jnp.dot(normed_two_low, wup_full, preferred_element_type=F32)
    active, gelu_back = jax.vjp(gelu_exact, pre_act)
    active_low = active.astype(BF16)
    output_rows = (residual + jnp.dot(active_low, wdown_full, preferred_element_type=F32)).astype(BF16)

    grad_wdown = jnp.einsum("tf,td->fd", active_low, grad_out, preferred_element_type=F32)
    grad_active = jnp.einsum("td,fd->tf", grad_out, wdown_full, preferred_element_type=F32)
    grad_pre = gelu_back(grad_active)[0].astype(BF16)
    grad_wup = jnp.einsum("td,tf->df", normed_two_low, grad_pre, preferred_element_type=F32)
    grad_norm_two = jnp.einsum("tf,df->td", grad_pre, wup_full, preferred_element_type=F32)
    resid_part, grad_gain_two, grad_bias_two = norm_two_back(grad_norm_two)
    grad_resid = grad_out.astype(F32) + resid_part
    branch_grad = grad_resid.astype(BF16)
    grad_wout = jnp.einsum("td,te->de", attended, branch_grad, preferred_element_type=F32)
    grad_att = jnp.einsum("te,de->td", branch_grad, wout_full, preferred_element_type=F32).astype(BF16)
    dq, dk, dv, dd = attention_bwd(base, queries, qx, keys_all, kx, values_all, attended, lse, grad_att)
    grad_kv = jnp.concatenate([dk, dv], axis=1)
    part_before = jnp.einsum(
        "tc,dc->td", grad_kv[: back * tok_dev], wqkv_full[:, width:], preferred_element_type=F32
    ).astype(BF16)
    returned = [
        lax.ppermute(
            part_before[(back - step) * tok_dev : (back - step + 1) * tok_dev],
            "seq",
            [(i + step, i) for i in range(splits - step)],
        )
        for step in range(back, 0, -1)
    ]
    grad_own = jnp.concatenate([dq, grad_kv[back * tok_dev :]], axis=1)
    grad_normed = jnp.einsum("tc,dc->td", grad_own, wqkv_full, preferred_element_type=F32)
    all_rows = jnp.concatenate([rows_before, normed_low], axis=0)
    grad_wq = jnp.einsum("td,tc->dc", normed_low, dq, preferred_element_type=F32)
    grad_wkv = jnp.einsum("td,tc->dc", all_rows, grad_kv, preferred_element_type=F32)
    grad_wqkv = jnp.concatenate([grad_wq, grad_wkv], axis=1)
    for part in returned:
        grad_normed = grad_normed + part.astype(F32)
    x_part, grad_gain_one, grad_bias_one = norm_one_back(grad_normed)
    grad_x = (grad_resid + x_part).astype(BF16)
    grad_rel = jnp.einsum(
        "cb,hc->bh", one_hot, dd.reshape(H, span), precision=lax.Precision.HIGHEST
    )

    def total(values):
        part = lax.psum_scatter(values.astype(BF16), "dp", scatter_dimension=0, tiled=True)
        return lax.psum(part, "seq").astype(F32)

    total_down = total(grad_wdown)
    total_up = total(grad_wup)
    total_out = total(grad_wout)
    total_qkv = total(grad_wqkv)
    small_grads = jnp.concatenate(
        [
            g.reshape(groups, -1)
            for g in (grad_gain_one, grad_bias_one, grad_gain_two, grad_bias_two, grad_rel)
        ],
        axis=1,
    )
    small_total = lax.psum(lax.psum_scatter(small_grads, "dp", scatter_dimension=0, tiled=True), "seq")[0]
    cut = [small_total[i * shard_rows : (i + 1) * shard_rows] for i in range(4)]
    total_rel = small_total[4 * shard_rows :].reshape(rel_bias.shape)

    returned_both = swap_slots(jnp.stack([output_rows.reshape(pieces), grad_x.reshape(pieces)], axis=1))
    output, grad_tokens = from_slots(deal_row, [returned_both[:, 0], returned_both[:, 1]])
    return (
        output.reshape(tok_dev, width),
        grad_tokens.reshape(tok_dev, width),
        cut[0],
        cut[1],
        total_qkv,
        total_out,
        total_rel,
        cut[2],
        cut[3],
        total_up,
        total_down,
    )


def solution(mesh):
    by_all, by_dp = P(("seq", "dp"), None), P("dp", None)
    return jax.shard_map(
        shards,
        mesh=mesh,
        in_specs=(
            by_all, by_all, by_all, by_dp, P(), P("dp"), P("dp"), by_dp, by_dp, by_dp, P("dp"), P("dp"), by_dp, by_dp,
        ),
        out_specs=(by_all, by_all, P("dp"), P("dp"), by_dp, by_dp, by_dp, P("dp"), P("dp"), by_dp, by_dp),
        check_vma=False,
    )
```

```python
import functools

import jax
import jax.numpy as jnp
from jax import lax
from jax.experimental import pallas as pl
from jax.experimental.pallas import tpu as pltpu
from jax.sharding import PartitionSpec as P

H = 8
HD = 64
NBK = 32
QB = 256
PAIR = 2 * HD
BIG = -1e30
F32 = jnp.float32
BF16 = jnp.bfloat16
VMEM_LIMIT = 60 * 1024 * 1024

NT = (((1,), (1,)), ((), ()))
NN = (((1,), (0,)), ((), ()))


def dot_nt(a, b):
    return lax.dot_general(a, b, NT, preferred_element_type=F32)


def dot_nn(a, b):
    return lax.dot_general(a, b, NN, preferred_element_type=F32)


def norm_rows(values, gain_vec, bias_vec):
    average = jnp.mean(values, axis=-1, keepdims=True)
    centred = values - average
    variance = jnp.mean(centred * centred, axis=-1, keepdims=True)
    return centred * lax.rsqrt(variance + 1e-05) * gain_vec + bias_vec


def gelu_exact(values):
    return jax.nn.gelu(values, approximate=False)


def toeplitz(row, width):
    return pltpu.roll(jnp.broadcast_to(row, (QB, width)), 0, 1, stride=1, stride_axis=0)


def attention_fwd_kernel(base_ref, q_ref, qx_ref, k_ref, kx_ref, v_ref, att_ref, lse_ref, bias, kaug, vaug, scores):
    rows = q_ref.shape[0]
    width = base_ref.shape[-1]
    tiles = width // QB
    lane_q = lax.broadcasted_iota(jnp.int32, (QB, PAIR), 1) < HD
    lane_k = lax.broadcasted_iota(jnp.int32, k_ref.shape, 1) < HD
    for h in range(2):
        mine_k = lane_k if h == 0 else jnp.logical_not(lane_k)
        mine_q = lane_q if h == 0 else jnp.logical_not(lane_q)
        bias[...] = toeplitz(base_ref[0, h : h + 1, :], width)
        kaug[...] = jnp.where(mine_k, k_ref[...], kx_ref[...])
        vaug[...] = jnp.where(mine_k, v_ref[...], jnp.ones_like(v_ref))
        for b in range(rows // QB):
            here = pl.ds(b * QB, QB)
            q_aug = jnp.where(mine_q, q_ref[here, :], qx_ref[here, :])
            top = None
            for j in range(tiles):
                cols = pl.ds(j * QB, QB)
                s = dot_nt(q_aug, kaug[pl.ds((b + j) * QB, QB), :]) + bias[:, cols]
                scores[:, cols] = s
                most = jnp.maximum(s[:, :128], s[:, 128:])
                top = most if top is None else jnp.maximum(top, most)
            top = jnp.max(top, axis=1, keepdims=True)
            acc = jnp.zeros((QB, PAIR), F32)
            for j in range(tiles):
                p = jnp.exp(scores[:, pl.ds(j * QB, QB)] - top).astype(BF16)
                acc = acc + dot_nn(p, vaug[pl.ds((b + j) * QB, QB), :])
            att = acc / pltpu.roll(acc, HD, 1)
            lse = top + jnp.log(acc)
            if h == 0:
                att_ref[here, :] = att.astype(BF16)
                lse_ref[here, :] = lse
            else:
                att_ref[here, :] = jnp.where(mine_q, att.astype(BF16), att_ref[here, :])
                lse_ref[here, :] = jnp.where(mine_q, lse_ref[here, :], lse)


def attention_bwd_kernel(
    base_ref, q_ref, qx_ref, k_ref, kx_ref, v_ref, att_ref, lse_ref, do_ref,
    dq_ref, dk_ref, dv_ref, dd_ref,
    bias, kaug, vaug, qaug, doaug, dsum, dkt, dvt,
):
    rows = q_ref.shape[0]
    width = base_ref.shape[-1]
    tiles = width // QB
    lane_q = lax.broadcasted_iota(jnp.int32, (rows, PAIR), 1)
    extra = lax.rem(lane_q, HD)
    lane_k = lax.broadcasted_iota(jnp.int32, k_ref.shape, 1) < HD
    swap = (
        (lax.broadcasted_iota(jnp.int32, (PAIR, PAIR), 0) < HD)
        != (lax.broadcasted_iota(jnp.int32, (PAIR, PAIR), 1) < HD)
    ).astype(BF16)
    prod = do_ref[...].astype(F32) * att_ref[...].astype(F32)
    prod_hi = prod.astype(BF16)
    prod_lo = (prod - prod_hi.astype(F32)).astype(BF16)
    delta = -(dot_nn(prod_hi, swap) + dot_nn(prod_lo, swap))
    delta_hi = delta.astype(BF16).astype(F32)
    lse = -lse_ref[...]
    lse_hi = lse.astype(BF16).astype(F32)
    lse_mid = (lse - lse_hi).astype(BF16).astype(F32)
    lse_lo = lse - lse_hi - lse_mid
    q_extra = jnp.where(
        extra == HD - 3, lse_hi, jnp.where(extra == HD - 2, lse_mid, jnp.where(extra == HD - 1, lse_lo, qx_ref[...].astype(F32)))
    ).astype(BF16)
    do_extra = jnp.where(extra == 0, delta_hi, jnp.where(extra == 1, delta - delta_hi, 0.0)).astype(BF16)
    dkt[...] = jnp.zeros_like(dkt)
    dvt[...] = jnp.zeros_like(dvt)
    for h in range(2):
        mine_k = lane_k if h == 0 else jnp.logical_not(lane_k)
        mine_q = (lane_q < HD) if h == 0 else (lane_q >= HD)
        bias[...] = toeplitz(base_ref[0, h : h + 1, :], width)
        kaug[...] = jnp.where(mine_k, k_ref[...], kx_ref[...])
        vaug[...] = jnp.where(mine_k, v_ref[...], jnp.ones_like(v_ref))
        qaug[...] = jnp.where(mine_q, q_ref[...], q_extra)
        doaug[...] = jnp.where(mine_q, do_ref[...], do_extra)
        feat = pl.ds(h * HD, HD)
        for b in range(rows // QB):
            here = pl.ds(b * QB, QB)
            q_t = q_ref[here, :].astype(F32).T[h * HD : (h + 1) * HD].astype(BF16)
            do_t = do_ref[here, :].astype(F32).T[h * HD : (h + 1) * HD].astype(BF16)
            dq = jnp.zeros((QB, PAIR), F32)
            for j in range(tiles):
                cols = pl.ds(j * QB, QB)
                keys = pl.ds((b + j) * QB, QB)
                p = jnp.exp(dot_nt(qaug[here, :], kaug[keys, :]) + bias[:, cols])
                ds = p * dot_nt(doaug[here, :], vaug[keys, :])
                ds_low = ds.astype(BF16)
                dvt[feat, keys] += dot_nn(do_t, p.astype(BF16))
                dkt[feat, keys] += dot_nn(q_t, ds_low)
                dq = dq + dot_nn(ds_low, k_ref[keys, :])
                if b == 0:
                    dsum[:, cols] = ds
                else:
                    dsum[:, cols] += ds
            dq = (dq * (HD**-0.5)).astype(BF16)
            if h == 0:
                dq_ref[here, :] = dq
            else:
                dq_ref[here, :] = jnp.where(mine_q[:QB], dq, dq_ref[here, :])
        left, half = dsum[...], QB // 2
        while half:
            left = left[:half] + pltpu.roll(left[half:], width - half, 1)
            half //= 2
        dd_ref[0, h : h + 1, :] = left
    dk_ref[...] = dkt[...].T.astype(BF16)
    dv_ref[...] = dvt[...].T.astype(BF16)


def column_block(rows):
    return pl.BlockSpec((rows, PAIR), lambda i: (0, i))


def whole_block(rows):
    return pl.BlockSpec((rows, PAIR), lambda i: (0, 0))


def attention_fwd(base, q, qx, k, kx, v):
    rows, width, window = q.shape[0], base.shape[-1], k.shape[0]
    return pl.pallas_call(
        attention_fwd_kernel,
        grid=(H // 2,),
        in_specs=[
            pl.BlockSpec((1, 2, width), lambda i: (i, 0, 0)),
            column_block(rows),
            whole_block(rows),
            column_block(window),
            whole_block(window),
            column_block(window),
        ],
        out_specs=[column_block(rows), column_block(rows)],
        out_shape=[jax.ShapeDtypeStruct(q.shape, BF16), jax.ShapeDtypeStruct(q.shape, F32)],
        scratch_shapes=[
            pltpu.VMEM((QB, width), F32),
            pltpu.VMEM((window, PAIR), BF16),
            pltpu.VMEM((window, PAIR), BF16),
            pltpu.VMEM((QB, width), F32),
        ],
        compiler_params=pltpu.CompilerParams(vmem_limit_bytes=VMEM_LIMIT),
        name="attention_fwd",
    )(base, q, qx, k, kx, v)


def attention_bwd(base, q, qx, k, kx, v, att, lse, do):
    rows, width, window = q.shape[0], base.shape[-1], k.shape[0]
    return pl.pallas_call(
        attention_bwd_kernel,
        grid=(H // 2,),
        in_specs=[
            pl.BlockSpec((1, 2, width), lambda i: (i, 0, 0)),
            column_block(rows),
            whole_block(rows),
            column_block(window),
            whole_block(window),
            column_block(window),
            column_block(rows),
            column_block(rows),
            column_block(rows),
        ],
        out_specs=[
            column_block(rows),
            column_block(window),
            column_block(window),
            pl.BlockSpec((1, 2, width), lambda i: (i, 0, 0)),
        ],
        out_shape=[
            jax.ShapeDtypeStruct(q.shape, BF16),
            jax.ShapeDtypeStruct(k.shape, BF16),
            jax.ShapeDtypeStruct(k.shape, BF16),
            jax.ShapeDtypeStruct(base.shape, F32),
        ],
        scratch_shapes=[
            pltpu.VMEM((QB, width), F32),
            pltpu.VMEM((window, PAIR), BF16),
            pltpu.VMEM((window, PAIR), BF16),
            pltpu.VMEM((rows, PAIR), BF16),
            pltpu.VMEM((rows, PAIR), BF16),
            pltpu.VMEM((QB, width), F32),
            pltpu.VMEM((PAIR, window), F32),
            pltpu.VMEM((PAIR, window), F32),
        ],
        compiler_params=pltpu.CompilerParams(vmem_limit_bytes=VMEM_LIMIT),
        name="attention_bwd",
    )(base, q, qx, k, kx, v, att, lse, do)


def copy_kernel(deal_ref, *refs):
    count = len(refs) // 2
    for i in range(count):
        refs[count + i][...] = refs[i][...]


def to_slots(deal_row, arrays):
    groups, length, width = arrays[0].shape
    spec_in = pl.BlockSpec((1, length, width), lambda g, deal: (g, 0, 0))
    spec_out = pl.BlockSpec((1, length, width), lambda g, deal: (deal[g], 0, 0))
    return pl.pallas_call(
        copy_kernel,
        grid_spec=pltpu.PrefetchScalarGridSpec(
            num_scalar_prefetch=1, grid=(groups,), in_specs=[spec_in] * len(arrays), out_specs=[spec_out] * len(arrays)
        ),
        out_shape=[jax.ShapeDtypeStruct(a.shape, a.dtype) for a in arrays],
        name="to_slots",
    )(deal_row, *arrays)


def add_low(first, *others):
    total = first.astype(F32)
    for other in others:
        total = total + other.astype(F32)
    return total


class Summer:
    def __init__(self, source, recv1, pair, recv2, mine, recv3, out, sems):
        self.source, self.recv1, self.pair, self.recv2 = source, recv1, pair, recv2
        self.mine, self.recv3, self.out, self.sems = mine, recv3, out, sems
        self.dp, self.seq = lax.axis_index("dp"), lax.axis_index("seq")
        self.pairs, self.splits = source.shape[0] // 2, lax.axis_size("seq")
        self.core, self.chip = lax.rem(self.dp, 2), self.dp // 2
        self.scatter = out.shape[1] < mine.shape[0]
        self.sent = []
        self.count = 0

    def send(self, src, dst, device):
        slot = self.count
        self.count += 1
        copy = pltpu.make_async_remote_copy(
            src_ref=src, dst_ref=dst, send_sem=self.sems.at[0, slot], recv_sem=self.sems.at[1, slot],
            device_id=device, device_id_type=pl.DeviceIdType.MESH,
        )
        copy.start()
        self.sent.append(copy)
        return copy

    def stage1(self):
        other = 1 - self.core
        self.first = [
            self.send(self.source.at[2 * k + other], self.recv1.at[k], {"dp": self.dp + 1 - 2 * self.core})
            for k in range(self.pairs)
        ]

    def stage2(self):
        self.second = []
        for step in range(self.pairs):
            k = lax.rem(self.chip + 1 + step, self.pairs)
            if step == 0:
                for copy in self.first:
                    copy.wait_recv()
            self.pair[k] = add_low(self.source[2 * k + self.core], self.recv1[k]).astype(self.pair.dtype)
            if step < self.pairs - 1:
                self.second.append(self.send(self.pair.at[k], self.recv2.at[step], {"dp": 2 * k + self.core}))

    def stage3(self):
        for copy in self.second:
            copy.wait_recv()
        total = add_low(self.pair[self.chip], *[self.recv2[step] for step in range(self.pairs - 1)])
        self.mine[...] = total.astype(self.mine.dtype)
        self.third = []
        rows = self.out.shape[1]
        for step in range(self.splits - 1):
            t = lax.rem(self.seq + 1 + step, self.splits)
            src = self.mine.at[pl.ds(pl.multiple_of(t * rows, rows), rows)] if self.scatter else self.mine
            dst = self.recv3.at[step] if self.scatter else self.out.at[self.seq]
            self.third.append(self.send(src, dst, {"seq": t}))
        if not self.scatter:
            self.out[self.seq] = self.mine[...]

    def stage4(self):
        for copy in self.third:
            copy.wait_recv()
        if not self.scatter:
            return
        rows = self.out.shape[1]
        own = self.mine[pl.ds(pl.multiple_of(self.seq * rows, rows), rows)]
        total = add_low(own, *[self.recv3[step] for step in range(self.splits - 1)])
        self.out[self.seq] = total.astype(self.out.dtype)
        self.fourth = [
            self.send(self.out.at[self.seq], self.out.at[self.seq], {"seq": lax.rem(self.seq + 1 + step, self.splits)})
            for step in range(self.splits - 1)
        ]

    def finish(self):
        if self.scatter:
            for copy in self.fourth:
                copy.wait_recv()
        for copy in self.sent:
            copy.wait_send()


def summer_shapes(shape, dtype, splits):
    groups, rows, cols = shape
    pairs = groups // 2
    scatter = rows % (16 * splits) == 0
    out = jax.ShapeDtypeStruct((splits, rows // splits if scatter else rows, cols), dtype)
    copies = pairs + (pairs - 1) + (splits - 1) * (2 if scatter else 1)
    scratch = [
        pltpu.VMEM((pairs, rows, cols), dtype),
        pltpu.VMEM((pairs, rows, cols), dtype),
        pltpu.VMEM((pairs - 1, rows, cols), dtype),
        pltpu.VMEM((rows, cols), dtype),
        pltpu.VMEM((splits - 1, out.shape[1] if scatter else 16, cols), dtype),
        pltpu.SemaphoreType.DMA((2, copies)),
    ]
    return out, scratch


def greet(peers):
    barrier = pltpu.get_barrier_semaphore()
    for device in peers:
        pl.semaphore_signal(barrier, inc=1, device_id=device, device_id_type=pl.DeviceIdType.MESH)
    pl.semaphore_wait(barrier, len(peers))


def others(axis):
    size, me = lax.axis_size(axis), lax.axis_index(axis)
    return [{axis: lax.rem(me + step, size)} for step in range(1, size)]


def tail_kernel(units, *refs):
    sources, slots = refs[:units], refs[units : units + 2]
    outs, landed = refs[units + 2 : 2 * units + 2], refs[2 * units + 2 : 2 * units + 4]
    scratch, ret_sems = refs[2 * units + 4 : -1], refs[-1]
    greet(others("dp") + others("seq"))
    summers = [
        Summer(sources[i], *scratch[6 * i : 6 * i + 5], outs[i], scratch[6 * i + 5]) for i in range(units)
    ]
    dp, groups = lax.axis_index("dp"), lax.axis_size("dp")
    for summer in summers:
        summer.stage1()
    back = []
    for a in range(2):
        landed[a][dp] = slots[a][dp]
        for step in range(1, groups):
            peer = lax.rem(dp + step, groups)
            copy = pltpu.make_async_remote_copy(
                src_ref=slots[a].at[peer], dst_ref=landed[a].at[dp],
                send_sem=ret_sems.at[0, a, step - 1], recv_sem=ret_sems.at[1, a, step - 1],
                device_id={"dp": peer}, device_id_type=pl.DeviceIdType.MESH,
            )
            copy.start()
            back.append(copy)
    for summer in summers:
        summer.stage2()
    for summer in summers:
        summer.stage3()
    for summer in summers:
        summer.stage4()
    for summer in summers:
        summer.finish()
    for copy in back:
        copy.wait()


def tail(partials, slots):
    splits, groups = lax.axis_size("seq"), lax.axis_size("dp")
    out_shapes, scratch = [], []
    for p in partials:
        out, more = summer_shapes(p.shape, p.dtype, splits)
        out_shapes.append(out)
        scratch += more
    vmem = pl.BlockSpec(memory_space=pltpu.VMEM)
    return pl.pallas_call(
        functools.partial(tail_kernel, len(partials)),
        in_specs=[vmem] * (len(partials) + 2),
        out_specs=[vmem] * (len(partials) + 2),
        out_shape=out_shapes + [jax.ShapeDtypeStruct(a.shape, a.dtype) for a in slots],
        scratch_shapes=scratch + [pltpu.SemaphoreType.DMA((2, 2, groups - 1))],
        compiler_params=pltpu.CompilerParams(
            collective_id=1, has_side_effects=True, vmem_limit_bytes=VMEM_LIMIT
        ),
        name="tail",
    )(*partials, *slots)


def finish_kernel(deal_ref, down, up, out, qkv, small, ret_out, ret_grad, *outs):
    o_out, o_grad, o_qkv, o_wout, o_up, o_down, o_small = outs
    length = ret_out.shape[1]
    for g in range(ret_out.shape[0]):
        piece = deal_ref[0, g]
        o_out[pl.ds(g * length, length), :] = ret_out[piece]
        o_grad[pl.ds(g * length, length), :] = ret_grad[piece]
    for source, target in ((down, o_down), (up, o_up), (out, o_wout), (qkv, o_qkv)):
        direct = source.shape[0] * source.shape[1] * source.shape[2] != target.shape[0] * target.shape[1]
        cols = source.shape[2]
        if direct:
            value = add_low(*[source[t] for t in range(source.shape[0])])
        else:
            value = source[...].reshape(-1, cols).astype(F32)
        height = target.shape[0]
        for c in range(target.shape[1] // cols):
            target[:, c * cols : (c + 1) * cols] = value[c * height : (c + 1) * height]
    o_small[...] = add_low(*[small[t] for t in range(small.shape[0])])


def finish(deal, sums, returned, shapes):
    return pl.pallas_call(
        finish_kernel,
        in_specs=[pl.BlockSpec(memory_space=pltpu.SMEM)] + [pl.BlockSpec(memory_space=pltpu.VMEM)] * 7,
        out_specs=[pl.BlockSpec(memory_space=pltpu.VMEM)] * len(shapes),
        out_shape=shapes,
        compiler_params=pltpu.CompilerParams(vmem_limit_bytes=VMEM_LIMIT),
        name="finish",
    )(deal, *sums, *returned)


def swap_slots(values):
    return lax.all_to_all(values, "dp", split_axis=0, concat_axis=0, tiled=True)


def shards(
    tokens,
    cotangent,
    deal,
    lengths,
    buckets,
    ln1_gain,
    ln1_bias,
    w_qkv,
    w_out,
    rel_bias,
    ln2_gain,
    ln2_bias,
    w_up,
    w_down,
):
    groups = lax.axis_size("dp")
    splits = lax.axis_size("seq")
    tok_dev, width = tokens.shape
    block_len = tok_dev // groups
    maxlen = buckets.shape[0]
    back = -(-maxlen // tok_dev)
    window = (back + 1) * tok_dev
    span = back * tok_dev + QB
    chunk = lax.axis_index("seq")
    deal_row = deal[0]
    shard_rows = ln1_gain.shape[0]

    small = jnp.concatenate([ln1_gain, ln1_bias, ln2_gain, ln2_bias, rel_bias.reshape(-1)])
    wqkv_full = lax.all_gather(w_qkv, "dp", axis=0, tiled=True)
    small_full = lax.all_gather(small, "dp", axis=0, tiled=False)
    wout_full = lax.all_gather(w_out, "dp", axis=0, tiled=True)
    wup_full = lax.all_gather(w_up, "dp", axis=0, tiled=True)
    wdown_full = lax.all_gather(w_down, "dp", axis=0, tiled=True)
    gains = small_full[:, : 4 * shard_rows].reshape(groups, 4, shard_rows).transpose(1, 0, 2).reshape(4, width)
    gain_one, bias_one, gain_two, bias_two = (gains[i].astype(F32) for i in range(4))
    rel_full = small_full[:, 4 * shard_rows :].reshape(NBK, H)

    pieces = (groups, block_len, width)
    slot_in, slot_grad = to_slots(deal_row, [tokens.reshape(pieces), cotangent.reshape(pieces)])
    dealt = swap_slots(jnp.stack([slot_in, slot_grad], axis=1))
    x_rows = dealt[:, 0].reshape(tok_dev, width).astype(F32)
    grad_out = dealt[:, 1].reshape(tok_dev, width)

    ends, so_far = [], 0
    for c in range(lengths.shape[1]):
        so_far = so_far + lengths[0, c]
        ends.append(so_far)
    lane = lax.rem(jnp.arange(PAIR, dtype=jnp.int32), HD)[None, :]
    key_pos = (chunk - back) * tok_dev + jnp.arange(window, dtype=jnp.int32)
    key_seg = sum((key_pos >= e).astype(jnp.int32) for e in ends)
    key_seg = jnp.where(key_pos < 0, len(ends), key_seg)[:, None]
    query_seg = key_seg[back * tok_dev :]
    kx = jnp.where((lane == key_seg) | (lane >= HD - 3), 1.0, 0.0).astype(BF16)
    qx = jnp.where((lane <= len(ends)) & (lane != query_seg), BIG, 0.0).astype(BF16)
    offset = jnp.arange(span, dtype=jnp.int32)
    distance = back * tok_dev - offset
    in_reach = (distance >= 0) & (distance < maxlen)
    table_bucket = jnp.concatenate(
        [jnp.zeros((back * tok_dev + 1 - maxlen,), jnp.int32), buckets[::-1], jnp.zeros((QB - 1,), jnp.int32)]
    )
    one_hot = ((table_bucket[:, None] == jnp.arange(NBK, dtype=jnp.int32)[None, :]) & in_reach[:, None]).astype(F32)
    base = jnp.einsum("cb,bh->hc", one_hot, rel_full.astype(F32), precision=lax.Precision.HIGHEST)
    base = jnp.where(in_reach[None], base, BIG).reshape(H // 2, 2, span)

    normed, norm_one_back = jax.vjp(norm_rows, x_rows, gain_one, bias_one)
    normed_low = normed.astype(BF16)
    earlier = [
        lax.ppermute(normed_low, "seq", [(i, i + step) for i in range(splits - step)]) for step in range(back, 0, -1)
    ]
    scale = HD**-0.5
    own_qkv = jnp.dot(normed_low, wqkv_full, preferred_element_type=F32).astype(BF16)
    rows_before = jnp.concatenate(earlier, axis=0)
    kv_before = jnp.dot(rows_before, wqkv_full[:, width:], preferred_element_type=F32).astype(BF16)
    queries = own_qkv[:, :width] * jnp.asarray(scale, BF16)
    keys_all = jnp.concatenate([kv_before[:, :width], own_qkv[:, width : 2 * width]], axis=0)
    values_all = jnp.concatenate([kv_before[:, width:], own_qkv[:, 2 * width :]], axis=0)
    attended, lse = attention_fwd(base, queries, qx, keys_all, kx, values_all)
    residual = x_rows + jnp.dot(attended, wout_full, preferred_element_type=F32)
    normed_two, norm_two_back = jax.vjp(norm_rows, residual, gain_two, bias_two)
    normed_two_low = normed_two.astype(BF16)
    pre_act = jnp.dot(normed_two_low, wup_full, preferred_element_type=F32)
    active, gelu_back = jax.vjp(gelu_exact, pre_act)
    active_low = active.astype(BF16)
    output_rows = (residual + jnp.dot(active_low, wdown_full, preferred_element_type=F32)).astype(BF16)

    grad_wdown = jnp.einsum("tf,td->fd", active_low, grad_out, preferred_element_type=F32)
    grad_active = jnp.einsum("td,fd->tf", grad_out, wdown_full, preferred_element_type=F32)
    grad_pre = gelu_back(grad_active)[0].astype(BF16)
    grad_wup = jnp.einsum("td,tf->df", normed_two_low, grad_pre, preferred_element_type=F32)
    grad_norm_two = jnp.einsum("tf,df->td", grad_pre, wup_full, preferred_element_type=F32)
    resid_part, grad_gain_two, grad_bias_two = norm_two_back(grad_norm_two)
    grad_resid = grad_out.astype(F32) + resid_part
    branch_grad = grad_resid.astype(BF16)
    grad_wout = jnp.einsum("td,te->de", attended, branch_grad, preferred_element_type=F32)
    grad_att = jnp.einsum("te,de->td", branch_grad, wout_full, preferred_element_type=F32).astype(BF16)
    dq, dk, dv, dd = attention_bwd(base, queries, qx, keys_all, kx, values_all, attended, lse, grad_att)
    grad_kv = jnp.concatenate([dk, dv], axis=1)
    part_before = jnp.einsum(
        "tc,dc->td", grad_kv[: back * tok_dev], wqkv_full[:, width:], preferred_element_type=F32
    ).astype(BF16)
    returned = [
        lax.ppermute(
            part_before[(back - step) * tok_dev : (back - step + 1) * tok_dev],
            "seq",
            [(i + step, i) for i in range(splits - step)],
        )
        for step in range(back, 0, -1)
    ]
    grad_own = jnp.concatenate([dq, grad_kv[back * tok_dev :]], axis=1)
    grad_normed = jnp.einsum("tc,dc->td", grad_own, wqkv_full, preferred_element_type=F32)
    all_rows = jnp.concatenate([rows_before, normed_low], axis=0)
    grad_wq = jnp.einsum("td,tc->dc", normed_low, dq, preferred_element_type=F32)
    grad_wkv = jnp.einsum("td,tc->dc", all_rows, grad_kv, preferred_element_type=F32)
    grad_wqkv = jnp.concatenate([grad_wq, grad_wkv], axis=1)
    for part in returned:
        grad_normed = grad_normed + part.astype(F32)
    x_part, grad_gain_one, grad_bias_one = norm_one_back(grad_normed)
    grad_x = (grad_resid + x_part).astype(BF16)
    grad_rel = jnp.einsum(
        "cb,hc->bh", one_hot, dd.reshape(H, span), precision=lax.Precision.HIGHEST
    )

    def by_owner(values):
        rows, cols = values.shape
        parts = values.astype(BF16).reshape(groups, rows // groups, cols // width, width)
        return parts.transpose(0, 2, 1, 3).reshape(groups, -1, width)

    small_grads = jnp.concatenate(
        [g.reshape(groups, -1) for g in (grad_gain_one, grad_bias_one, grad_gain_two, grad_bias_two, grad_rel)], axis=1
    )
    small_cols = small_grads.shape[1]
    small_grads = jnp.pad(small_grads, ((0, 0), (0, 8 * PAIR - small_cols))).reshape(groups, 8, PAIR)
    *sums, back_out, back_grad = tail(
        [by_owner(grad_wdown), by_owner(grad_wup), by_owner(grad_wout), by_owner(grad_wqkv), small_grads],
        [output_rows.reshape(pieces), grad_x.reshape(pieces)],
    )
    output, grad_tokens, total_qkv, total_out, total_up, total_down, small_total = finish(
        deal,
        sums,
        [back_out, back_grad],
        [
            jax.ShapeDtypeStruct((tok_dev, width), BF16),
            jax.ShapeDtypeStruct((tok_dev, width), BF16),
            jax.ShapeDtypeStruct(w_qkv.shape, F32),
            jax.ShapeDtypeStruct(w_out.shape, F32),
            jax.ShapeDtypeStruct(w_up.shape, F32),
            jax.ShapeDtypeStruct(w_down.shape, F32),
            jax.ShapeDtypeStruct((8, PAIR), F32),
        ],
    )
    small_total = small_total.reshape(-1)[:small_cols]
    cut = [small_total[i * shard_rows : (i + 1) * shard_rows] for i in range(4)]
    total_rel = small_total[4 * shard_rows :].reshape(rel_bias.shape)
    return (
        output,
        grad_tokens,
        cut[0],
        cut[1],
        total_qkv,
        total_out,
        total_rel,
        cut[2],
        cut[3],
        total_up,
        total_down,
    )


def solution(mesh):
    by_all, by_dp = P(("seq", "dp"), None), P("dp", None)
    return jax.shard_map(
        shards,
        mesh=mesh,
        in_specs=(
            by_all, by_all, by_all, by_dp, P(), P("dp"), P("dp"), by_dp, by_dp, by_dp, P("dp"), P("dp"), by_dp, by_dp,
        ),
        out_specs=(by_all, by_all, P("dp"), P("dp"), by_dp, by_dp, by_dp, P("dp"), P("dp"), by_dp, by_dp),
        check_vma=False,
    )
```

```python
import functools

import jax
import jax.numpy as jnp
from jax import lax
from jax.experimental import pallas as pl
from jax.experimental.pallas import tpu as pltpu
from jax.sharding import PartitionSpec as P

H = 8
HD = 64
NBK = 32
QB = 256
PAIR = 2 * HD
BIG = -1e30
F32 = jnp.float32
BF16 = jnp.bfloat16
VMEM_LIMIT = 60 * 1024 * 1024

NT = (((1,), (1,)), ((), ()))
NN = (((1,), (0,)), ((), ()))


def dot_nt(a, b):
    return lax.dot_general(a, b, NT, preferred_element_type=F32)


def dot_nn(a, b):
    return lax.dot_general(a, b, NN, preferred_element_type=F32)


def norm_rows(values, gain_vec, bias_vec):
    average = jnp.mean(values, axis=-1, keepdims=True)
    centred = values - average
    variance = jnp.mean(centred * centred, axis=-1, keepdims=True)
    return centred * lax.rsqrt(variance + 1e-05) * gain_vec + bias_vec


def toeplitz(row):
    width = row.shape[1]
    return pltpu.roll(jnp.broadcast_to(row, (QB, width)), 0, 1, stride=1, stride_axis=0)[:, QB:]


def attention_fwd_kernel(base_ref, q_ref, qx_ref, k_ref, kx_ref, v_ref, att_ref, lse_ref, bias, kaug, vaug, scores):
    rows = q_ref.shape[0]
    tiles = base_ref.shape[-1] // QB - 1
    lane_q = lax.broadcasted_iota(jnp.int32, (QB, PAIR), 1) < HD
    lane_k = lax.broadcasted_iota(jnp.int32, k_ref.shape, 1) < HD
    for h in range(2):
        mine_k = lane_k if h == 0 else jnp.logical_not(lane_k)
        mine_q = lane_q if h == 0 else jnp.logical_not(lane_q)
        bias[...] = toeplitz(base_ref[0, h : h + 1, :])
        kaug[...] = jnp.where(mine_k, k_ref[...], kx_ref[...])
        vaug[...] = jnp.where(mine_k, v_ref[...], jnp.ones_like(v_ref))
        for b in range(rows // QB):
            here = pl.ds(b * QB, QB)
            q_aug = jnp.where(mine_q, q_ref[here, :], qx_ref[here, :])
            top = None
            for j in range(tiles):
                cols = pl.ds(j * QB, QB)
                s = dot_nt(q_aug, kaug[pl.ds((b + j) * QB, QB), :]) + bias[:, cols]
                scores[:, cols] = s
                most = jnp.maximum(s[:, :128], s[:, 128:])
                top = most if top is None else jnp.maximum(top, most)
            top = jnp.max(top, axis=1, keepdims=True)
            acc = jnp.zeros((QB, PAIR), F32)
            for j in range(tiles):
                p = jnp.exp(scores[:, pl.ds(j * QB, QB)] - top).astype(BF16)
                acc = acc + dot_nn(p, vaug[pl.ds((b + j) * QB, QB), :])
            att = acc / pltpu.roll(acc, HD, 1)
            lse = top + jnp.log(acc)
            if h == 0:
                att_ref[here, :] = att.astype(BF16)
                lse_ref[here, :] = lse
            else:
                att_ref[here, :] = jnp.where(mine_q, att.astype(BF16), att_ref[here, :])
                lse_ref[here, :] = jnp.where(mine_q, lse_ref[here, :], lse)


def column_block(rows):
    return pl.BlockSpec((rows, PAIR), lambda i: (0, i))


def whole_block(rows):
    return pl.BlockSpec((rows, PAIR), lambda i: (0, 0))


def attention_fwd(base, q, qx, k, kx, v):
    rows, width, window = q.shape[0], base.shape[-1], k.shape[0]
    return pl.pallas_call(
        attention_fwd_kernel,
        grid=(H // 2,),
        in_specs=[
            pl.BlockSpec((1, 2, width), lambda i: (i, 0, 0)),
            column_block(rows),
            whole_block(rows),
            column_block(window),
            whole_block(window),
            column_block(window),
        ],
        out_specs=[column_block(rows), column_block(rows)],
        out_shape=[jax.ShapeDtypeStruct(q.shape, BF16), jax.ShapeDtypeStruct(q.shape, F32)],
        scratch_shapes=[
            pltpu.VMEM((QB, width - QB), F32),
            pltpu.VMEM((window, PAIR), BF16),
            pltpu.VMEM((window, PAIR), BF16),
            pltpu.VMEM((QB, width - QB), F32),
        ],
        compiler_params=pltpu.CompilerParams(vmem_limit_bytes=VMEM_LIMIT),
        name="attention_fwd",
    )(base, q, qx, k, kx, v)


def copy_kernel(deal_ref, *refs):
    count = len(refs) // 2
    for i in range(count):
        refs[count + i][...] = refs[i][...]


def to_slots(deal_row, arrays):
    groups, length, width = arrays[0].shape
    spec_in = pl.BlockSpec((1, length, width), lambda g, deal: (g, 0, 0))
    spec_out = pl.BlockSpec((1, length, width), lambda g, deal: (deal[g], 0, 0))
    return pl.pallas_call(
        copy_kernel,
        grid_spec=pltpu.PrefetchScalarGridSpec(
            num_scalar_prefetch=1, grid=(groups,), in_specs=[spec_in] * len(arrays), out_specs=[spec_out] * len(arrays)
        ),
        out_shape=[jax.ShapeDtypeStruct(a.shape, a.dtype) for a in arrays],
        name="to_slots",
    )(deal_row, *arrays)


def add_low(first, *others):
    total = first.astype(F32)
    for other in others:
        total = total + other.astype(F32)
    return total


class Summer:
    def __init__(self, source, pair, recv2, mine, recv3, out, sems):
        self.source, self.pair, self.recv2 = source, pair, recv2
        self.mine, self.recv3, self.out, self.sems = mine, recv3, out, sems
        self.dp, self.seq = lax.axis_index("dp"), lax.axis_index("seq")
        self.pairs, self.splits = source.shape[0] // 2, lax.axis_size("seq")
        self.core, self.chip = lax.rem(self.dp, 2), self.dp // 2
        self.scatter = out.shape[1] < mine.shape[0]
        self.sent = []
        self.count = 0

    def send(self, src, dst, device):
        slot = self.count
        self.count += 1
        copy = pltpu.make_async_remote_copy(
            src_ref=src, dst_ref=dst, send_sem=self.sems.at[0, slot], recv_sem=self.sems.at[1, slot],
            device_id=device, device_id_type=pl.DeviceIdType.MESH,
        )
        copy.start()
        self.sent.append(copy)
        return copy

    def stage1(self):
        other = 1 - self.core
        self.first = [
            self.send(self.source.at[2 * k + other], self.pair.at[k], {"dp": self.dp + 1 - 2 * self.core})
            for k in range(self.pairs)
        ]

    def stage2(self):
        self.second = []
        for step in range(self.pairs):
            k = lax.rem(self.chip + 1 + step, self.pairs)
            if step == 0:
                for copy in self.first:
                    copy.wait_recv()
            self.pair[k] = add_low(self.source[2 * k + self.core], self.pair[k]).astype(self.pair.dtype)
            if step < self.pairs - 1:
                self.second.append(self.send(self.pair.at[k], self.recv2.at[step], {"dp": 2 * k + self.core}))

    def stage3(self):
        for copy in self.second:
            copy.wait_recv()
        total = add_low(self.pair[self.chip], *[self.recv2[step] for step in range(self.pairs - 1)])
        self.mine[...] = total.astype(self.mine.dtype)
        self.third = []
        rows = self.out.shape[1]
        for step in range(self.splits - 1):
            t = lax.rem(self.seq + 1 + step, self.splits)
            src = self.mine.at[pl.ds(pl.multiple_of(t * rows, rows), rows)] if self.scatter else self.mine
            dst = self.recv3.at[step] if self.scatter else self.out.at[self.seq]
            self.third.append(self.send(src, dst, {"seq": t}))
        if not self.scatter:
            self.out[self.seq] = self.mine[...]

    def stage4(self):
        for copy in self.third:
            copy.wait_recv()
        if not self.scatter:
            return
        rows = self.out.shape[1]
        own = self.mine[pl.ds(pl.multiple_of(self.seq * rows, rows), rows)]
        total = add_low(own, *[self.recv3[step] for step in range(self.splits - 1)])
        self.out[self.seq] = total.astype(self.out.dtype)
        self.fourth = [
            self.send(self.out.at[self.seq], self.out.at[self.seq], {"seq": lax.rem(self.seq + 1 + step, self.splits)})
            for step in range(self.splits - 1)
        ]

    def finish(self):
        if self.scatter:
            for copy in self.fourth:
                copy.wait_recv()
        for copy in self.sent:
            copy.wait_send()


def summer_shapes(shape, dtype, splits):
    groups, rows, cols = shape
    pairs = groups // 2
    scatter = rows % (16 * splits) == 0
    out = jax.ShapeDtypeStruct((splits, rows // splits if scatter else rows, cols), dtype)
    copies = pairs + (pairs - 1) + (splits - 1) * (2 if scatter else 1)
    scratch = [
        pltpu.VMEM((pairs, rows, cols), dtype),
        pltpu.VMEM((pairs - 1, rows, cols), dtype),
        pltpu.VMEM((rows, cols), dtype),
        pltpu.VMEM((splits - 1, out.shape[1] if scatter else 16, cols), dtype),
        pltpu.SemaphoreType.DMA((2, copies)),
    ]
    return out, scratch


def greet(peers):
    barrier = pltpu.get_barrier_semaphore()
    for device in peers:
        pl.semaphore_signal(barrier, inc=1, device_id=device, device_id_type=pl.DeviceIdType.MESH)
    pl.semaphore_wait(barrier, len(peers))


def others(axis):
    size, me = lax.axis_size(axis), lax.axis_index(axis)
    return [{axis: lax.rem(me + step, size)} for step in range(1, size)]


class SmallSummer:
    def __init__(self, ref, land, sems):
        self.ref, self.land, self.sems = ref, land, sems
        self.dp, self.seq = lax.axis_index("dp"), lax.axis_index("seq")
        self.pairs, self.splits = lax.axis_size("dp") // 2, lax.axis_size("seq")
        self.slot, self.copies, self.sent = 0, [], []

    def send(self, devices):
        self.copies = []
        for device in devices:
            copy = pltpu.make_async_remote_copy(
                src_ref=self.ref.at[len(self.sent)], dst_ref=self.land.at[self.slot],
                send_sem=self.sems.at[0, self.slot], recv_sem=self.sems.at[1, self.slot],
                device_id=device, device_id_type=pl.DeviceIdType.MESH,
            )
            copy.start()
            self.copies.append((self.slot, copy))
            self.slot += 1
        self.sent.append(self.copies)

    def take(self):
        stage = len(self.sent) - 1
        total = self.ref[stage]
        for slot, copy in self.copies:
            copy.wait_recv()
            total = total + self.land[slot]
        self.ref[stage + 1] = total

    def pair(self):
        self.send([{"dp": self.dp + 1 - 2 * lax.rem(self.dp, 2)}])

    def plane(self):
        core, chip = lax.rem(self.dp, 2), self.dp // 2
        self.send([{"dp": 2 * lax.rem(chip + step, self.pairs) + core} for step in range(1, self.pairs)])

    def along(self):
        self.send([{"seq": lax.rem(self.seq + step, self.splits)} for step in range(1, self.splits)])

    def finish(self):
        for copies in self.sent:
            for _, copy in copies:
                copy.wait_send()


def norm_stats(values):
    average = jnp.mean(values, axis=-1, keepdims=True)
    centred = values - average
    scale = lax.rsqrt(jnp.mean(centred * centred, axis=-1, keepdims=True) + 1e-05)
    return centred * scale, scale


def norm_back(grad, normal, scale):
    return scale * (
        grad - jnp.mean(grad, axis=-1, keepdims=True) - normal * jnp.mean(grad * normal, axis=-1, keepdims=True)
    )


def flip(values):
    return values.astype(F32).T.astype(BF16)


def phase_spans(back, per_chunk, tiles):
    spans = []
    for chunk in range(back + 1):
        jobs = [
            (kt, b, chunk * per_chunk + kt - b)
            for kt in range(per_chunk)
            for b in range(per_chunk)
            if 0 <= chunk * per_chunk + kt - b < tiles
        ]
        first, last = min(j[2] for j in jobs), max(j[2] for j in jobs)
        spans.append((chunk, first, last - first + 1, jobs))
    return spans


def rest_kernel(back, *refs):
    (
        x_ref, g_ref, gains_ref, wqkv_ref, wout_ref, wup_ref, wdown_ref, rows_ref,
        base_ref, hot_hi_ref, q_ref, qx_ref, k_ref, kx_ref, v_ref, att_ref, lse_ref,
    ) = refs[:17]
    sum_down, sum_up, sum_out, sum_qkv, small_out, ret_out, ret_grad = refs[17:24]
    it = iter(refs[24:])
    sources = [next(it) for _ in range(4)]
    summers = [
        Summer(source, *[next(it) for _ in range(4)], out, next(it))
        for source, out in zip(sources, (sum_down, sum_up, sum_out, sum_qkv))
    ]
    down, up, out_sum, qkv_sum = summers
    small_ref, small_land, small_sems = next(it), next(it), next(it)
    slots, ret_sems, halo_send, halo_land, halo_sems = (next(it) for _ in range(5))
    dres_ref, do_ref, qaug, doaug, q_t, do_t = (next(it) for _ in range(6))
    bias, dsum, dd, dq_acc, dkt, dvt, dkv, gkv = (next(it) for _ in range(8))
    dp, groups = lax.axis_index("dp"), lax.axis_size("dp")
    seq, splits = lax.axis_index("seq"), lax.axis_size("seq")
    tokens, width = x_ref.shape
    length = tokens // groups
    per_chunk = tokens // QB
    tiles = base_ref.shape[-1] // QB - 1
    greet(others("dp") + others("seq"))

    returns = []

    def send_back(which, landed):
        landed[dp] = slots[which, dp]
        for step in range(1, groups):
            peer = lax.rem(dp + step, groups)
            copy = pltpu.make_async_remote_copy(
                src_ref=slots.at[which, peer], dst_ref=landed.at[dp],
                send_sem=ret_sems.at[0, which, step - 1], recv_sem=ret_sems.at[1, which, step - 1],
                device_id={"dp": peer}, device_id_type=pl.DeviceIdType.MESH,
            )
            copy.start()
            returns.append(copy)

    resid = x_ref[...].astype(F32) + dot_nn(att_ref[...], wout_ref[...])
    normal, scale = norm_stats(resid)
    gain_two = gains_ref[2:3, :]
    a2 = (normal * gain_two + gains_ref[3:4, :]).astype(BF16)
    a2_t = flip(a2)
    g = g_ref[...]
    y = resid
    da2 = jnp.zeros((tokens, width), F32)
    rows_up, rows_down = width // groups, wdown_ref.shape[0] // groups
    for c in range(wdown_ref.shape[0] // width):
        cols = pl.ds(c * width, width)
        upper = dot_nn(a2, wup_ref[:, cols])
        phi = 0.5 + 0.5 * lax.erf(upper * (0.5**0.5))
        act = (upper * phi).astype(BF16)
        y = y + dot_nn(act, wdown_ref[cols, :])
        slope = phi + upper * (jnp.exp(-0.5 * upper * upper) * 0.3989422804014327)
        dup = (dot_nt(g, wdown_ref[cols, :]) * slope).astype(BF16)
        da2 = da2 + dot_nt(dup, wup_ref[:, cols])
        grad_down = dot_nn(flip(act), g).astype(BF16)
        for o in range(width // rows_down):
            sources[0][c * (width // rows_down) + o] = grad_down[o * rows_down : (o + 1) * rows_down]
        grad_up = dot_nn(a2_t, dup).astype(BF16)
        for o in range(groups):
            sources[1][o, c * rows_up : (c + 1) * rows_up] = grad_up[o * rows_up : (o + 1) * rows_up]
    down.stage1()
    up.stage1()
    y = y.astype(BF16)
    for o in range(groups):
        slots[0, o] = y[o * length : (o + 1) * length]
    send_back(0, ret_out)
    small_ref[0, 2:3, :] = jnp.sum(da2 * normal, axis=0, keepdims=True)
    small_ref[0, 3:4, :] = jnp.sum(da2, axis=0, keepdims=True)
    dres = g.astype(F32) + norm_back(da2 * gain_two, normal, scale)
    dres_ref[...] = dres
    dbr = dres.astype(BF16)
    grad_out = dot_nn(flip(att_ref[...]), dbr).astype(BF16)
    rows_out = width // groups
    for o in range(groups):
        sources[2][o] = grad_out[o * rows_out : (o + 1) * rows_out]
    out_sum.stage1()
    do_ref[...] = dot_nt(dbr, wout_ref[...]).astype(BF16)
    q_t[...] = flip(q_ref[...])
    do_t[...] = flip(do_ref[...])

    lane = lax.broadcasted_iota(jnp.int32, (tokens, PAIR), 1)
    extra = lax.rem(lane, HD)
    low_half = lane < HD
    swap = (
        (lax.broadcasted_iota(jnp.int32, (PAIR, PAIR), 0) < HD)
        != (lax.broadcasted_iota(jnp.int32, (PAIR, PAIR), 1) < HD)
    ).astype(BF16)

    def prepare(pair, _):
        cols = pl.ds(pl.multiple_of(pair * PAIR, PAIR), PAIR)
        prod = do_ref[:, cols].astype(F32) * att_ref[:, cols].astype(F32)
        prod_hi = prod.astype(BF16)
        prod_lo = (prod - prod_hi.astype(F32)).astype(BF16)
        delta = -(dot_nn(prod_hi, swap) + dot_nn(prod_lo, swap))
        delta_hi = delta.astype(BF16).astype(F32)
        lse = -lse_ref[:, cols]
        lse_hi = lse.astype(BF16).astype(F32)
        lse_mid = (lse - lse_hi).astype(BF16).astype(F32)
        lse_lo = lse - lse_hi - lse_mid
        q_extra = jnp.where(
            extra == HD - 3,
            lse_hi,
            jnp.where(extra == HD - 2, lse_mid, jnp.where(extra == HD - 1, lse_lo, qx_ref[...].astype(F32))),
        ).astype(BF16)
        do_extra = jnp.where(extra == 0, delta_hi, jnp.where(extra == 1, delta - delta_hi, 0.0)).astype(BF16)
        qaug[2 * pair] = jnp.where(low_half, q_ref[:, cols], q_extra)
        qaug[2 * pair + 1] = jnp.where(low_half, q_extra, q_ref[:, cols])
        doaug[2 * pair] = jnp.where(low_half, do_ref[:, cols], do_extra)
        doaug[2 * pair + 1] = jnp.where(low_half, do_extra, do_ref[:, cols])
        return _

    lax.fori_loop(0, H // 2, prepare, 0)
    dd[...] = jnp.zeros_like(dd)
    dq_acc[...] = jnp.zeros_like(dq_acc)
    halo = []

    def attend(chunk, first, count, jobs):
        span = count * QB
        keys = pl.ds(chunk * tokens, tokens)
        fresh = set()

        def body(pair, _):
            cols = pl.ds(pl.multiple_of(pair * PAIR, PAIR), PAIR)
            k_pair, v_pair, kx = k_ref[keys, cols], v_ref[keys, cols], kx_ref[keys, :]
            for h in range(2):
                mine = low_half if h == 0 else jnp.logical_not(low_half)
                head = 2 * pair + h
                bias[:, :span] = toeplitz(base_ref[pair, h : h + 1, first * QB : (first + count + 1) * QB])
                k_aug = jnp.where(mine, k_pair, kx)
                v_aug = jnp.where(mine, v_pair, jnp.ones_like(v_pair))
                feat = pl.ds(pl.multiple_of(head * HD, HD), HD)
                spot = pl.ds(h * HD, HD)
                fresh.clear()
                dq = [None] * per_chunk
                for kt in range(per_chunk):
                    part = slice(kt * QB, (kt + 1) * QB)
                    dk_t = dv_t = None
                    for b in range(per_chunk):
                        if (kt, b, chunk * per_chunk + kt - b) not in jobs:
                            continue
                        j = chunk * per_chunk + kt - b - first
                        here = pl.ds(b * QB, QB)
                        over = pl.ds(j * QB, QB)
                        p = jnp.exp(dot_nt(qaug[head, here, :], k_aug[part]) + bias[:, over])
                        ds = p * dot_nt(doaug[head, here, :], v_aug[part])
                        ds_low = ds.astype(BF16)
                        more_v = dot_nn(do_t[feat, here], p.astype(BF16))
                        more_k = dot_nn(q_t[feat, here], ds_low)
                        more_q = dot_nn(ds_low, k_pair[part])
                        dv_t = more_v if dv_t is None else dv_t + more_v
                        dk_t = more_k if dk_t is None else dk_t + more_k
                        dq[b] = more_q if dq[b] is None else dq[b] + more_q
                        if j in fresh:
                            dsum[:, over] += ds
                        else:
                            fresh.add(j)
                            dsum[:, over] = ds
                    dkt[spot, part] = dk_t
                    dvt[spot, part] = dv_t
                for b in range(per_chunk):
                    if dq[b] is not None:
                        here = pl.ds(b * QB, QB)
                        dq_acc[here, cols] += jnp.where(mine[:QB], dq[b], 0.0)
                left = jnp.concatenate([jnp.zeros((QB, QB), F32), dsum[:, :span]], axis=1)
                half = QB // 2
                while half:
                    left = left[:half] + pltpu.roll(left[half:], span + QB - half, 1)
                    half //= 2
                dd[pair, h : h + 1, first * QB : (first + count + 1) * QB] += left
            dkv[:, cols] = dkt[...].T.astype(BF16)
            dkv[:, pl.ds(pl.multiple_of(width + pair * PAIR, PAIR), PAIR)] = dvt[...].T.astype(BF16)
            return _

        lax.fori_loop(0, H // 2, body, 0)

    def halo_copy(step):
        return pltpu.make_async_remote_copy(
            src_ref=halo_send.at[step - 1], dst_ref=halo_land.at[step - 1],
            send_sem=halo_sems.at[0, step - 1], recv_sem=halo_sems.at[1, step - 1],
            device_id={"seq": lax.rem(seq + splits - 1, splits)}, device_id_type=pl.DeviceIdType.MESH,
        )

    grad_normed = None
    for index, (chunk, first, count, jobs) in enumerate(phase_spans(back, per_chunk, tiles)):
        attend(chunk, first, count, jobs)
        step = back - chunk
        part = dot_nt(dkv[...], wqkv_ref[:, width:])
        rows_t = flip(rows_ref[chunk * tokens : (chunk + 1) * tokens, :])
        if index == 0:
            gkv[...] = dot_nn(rows_t, dkv[...])
        else:
            gkv[...] += dot_nn(rows_t, dkv[...])
        if step == 0:
            dq_low = (dq_acc[...] * (HD**-0.5)).astype(BF16)
            grad_normed = part + dot_nt(dq_low, wqkv_ref[:, :width])
            grad_q = dot_nn(rows_t, dq_low).astype(BF16)
            for o in range(groups):
                take = slice(o * rows_up, (o + 1) * rows_up)
                sources[3][o, :rows_up] = grad_q[take]
                sources[3][o, rows_up : 2 * rows_up] = gkv[take, :width].astype(BF16)
                sources[3][o, 2 * rows_up :] = gkv[take, width:].astype(BF16)
            qkv_sum.stage1()
        else:
            if step < back:

                @pl.when((seq + 1 < splits) & (seq >= step))
                def _(step=step):
                    halo_copy(step + 1).wait_recv()

                arrived = jnp.where((seq + 1 < splits) & (seq >= step), halo_land[step].astype(F32), 0.0)
                part = part + arrived
            halo_send[step - 1] = part.astype(BF16)

            @pl.when(seq >= step)
            def _(step=step):
                halo_copy(step).start()

        if index == 0:
            down.stage2()
            up.stage2()
            out_sum.stage2()
        if index == back - 1 and back > 0:
            down.stage3()
    up.stage3()
    out_sum.stage3()
    qkv_sum.stage2()

    @pl.when(seq + 1 < splits)
    def _():
        halo_copy(1).wait_recv()

    grad_normed = grad_normed + jnp.where(seq + 1 < splits, halo_land[0].astype(F32), 0.0)
    normal, scale = norm_stats(x_ref[...].astype(F32))
    small_ref[0, 0:1, :] = jnp.sum(grad_normed * normal, axis=0, keepdims=True)
    small_ref[0, 1:2, :] = jnp.sum(grad_normed, axis=0, keepdims=True)
    small_ref[0, 4:8, :] = jnp.zeros((4, width), F32)
    dd_all = dd[...].reshape(H, dd.shape[-1])
    dd_hi = dd_all.astype(BF16)
    dd_mid = (dd_all - dd_hi.astype(F32)).astype(BF16)
    small_ref[0, 8:16, :PAIR] = dot_nn(dd_hi, hot_hi_ref[...]) + dot_nn(dd_mid, hot_hi_ref[...])
    small_ref[0, 8:16, PAIR:] = jnp.zeros((8, width - PAIR), F32)
    small = SmallSummer(small_ref, small_land, small_sems)
    small.pair()
    dx = (dres_ref[...] + norm_back(grad_normed * gains_ref[0:1, :], normal, scale)).astype(BF16)
    for o in range(groups):
        slots[1, o] = dx[o * length : (o + 1) * length]
    send_back(1, ret_grad)
    small.take()
    small.plane()
    down.stage4()
    up.stage4()
    qkv_sum.stage3()
    small.take()
    small.along()
    out_sum.stage4()
    qkv_sum.stage4()
    small.take()
    small_out[...] = small_ref[3]
    for summer in summers:
        summer.finish()
    small.finish()
    for copy in returns:
        copy.wait()
    for step in range(1, back + 1):

        @pl.when(seq >= step)
        def _(step=step):
            halo_copy(step).wait_send()


def rest(back, x, g, gains, wqkv, wout, wup, wdown, rows, base, hot, q, qx, k, kx, v, att, lse):
    splits, groups = lax.axis_size("seq"), lax.axis_size("dp")
    tokens, width = x.shape
    length = tokens // groups
    per_chunk = tokens // QB
    span = max(count for _, _, count, _ in phase_spans(back, per_chunk, base.shape[-1] // QB - 1)) * QB
    grads = [(wdown.shape[0] // groups), (wup.shape[1] // groups), width // groups, 3 * width // groups]
    out_shapes, more, sources = [], [], []
    for height in grads:
        shape = (groups, height, width)
        out, scratch = summer_shapes(shape, BF16, splits)
        sources.append(pltpu.VMEM(shape, BF16))
        out_shapes.append(out)
        more += scratch
    out_shapes.append(jax.ShapeDtypeStruct((16, width), F32))
    out_shapes += [jax.ShapeDtypeStruct((groups, length, width), BF16)] * 2
    small_copies = 1 + (groups // 2 - 1) + (splits - 1)
    scratch = sources + more + [
        pltpu.VMEM((4, 16, width), F32),
        pltpu.VMEM((small_copies, 16, width), F32),
        pltpu.SemaphoreType.DMA((2, small_copies)),
        pltpu.VMEM((2, groups, length, width), BF16),
        pltpu.SemaphoreType.DMA((2, 2, groups - 1)),
        pltpu.VMEM((back, tokens, width), BF16),
        pltpu.VMEM((back, tokens, width), BF16),
        pltpu.SemaphoreType.DMA((2, back)),
        pltpu.VMEM((tokens, width), F32),
        pltpu.VMEM((tokens, width), BF16),
        pltpu.VMEM((H, tokens, PAIR), BF16),
        pltpu.VMEM((H, tokens, PAIR), BF16),
        pltpu.VMEM((width, tokens), BF16),
        pltpu.VMEM((width, tokens), BF16),
        pltpu.VMEM((QB, span), F32),
        pltpu.VMEM((QB, span), F32),
        pltpu.VMEM(base.shape, F32),
        pltpu.VMEM((tokens, width), F32),
        pltpu.VMEM((PAIR, tokens), F32),
        pltpu.VMEM((PAIR, tokens), F32),
        pltpu.VMEM((tokens, 2 * width), BF16),
        pltpu.VMEM((width, 2 * width), F32),
    ]
    vmem = pl.BlockSpec(memory_space=pltpu.VMEM)
    return pl.pallas_call(
        functools.partial(rest_kernel, back),
        in_specs=[vmem] * 17,
        out_specs=[vmem] * len(out_shapes),
        out_shape=out_shapes,
        scratch_shapes=scratch,
        compiler_params=pltpu.CompilerParams(collective_id=1, has_side_effects=True, vmem_limit_bytes=VMEM_LIMIT),
        name="rest",
    )(x, g, gains, wqkv, wout, wup, wdown, rows, base, hot, q, qx, k, kx, v, att, lse)


def finish_kernel(deal_ref, down, up, out, qkv, ret_out, ret_grad, *outs):
    o_out, o_grad, o_qkv, o_wout, o_up, o_down = outs
    length = ret_out.shape[1]
    for g in range(ret_out.shape[0]):
        piece = deal_ref[0, g]
        o_out[pl.ds(g * length, length), :] = ret_out[piece]
        o_grad[pl.ds(g * length, length), :] = ret_grad[piece]
    for source, target in ((down, o_down), (up, o_up), (out, o_wout), (qkv, o_qkv)):
        direct = source.shape[0] * source.shape[1] * source.shape[2] != target.shape[0] * target.shape[1]
        cols = source.shape[2]
        if direct:
            value = add_low(*[source[t] for t in range(source.shape[0])])
        else:
            value = source[...].reshape(-1, cols).astype(F32)
        height = target.shape[0]
        for c in range(target.shape[1] // cols):
            target[:, c * cols : (c + 1) * cols] = value[c * height : (c + 1) * height]


def finish(deal, sums, returned, shapes):
    return pl.pallas_call(
        finish_kernel,
        in_specs=[pl.BlockSpec(memory_space=pltpu.SMEM)] + [pl.BlockSpec(memory_space=pltpu.VMEM)] * 6,
        out_specs=[pl.BlockSpec(memory_space=pltpu.VMEM)] * len(shapes),
        out_shape=shapes,
        compiler_params=pltpu.CompilerParams(vmem_limit_bytes=VMEM_LIMIT),
        name="finish",
    )(deal, *sums, *returned)


def swap_slots(values):
    return lax.all_to_all(values, "dp", split_axis=0, concat_axis=0, tiled=True)


def shards(
    tokens,
    cotangent,
    deal,
    lengths,
    buckets,
    ln1_gain,
    ln1_bias,
    w_qkv,
    w_out,
    rel_bias,
    ln2_gain,
    ln2_bias,
    w_up,
    w_down,
):
    groups = lax.axis_size("dp")
    splits = lax.axis_size("seq")
    tok_dev, width = tokens.shape
    block_len = tok_dev // groups
    maxlen = buckets.shape[0]
    back = -(-maxlen // tok_dev)
    window = (back + 1) * tok_dev
    span = back * tok_dev + QB
    chunk = lax.axis_index("seq")
    deal_row = deal[0]
    shard_rows = ln1_gain.shape[0]

    small = jnp.concatenate([ln1_gain, ln1_bias, ln2_gain, ln2_bias, rel_bias.reshape(-1)])
    wqkv_full = lax.all_gather(w_qkv, "dp", axis=0, tiled=True)
    small_full = lax.all_gather(small, "dp", axis=0, tiled=False)
    wout_full = lax.all_gather(w_out, "dp", axis=0, tiled=True)
    wup_full = lax.all_gather(w_up, "dp", axis=0, tiled=True)
    wdown_full = lax.all_gather(w_down, "dp", axis=0, tiled=True)
    gains = small_full[:, : 4 * shard_rows].reshape(groups, 4, shard_rows).transpose(1, 0, 2).reshape(4, width)
    gain_one, bias_one = (gains[i].astype(F32) for i in range(2))
    rel_full = small_full[:, 4 * shard_rows :].reshape(NBK, H)

    pieces = (groups, block_len, width)
    slot_in, slot_grad = to_slots(deal_row, [tokens.reshape(pieces), cotangent.reshape(pieces)])
    dealt = swap_slots(jnp.stack([slot_in, slot_grad], axis=1))
    x_rows = dealt[:, 0].reshape(tok_dev, width).astype(F32)
    grad_out = dealt[:, 1].reshape(tok_dev, width)

    ends, so_far = [], 0
    for c in range(lengths.shape[1]):
        so_far = so_far + lengths[0, c]
        ends.append(so_far)
    lane = lax.rem(jnp.arange(PAIR, dtype=jnp.int32), HD)[None, :]
    key_pos = (chunk - back) * tok_dev + jnp.arange(window, dtype=jnp.int32)
    key_seg = sum((key_pos >= e).astype(jnp.int32) for e in ends)
    key_seg = jnp.where(key_pos < 0, len(ends), key_seg)[:, None]
    query_seg = key_seg[back * tok_dev :]
    kx = jnp.where((lane == key_seg) | (lane >= HD - 3), 1.0, 0.0).astype(BF16)
    qx = jnp.where((lane <= len(ends)) & (lane != query_seg), BIG, 0.0).astype(BF16)
    offset = jnp.arange(span + QB, dtype=jnp.int32) - QB
    distance = back * tok_dev - offset
    in_reach = (distance >= 0) & (distance < maxlen) & (offset >= 0)
    table_bucket = jnp.concatenate(
        [
            jnp.zeros((QB + back * tok_dev + 1 - maxlen,), jnp.int32),
            buckets[::-1],
            jnp.zeros((QB - 1,), jnp.int32),
        ]
    )
    hot = (table_bucket[:, None] == jnp.arange(PAIR, dtype=jnp.int32)[None, :]) & in_reach[:, None]
    hot = hot.astype(BF16)
    base = jnp.einsum("cb,bh->hc", hot[:, :NBK], rel_full, preferred_element_type=F32)
    base = jnp.where(in_reach[None], base, BIG).reshape(H // 2, 2, span + QB)

    normed_low = norm_rows(x_rows, gain_one, bias_one).astype(BF16)
    earlier = [
        lax.ppermute(normed_low, "seq", [(i, i + step) for i in range(splits - step)]) for step in range(back, 0, -1)
    ]
    scale = HD**-0.5
    own_qkv = jnp.dot(normed_low, wqkv_full, preferred_element_type=F32).astype(BF16)
    rows_before = jnp.concatenate(earlier, axis=0)
    kv_before = jnp.dot(rows_before, wqkv_full[:, width:], preferred_element_type=F32).astype(BF16)
    queries = own_qkv[:, :width] * jnp.asarray(scale, BF16)
    keys_all = jnp.concatenate([kv_before[:, :width], own_qkv[:, width : 2 * width]], axis=0)
    values_all = jnp.concatenate([kv_before[:, width:], own_qkv[:, 2 * width :]], axis=0)
    attended, lse = attention_fwd(base, queries, qx, keys_all, kx, values_all)
    gains_all = jnp.pad(gains.astype(F32), ((0, 4), (0, 0)))
    *sums, small_total, back_out, back_grad = rest(
        back, dealt[:, 0].reshape(tok_dev, width), grad_out, gains_all, wqkv_full, wout_full, wup_full, wdown_full,
        jnp.concatenate([rows_before, normed_low], axis=0), base, hot, queries, qx, keys_all, kx, values_all, attended, lse,
    )
    output, grad_tokens, total_qkv, total_out, total_up, total_down = finish(
        deal,
        sums,
        [back_out, back_grad],
        [
            jax.ShapeDtypeStruct((tok_dev, width), BF16),
            jax.ShapeDtypeStruct((tok_dev, width), BF16),
            jax.ShapeDtypeStruct(w_qkv.shape, F32),
            jax.ShapeDtypeStruct(w_out.shape, F32),
            jax.ShapeDtypeStruct(w_up.shape, F32),
            jax.ShapeDtypeStruct(w_down.shape, F32),
        ],
    )
    slice_of = lax.axis_index("dp")
    cut = [lax.dynamic_slice_in_dim(small_total[i], slice_of * shard_rows, shard_rows) for i in range(4)]
    rel_rows = rel_bias.shape[0]
    total_rel = lax.dynamic_slice_in_dim(small_total[8 : 8 + H, :NBK].T, slice_of * rel_rows, rel_rows)
    return (
        output,
        grad_tokens,
        cut[0],
        cut[1],
        total_qkv,
        total_out,
        total_rel,
        cut[2],
        cut[3],
        total_up,
        total_down,
    )


def solution(mesh):
    by_all, by_dp = P(("seq", "dp"), None), P("dp", None)
    return jax.shard_map(
        shards,
        mesh=mesh,
        in_specs=(
            by_all, by_all, by_all, by_dp, P(), P("dp"), P("dp"), by_dp, by_dp, by_dp, P("dp"), P("dp"), by_dp, by_dp,
        ),
        out_specs=(by_all, by_all, P("dp"), P("dp"), by_dp, by_dp, by_dp, P("dp"), P("dp"), by_dp, by_dp),
        check_vma=False,
    )
```

```python
import functools

import jax
import jax.numpy as jnp
from jax import lax
from jax.experimental import pallas as pl
from jax.experimental.pallas import tpu as pltpu
from jax.sharding import PartitionSpec as P

H = 8
HD = 64
NBK = 32
QB = 256
PAIR = 2 * HD
BIG = -1e30
F32 = jnp.float32
BF16 = jnp.bfloat16
VMEM_LIMIT = 60 * 1024 * 1024

NT = (((1,), (1,)), ((), ()))
NN = (((1,), (0,)), ((), ()))


def dot_nt(a, b):
    return lax.dot_general(a, b, NT, preferred_element_type=F32)


def dot_nn(a, b):
    return lax.dot_general(a, b, NN, preferred_element_type=F32)


def toeplitz(row):
    width = row.shape[1]
    return pltpu.roll(jnp.broadcast_to(row, (QB, width)), 0, 1, stride=1, stride_axis=0)[:, QB:]


def add_low(first, *others):
    total = first.astype(F32)
    for other in others:
        total = total + other.astype(F32)
    return total


class Summer:
    def __init__(self, source, pair, recv2, mine, recv3, out, sems):
        self.source, self.pair, self.recv2 = source, pair, recv2
        self.mine, self.recv3, self.out, self.sems = mine, recv3, out, sems
        self.dp, self.seq = lax.axis_index("dp"), lax.axis_index("seq")
        self.pairs, self.splits = source.shape[0] // 2, lax.axis_size("seq")
        self.core, self.chip = lax.rem(self.dp, 2), self.dp // 2
        self.scatter = out.shape[1] < mine.shape[0]
        self.sent = []
        self.count = 0

    def send(self, src, dst, device):
        slot = self.count
        self.count += 1
        copy = pltpu.make_async_remote_copy(
            src_ref=src, dst_ref=dst, send_sem=self.sems.at[0, slot], recv_sem=self.sems.at[1, slot],
            device_id=device, device_id_type=pl.DeviceIdType.MESH,
        )
        copy.start()
        self.sent.append(copy)
        return copy

    def stage1(self):
        other = 1 - self.core
        self.first = [
            self.send(self.source.at[2 * k + other], self.pair.at[k], {"dp": self.dp + 1 - 2 * self.core})
            for k in range(self.pairs)
        ]

    def stage2(self):
        self.second = []
        for step in range(self.pairs):
            k = lax.rem(self.chip + 1 + step, self.pairs)
            if step == 0:
                for copy in self.first:
                    copy.wait_recv()
            self.pair[k] = add_low(self.source[2 * k + self.core], self.pair[k]).astype(self.pair.dtype)
            if step < self.pairs - 1:
                self.second.append(self.send(self.pair.at[k], self.recv2.at[step], {"dp": 2 * k + self.core}))

    def stage3(self):
        for copy in self.second:
            copy.wait_recv()
        total = add_low(self.pair[self.chip], *[self.recv2[step] for step in range(self.pairs - 1)])
        self.mine[...] = total.astype(self.mine.dtype)
        self.third = []
        rows = self.out.shape[1]
        for step in range(self.splits - 1):
            t = lax.rem(self.seq + 1 + step, self.splits)
            src = self.mine.at[pl.ds(pl.multiple_of(t * rows, rows), rows)] if self.scatter else self.mine
            dst = self.recv3.at[step] if self.scatter else self.out.at[self.seq]
            self.third.append(self.send(src, dst, {"seq": t}))
        if not self.scatter:
            self.out[self.seq] = self.mine[...]

    def stage4(self):
        for copy in self.third:
            copy.wait_recv()
        if not self.scatter:
            return
        rows = self.out.shape[1]
        own = self.mine[pl.ds(pl.multiple_of(self.seq * rows, rows), rows)]
        total = add_low(own, *[self.recv3[step] for step in range(self.splits - 1)])
        self.out[self.seq] = total.astype(self.out.dtype)
        self.fourth = [
            self.send(self.out.at[self.seq], self.out.at[self.seq], {"seq": lax.rem(self.seq + 1 + step, self.splits)})
            for step in range(self.splits - 1)
        ]

    def finish(self):
        if self.scatter:
            for copy in self.fourth:
                copy.wait_recv()
        for copy in self.sent:
            copy.wait_send()


def summer_shapes(shape, dtype, splits):
    groups, rows, cols = shape
    pairs = groups // 2
    scatter = rows % (16 * splits) == 0
    out = jax.ShapeDtypeStruct((splits, rows // splits if scatter else rows, cols), dtype)
    copies = pairs + (pairs - 1) + (splits - 1) * (2 if scatter else 1)
    scratch = [
        pltpu.VMEM((pairs, rows, cols), dtype),
        pltpu.VMEM((pairs - 1, rows, cols), dtype),
        pltpu.VMEM((rows, cols), dtype),
        pltpu.VMEM((splits - 1, out.shape[1] if scatter else 16, cols), dtype),
        pltpu.SemaphoreType.DMA((2, copies)),
    ]
    return out, scratch


def greet(peers):
    barrier = pltpu.get_barrier_semaphore()
    for device in peers:
        pl.semaphore_signal(barrier, inc=1, device_id=device, device_id_type=pl.DeviceIdType.MESH)
    pl.semaphore_wait(barrier, len(peers))


def others(axis):
    size, me = lax.axis_size(axis), lax.axis_index(axis)
    return [{axis: lax.rem(me + step, size)} for step in range(1, size)]


class SmallSummer:
    def __init__(self, ref, land, sems):
        self.ref, self.land, self.sems = ref, land, sems
        self.dp, self.seq = lax.axis_index("dp"), lax.axis_index("seq")
        self.pairs, self.splits = lax.axis_size("dp") // 2, lax.axis_size("seq")
        self.slot, self.copies, self.sent = 0, [], []

    def send(self, devices):
        self.copies = []
        for device in devices:
            copy = pltpu.make_async_remote_copy(
                src_ref=self.ref.at[len(self.sent)], dst_ref=self.land.at[self.slot],
                send_sem=self.sems.at[0, self.slot], recv_sem=self.sems.at[1, self.slot],
                device_id=device, device_id_type=pl.DeviceIdType.MESH,
            )
            copy.start()
            self.copies.append((self.slot, copy))
            self.slot += 1
        self.sent.append(self.copies)

    def take(self):
        stage = len(self.sent) - 1
        total = self.ref[stage]
        for slot, copy in self.copies:
            copy.wait_recv()
            total = total + self.land[slot]
        self.ref[stage + 1] = total

    def pair(self):
        self.send([{"dp": self.dp + 1 - 2 * lax.rem(self.dp, 2)}])

    def plane(self):
        core, chip = lax.rem(self.dp, 2), self.dp // 2
        self.send([{"dp": 2 * lax.rem(chip + step, self.pairs) + core} for step in range(1, self.pairs)])

    def along(self):
        self.send([{"seq": lax.rem(self.seq + step, self.splits)} for step in range(1, self.splits)])

    def finish(self):
        for copies in self.sent:
            for _, copy in copies:
                copy.wait_send()


def norm_stats(values):
    average = jnp.mean(values, axis=-1, keepdims=True)
    centred = values - average
    scale = lax.rsqrt(jnp.mean(centred * centred, axis=-1, keepdims=True) + 1e-05)
    return centred * scale, scale


def norm_back(grad, normal, scale):
    return scale * (
        grad - jnp.mean(grad, axis=-1, keepdims=True) - normal * jnp.mean(grad * normal, axis=-1, keepdims=True)
    )


def flip(values):
    return values.astype(F32).T.astype(BF16)


def phase_spans(back, per_chunk, tiles):
    spans = []
    for chunk in range(back + 1):
        jobs = [
            (kt, b, chunk * per_chunk + kt - b)
            for kt in range(per_chunk)
            for b in range(per_chunk)
            if 0 <= chunk * per_chunk + kt - b < tiles
        ]
        first, last = min(j[2] for j in jobs), max(j[2] for j in jobs)
        spans.append((chunk, first, last - first + 1, jobs))
    return spans


class Gather:
    def __init__(self, shard, full, sems, own_sem):
        self.shard, self.full, self.sems = shard, full, sems
        self.rows = shard.shape[0]
        self.dp = lax.axis_index("dp")
        self.pairs = lax.axis_size("dp") // 2
        self.core, self.chip = lax.rem(self.dp, 2), self.dp // 2
        self.sibling = {"dp": self.dp + 1 - 2 * self.core}
        self.own = pltpu.make_async_copy(shard, self.place(self.dp), own_sem)

    def place(self, owner):
        return self.full.at[pl.ds(pl.multiple_of(owner * self.rows, self.rows), self.rows)]

    def copy(self, src, owner, slot, device):
        return pltpu.make_async_remote_copy(
            src_ref=src, dst_ref=self.place(owner), send_sem=self.sems.at[0, slot], recv_sem=self.sems.at[1, slot],
            device_id=device, device_id_type=pl.DeviceIdType.MESH,
        )

    def start(self):
        self.sent = [
            self.copy(self.shard, self.dp, step, {"dp": 2 * lax.rem(self.chip + step, self.pairs) + self.core})
            for step in range(1, self.pairs)
        ]
        self.near = self.copy(self.shard, self.dp, 0, self.sibling)
        for copy in self.sent + [self.near]:
            copy.start()
        self.own.start()

    def relay(self):
        self.relayed = []
        for step in range(1, self.pairs):
            self.sent[step - 1].wait_recv()
            owner = 2 * lax.rem(self.chip + self.pairs - step, self.pairs) + self.core
            self.relayed.append(self.copy(self.place(owner), owner, self.pairs - 1 + step, self.sibling))
            self.relayed[-1].start()

    def arrive(self):
        self.own.wait()
        for copy in [self.near] + self.relayed:
            copy.wait_recv()

    def finish(self):
        for copy in self.sent + [self.near] + self.relayed:
            copy.wait_send()


def layer_kernel(back, maxlen, *refs):
    (
        tokens_ref, cotangent_ref, deal_ref, small_in, wqkv_s, wout_s, wup_s, wdown_s, hot_ref, qx_ref, kx_ref,
    ) = refs[:11]
    sum_down, sum_up, sum_out, sum_qkv, small_out, ret_out, ret_grad = refs[11:18]
    it = iter(refs[18:])
    sources = [next(it) for _ in range(4)]
    summers = [
        Summer(source, *[next(it) for _ in range(4)], out, next(it))
        for source, out in zip(sources, (sum_down, sum_up, sum_out, sum_qkv))
    ]
    down, up, out_sum, qkv_sum = summers
    small_ref, small_land, small_sems = next(it), next(it), next(it)
    slots, ret_sems, halo_send, halo_land, halo_sems = (next(it) for _ in range(5))
    dres_ref, do_ref, qaug, doaug, q_t, do_t = (next(it) for _ in range(6))
    bias, dsum, dd, dq_acc, dkt, dvt, dkv, gkv = (next(it) for _ in range(8))
    xwin, g_ref, wqkv_ref, wout_ref, wup_ref, wdown_ref = (next(it) for _ in range(6))
    gather_sems, own_sems, deal_sems, row_sems, few_land, few_sems = (next(it) for _ in range(6))
    gains_ref, base_ref, q_ref, k_ref, v_ref, att_ref, lse_ref = (next(it) for _ in range(7))
    dp, groups = lax.axis_index("dp"), lax.axis_size("dp")
    seq, splits = lax.axis_index("seq"), lax.axis_size("seq")
    tokens, width = tokens_ref.shape
    length = tokens // groups
    per_chunk = tokens // QB
    tiles = base_ref.shape[-1] // QB - 1
    spans = phase_spans(back, per_chunk, tiles)
    mesh_ids = pl.DeviceIdType.MESH
    greet(others("dp") + others("seq"))

    def deal_out(which, source, target, first_row):
        for j in range(groups):
            piece = source[:length, :]
            for k in range(1, groups):
                piece = jnp.where(deal_ref[0, k] == j, source[k * length : (k + 1) * length, :], piece)
            slots[which, j] = piece
        copies = []
        rows_here = pl.ds(pl.multiple_of(first_row + dp * length, length), length)
        for step in range(1, groups):
            peer = lax.rem(dp + step, groups)
            copy = pltpu.make_async_remote_copy(
                src_ref=slots.at[which, peer], dst_ref=target.at[rows_here],
                send_sem=deal_sems.at[0, which, step - 1], recv_sem=deal_sems.at[1, which, step - 1],
                device_id={"dp": peer}, device_id_type=mesh_ids,
            )
            copy.start()
            copies.append(copy)
        target[rows_here, :] = slots[which, dp]
        return copies

    own_first = back * tokens
    own_rows = pl.ds(own_first, tokens)
    dealt = deal_out(0, tokens_ref, xwin, own_first)
    few = []
    for step in range(1, groups):
        copy = pltpu.make_async_remote_copy(
            src_ref=small_in, dst_ref=few_land.at[step - 1],
            send_sem=few_sems.at[0, step - 1], recv_sem=few_sems.at[1, step - 1],
            device_id={"dp": lax.rem(dp + step, groups)}, device_id_type=mesh_ids,
        )
        copy.start()
        few.append(copy)
    gathers = [
        Gather(shard, full, gather_sems.at[i], own_sems.at[i])
        for i, (shard, full) in enumerate(
            ((wqkv_s, wqkv_ref), (wout_s, wout_ref), (wup_s, wup_ref), (wdown_s, wdown_ref))
        )
    ]
    gathers[0].start()
    for copy in dealt:
        copy.wait_recv()

    def row_copy(step):
        return pltpu.make_async_remote_copy(
            src_ref=xwin.at[pl.ds((back - step + 1) * tokens, tokens)],
            dst_ref=xwin.at[pl.ds((back - step) * tokens, tokens)],
            send_sem=row_sems.at[0, step - 1], recv_sem=row_sems.at[1, step - 1],
            device_id={"seq": lax.rem(seq + 1, splits)}, device_id_type=mesh_ids,
        )

    def row_send(step):
        @pl.when((seq + 1 < splits) & (seq + 1 >= step))
        def _():
            row_copy(step).start()

    def row_wait(step):
        @pl.when(seq >= step)
        def _():
            row_copy(step).wait_recv()

    row_send(1)
    dealt_grad = deal_out(1, cotangent_ref, g_ref, 0)
    for gather in gathers[1:]:
        gather.start()
    little = small_in[...].astype(F32)
    for step in range(1, groups):
        few[step - 1].wait_recv()
        little = little + few_land[step - 1].astype(F32)
    gains_ref[...] = little[:8]
    reach = lax.broadcasted_iota(jnp.int32, (H, base_ref.shape[-1]), 1) - QB
    far = back * tokens - reach
    table = dot_nt(little[8 : 8 + H, :PAIR].astype(BF16), hot_ref[...])
    base_ref[...] = jnp.where((far >= 0) & (far < maxlen) & (reach >= 0), table, BIG).reshape(base_ref.shape)

    def first_norm(chunk):
        normal, _ = norm_stats(xwin[chunk * tokens : (chunk + 1) * tokens, :].astype(F32))
        return (normal * gains_ref[0:1, :] + gains_ref[1:2, :]).astype(BF16)

    own_normed = first_norm(back)
    gathers[0].relay()
    gathers[0].arrive()
    q_ref[...] = (dot_nn(own_normed, wqkv_ref[:, :width])).astype(BF16) * jnp.asarray(HD**-0.5, BF16)
    k_ref[own_rows, :] = dot_nn(own_normed, wqkv_ref[:, width : 2 * width]).astype(BF16)
    v_ref[own_rows, :] = dot_nn(own_normed, wqkv_ref[:, 2 * width :]).astype(BF16)

    low_tile = lax.broadcasted_iota(jnp.int32, (QB, PAIR), 1) < HD

    def look(chunk, first, count, jobs):
        span = count * QB
        keys = pl.ds(chunk * tokens, tokens)
        started, last = chunk < back, chunk == 0

        def body(pair, _):
            cols = pl.ds(pl.multiple_of(pair * PAIR, PAIR), PAIR)
            k_pair, v_pair, kx = k_ref[keys, cols], v_ref[keys, cols], kx_ref[keys, :]
            low_k = lax.broadcasted_iota(jnp.int32, (tokens, PAIR), 1) < HD
            for h in range(2):
                mine_k = low_k if h == 0 else jnp.logical_not(low_k)
                mine = low_tile if h == 0 else jnp.logical_not(low_tile)
                bias[:, :span] = toeplitz(base_ref[pair, h : h + 1, first * QB : (first + count + 1) * QB])
                k_aug = jnp.where(mine_k, k_pair, kx)
                v_aug = jnp.where(mine_k, v_pair, jnp.ones_like(v_pair))
                held = pl.ds(pl.multiple_of((2 * pair + h) * PAIR, PAIR), PAIR)
                for b in range(per_chunk):
                    here = pl.ds(b * QB, QB)
                    work = [(kt, j - first) for kt, block, j in jobs if block == b]
                    q_aug = jnp.where(mine, q_ref[here, cols], qx_ref[here, :])
                    top = None
                    for kt, j in work:
                        over = pl.ds(j * QB, QB)
                        score = dot_nt(q_aug, k_aug[kt * QB : (kt + 1) * QB]) + bias[:, over]
                        dsum[:, over] = score
                        most = jnp.maximum(score[:, :128], score[:, 128:])
                        top = most if top is None else jnp.maximum(top, most)
                    top = jnp.max(top, axis=1, keepdims=True)
                    acc = None
                    if started:
                        lane_at = HD if h == 0 else 0
                        before = lse_ref[here, cols][:, lane_at : lane_at + 1]
                        top = jnp.maximum(top, before)
                        acc = gkv[here, held] * jnp.exp(before - top)
                    for kt, j in work:
                        p = jnp.exp(dsum[:, pl.ds(j * QB, QB)] - top).astype(BF16)
                        more = dot_nn(p, v_aug[kt * QB : (kt + 1) * QB])
                        acc = more if acc is None else acc + more
                    if last:
                        value = (acc / pltpu.roll(acc, HD, 1)).astype(BF16)
                        att_ref[here, cols] = value if h == 0 else jnp.where(mine, value, att_ref[here, cols])
                        stat = top + jnp.log(acc)
                    else:
                        gkv[here, held] = acc
                        stat = jnp.broadcast_to(top, (QB, PAIR))
                    lse_ref[here, cols] = jnp.where(mine, lse_ref[here, cols], stat)
            return _

        lax.fori_loop(0, H // 2, body, 0)

    for chunk, first, count, jobs in reversed(spans):
        step = back - chunk
        if step > 0:
            row_wait(step)
            if step < back:
                row_send(step + 1)
            normed = jnp.where(seq >= step, first_norm(chunk).astype(F32), 0.0).astype(BF16)
            here = pl.ds(chunk * tokens, tokens)
            k_ref[here, :] = dot_nn(normed, wqkv_ref[:, width : 2 * width]).astype(BF16)
            v_ref[here, :] = dot_nn(normed, wqkv_ref[:, 2 * width :]).astype(BF16)
        look(chunk, first, count, jobs)
        if step == 0:
            gathers[1].relay()
            gathers[2].relay()
    gathers[3].relay()
    for gather in gathers[1:]:
        gather.arrive()
    for copy in dealt_grad:
        copy.wait_recv()
    for copy in dealt + dealt_grad:
        copy.wait_send()

    returns = []

    def send_back(which, landed):
        landed[dp] = slots[which, dp]
        for step in range(1, groups):
            peer = lax.rem(dp + step, groups)
            copy = pltpu.make_async_remote_copy(
                src_ref=slots.at[which, peer], dst_ref=landed.at[dp],
                send_sem=ret_sems.at[0, which, step - 1], recv_sem=ret_sems.at[1, which, step - 1],
                device_id={"dp": peer}, device_id_type=mesh_ids,
            )
            copy.start()
            returns.append(copy)

    resid = xwin[own_rows, :].astype(F32) + dot_nn(att_ref[...], wout_ref[...])
    normal, scale = norm_stats(resid)
    gain_two = gains_ref[2:3, :]
    a2 = (normal * gain_two + gains_ref[3:4, :]).astype(BF16)
    a2_t = flip(a2)
    g = g_ref[...]
    y = resid
    da2 = jnp.zeros((tokens, width), F32)
    rows_up, rows_down = width // groups, wdown_ref.shape[0] // groups
    for c in range(wdown_ref.shape[0] // width):
        cols = pl.ds(c * width, width)
        upper = dot_nn(a2, wup_ref[:, cols])
        phi = 0.5 + 0.5 * lax.erf(upper * (0.5**0.5))
        act = (upper * phi).astype(BF16)
        y = y + dot_nn(act, wdown_ref[cols, :])
        slope = phi + upper * (jnp.exp(-0.5 * upper * upper) * 0.3989422804014327)
        dup = (dot_nt(g, wdown_ref[cols, :]) * slope).astype(BF16)
        da2 = da2 + dot_nt(dup, wup_ref[:, cols])
        grad_down = dot_nn(flip(act), g).astype(BF16)
        for o in range(width // rows_down):
            sources[0][c * (width // rows_down) + o] = grad_down[o * rows_down : (o + 1) * rows_down]
        grad_up = dot_nn(a2_t, dup).astype(BF16)
        for o in range(groups):
            sources[1][o, c * rows_up : (c + 1) * rows_up] = grad_up[o * rows_up : (o + 1) * rows_up]
    down.stage1()
    up.stage1()
    y = y.astype(BF16)
    for o in range(groups):
        slots[0, o] = y[o * length : (o + 1) * length]
    send_back(0, ret_out)
    small_ref[0, 2:3, :] = jnp.sum(da2 * normal, axis=0, keepdims=True)
    small_ref[0, 3:4, :] = jnp.sum(da2, axis=0, keepdims=True)
    dres = g.astype(F32) + norm_back(da2 * gain_two, normal, scale)
    dres_ref[...] = dres
    dbr = dres.astype(BF16)
    grad_out = dot_nn(flip(att_ref[...]), dbr).astype(BF16)
    rows_out = width // groups
    for o in range(groups):
        sources[2][o] = grad_out[o * rows_out : (o + 1) * rows_out]
    out_sum.stage1()
    do_ref[...] = dot_nt(dbr, wout_ref[...]).astype(BF16)
    q_t[...] = flip(q_ref[...])
    do_t[...] = flip(do_ref[...])

    lane = lax.broadcasted_iota(jnp.int32, (tokens, PAIR), 1)
    extra = lax.rem(lane, HD)
    low_half = lane < HD
    swap = (
        (lax.broadcasted_iota(jnp.int32, (PAIR, PAIR), 0) < HD)
        != (lax.broadcasted_iota(jnp.int32, (PAIR, PAIR), 1) < HD)
    ).astype(BF16)

    def prepare(pair, _):
        cols = pl.ds(pl.multiple_of(pair * PAIR, PAIR), PAIR)
        prod = do_ref[:, cols].astype(F32) * att_ref[:, cols].astype(F32)
        prod_hi = prod.astype(BF16)
        prod_lo = (prod - prod_hi.astype(F32)).astype(BF16)
        delta = -(dot_nn(prod_hi, swap) + dot_nn(prod_lo, swap))
        delta_hi = delta.astype(BF16).astype(F32)
        lse = -lse_ref[:, cols]
        lse_hi = lse.astype(BF16).astype(F32)
        lse_mid = (lse - lse_hi).astype(BF16).astype(F32)
        lse_lo = lse - lse_hi - lse_mid
        q_extra = jnp.where(
            extra == HD - 3,
            lse_hi,
            jnp.where(extra == HD - 2, lse_mid, jnp.where(extra == HD - 1, lse_lo, qx_ref[...].astype(F32))),
        ).astype(BF16)
        do_extra = jnp.where(extra == 0, delta_hi, jnp.where(extra == 1, delta - delta_hi, 0.0)).astype(BF16)
        qaug[2 * pair] = jnp.where(low_half, q_ref[:, cols], q_extra)
        qaug[2 * pair + 1] = jnp.where(low_half, q_extra, q_ref[:, cols])
        doaug[2 * pair] = jnp.where(low_half, do_ref[:, cols], do_extra)
        doaug[2 * pair + 1] = jnp.where(low_half, do_extra, do_ref[:, cols])
        return _

    lax.fori_loop(0, H // 2, prepare, 0)
    dd[...] = jnp.zeros_like(dd)
    dq_acc[...] = jnp.zeros_like(dq_acc)
    halo = []

    def attend(chunk, first, count, jobs):
        span = count * QB
        keys = pl.ds(chunk * tokens, tokens)
        fresh = set()

        def body(pair, _):
            cols = pl.ds(pl.multiple_of(pair * PAIR, PAIR), PAIR)
            k_pair, v_pair, kx = k_ref[keys, cols], v_ref[keys, cols], kx_ref[keys, :]
            for h in range(2):
                mine = low_half if h == 0 else jnp.logical_not(low_half)
                head = 2 * pair + h
                bias[:, :span] = toeplitz(base_ref[pair, h : h + 1, first * QB : (first + count + 1) * QB])
                k_aug = jnp.where(mine, k_pair, kx)
                v_aug = jnp.where(mine, v_pair, jnp.ones_like(v_pair))
                feat = pl.ds(pl.multiple_of(head * HD, HD), HD)
                spot = pl.ds(h * HD, HD)
                fresh.clear()
                dq = [None] * per_chunk
                for kt in range(per_chunk):
                    part = slice(kt * QB, (kt + 1) * QB)
                    dk_t = dv_t = None
                    for b in range(per_chunk):
                        if (kt, b, chunk * per_chunk + kt - b) not in jobs:
                            continue
                        j = chunk * per_chunk + kt - b - first
                        here = pl.ds(b * QB, QB)
                        over = pl.ds(j * QB, QB)
                        p = jnp.exp(dot_nt(qaug[head, here, :], k_aug[part]) + bias[:, over])
                        ds = p * dot_nt(doaug[head, here, :], v_aug[part])
                        ds_low = ds.astype(BF16)
                        more_v = dot_nn(do_t[feat, here], p.astype(BF16))
                        more_k = dot_nn(q_t[feat, here], ds_low)
                        more_q = dot_nn(ds_low, k_pair[part])
                        dv_t = more_v if dv_t is None else dv_t + more_v
                        dk_t = more_k if dk_t is None else dk_t + more_k
                        dq[b] = more_q if dq[b] is None else dq[b] + more_q
                        if j in fresh:
                            dsum[:, over] += ds
                        else:
                            fresh.add(j)
                            dsum[:, over] = ds
                    dkt[spot, part] = dk_t
                    dvt[spot, part] = dv_t
                for b in range(per_chunk):
                    if dq[b] is not None:
                        here = pl.ds(b * QB, QB)
                        dq_acc[here, cols] += jnp.where(mine[:QB], dq[b], 0.0)
                left = jnp.concatenate([jnp.zeros((QB, QB), F32), dsum[:, :span]], axis=1)
                half = QB // 2
                while half:
                    left = left[:half] + pltpu.roll(left[half:], span + QB - half, 1)
                    half //= 2
                dd[pair, h : h + 1, first * QB : (first + count + 1) * QB] += left
            dkv[:, cols] = dkt[...].T.astype(BF16)
            dkv[:, pl.ds(pl.multiple_of(width + pair * PAIR, PAIR), PAIR)] = dvt[...].T.astype(BF16)
            return _

        lax.fori_loop(0, H // 2, body, 0)

    def halo_copy(step):
        return pltpu.make_async_remote_copy(
            src_ref=halo_send.at[step - 1], dst_ref=halo_land.at[step - 1],
            send_sem=halo_sems.at[0, step - 1], recv_sem=halo_sems.at[1, step - 1],
            device_id={"seq": lax.rem(seq + splits - 1, splits)}, device_id_type=pl.DeviceIdType.MESH,
        )

    grad_normed = None
    for index, (chunk, first, count, jobs) in enumerate(spans):
        attend(chunk, first, count, jobs)
        step = back - chunk
        part = dot_nt(dkv[...], wqkv_ref[:, width:])
        rows_t = first_norm(chunk)
        if step > 0:
            rows_t = jnp.where(seq >= step, rows_t.astype(F32), 0.0)
        rows_t = flip(rows_t)
        if index == 0:
            gkv[...] = dot_nn(rows_t, dkv[...])
        else:
            gkv[...] += dot_nn(rows_t, dkv[...])
        if step == 0:
            dq_low = (dq_acc[...] * (HD**-0.5)).astype(BF16)
            grad_normed = part + dot_nt(dq_low, wqkv_ref[:, :width])
            grad_q = dot_nn(rows_t, dq_low).astype(BF16)
            for o in range(groups):
                take = slice(o * rows_up, (o + 1) * rows_up)
                sources[3][o, :rows_up] = grad_q[take]
                sources[3][o, rows_up : 2 * rows_up] = gkv[take, :width].astype(BF16)
                sources[3][o, 2 * rows_up :] = gkv[take, width:].astype(BF16)
            qkv_sum.stage1()
        else:
            if step < back:

                @pl.when((seq + 1 < splits) & (seq >= step))
                def _(step=step):
                    halo_copy(step + 1).wait_recv()

                arrived = jnp.where((seq + 1 < splits) & (seq >= step), halo_land[step].astype(F32), 0.0)
                part = part + arrived
            halo_send[step - 1] = part.astype(BF16)

            @pl.when(seq >= step)
            def _(step=step):
                halo_copy(step).start()

        if index == 0:
            down.stage2()
            up.stage2()
            out_sum.stage2()
        if index == back - 1 and back > 0:
            down.stage3()
    up.stage3()
    out_sum.stage3()
    qkv_sum.stage2()

    @pl.when(seq + 1 < splits)
    def _():
        halo_copy(1).wait_recv()

    grad_normed = grad_normed + jnp.where(seq + 1 < splits, halo_land[0].astype(F32), 0.0)
    normal, scale = norm_stats(xwin[own_rows, :].astype(F32))
    small_ref[0, 0:1, :] = jnp.sum(grad_normed * normal, axis=0, keepdims=True)
    small_ref[0, 1:2, :] = jnp.sum(grad_normed, axis=0, keepdims=True)
    small_ref[0, 4:8, :] = jnp.zeros((4, width), F32)
    dd_all = dd[...].reshape(H, dd.shape[-1])
    dd_hi = dd_all.astype(BF16)
    dd_mid = (dd_all - dd_hi.astype(F32)).astype(BF16)
    small_ref[0, 8:16, :PAIR] = dot_nn(dd_hi, hot_ref[...]) + dot_nn(dd_mid, hot_ref[...])
    small_ref[0, 8:16, PAIR:] = jnp.zeros((8, width - PAIR), F32)
    small = SmallSummer(small_ref, small_land, small_sems)
    small.pair()
    dx = (dres_ref[...] + norm_back(grad_normed * gains_ref[0:1, :], normal, scale)).astype(BF16)
    for o in range(groups):
        slots[1, o] = dx[o * length : (o + 1) * length]
    send_back(1, ret_grad)
    small.take()
    small.plane()
    down.stage4()
    up.stage4()
    qkv_sum.stage3()
    small.take()
    small.along()
    out_sum.stage4()
    qkv_sum.stage4()
    small.take()
    small_out[...] = small_ref[3]
    for summer in summers:
        summer.finish()
    small.finish()
    for copy in returns:
        copy.wait()
    for gather in gathers:
        gather.finish()
    for copy in few:
        copy.wait_send()
    for step in range(1, back + 1):

        @pl.when((seq + 1 < splits) & (seq + 1 >= step))
        def _(step=step):
            row_copy(step).wait_send()
    for step in range(1, back + 1):

        @pl.when(seq >= step)
        def _(step=step):
            halo_copy(step).wait_send()


def layer(back, maxlen, tokens_in, cotangent, deal, small, wqkv, wout, wup, wdown, hot, qx, kx):
    splits, groups = lax.axis_size("seq"), lax.axis_size("dp")
    tokens, width = tokens_in.shape
    length = tokens // groups
    per_chunk = tokens // QB
    window, reach = kx.shape[0], hot.shape[0]
    span = max(count for _, _, count, _ in phase_spans(back, per_chunk, reach // QB - 1)) * QB
    grads = [wdown.shape[0], wup.shape[0] * wup.shape[1] // width, width // groups, 3 * width // groups]
    out_shapes, more, sources = [], [], []
    for height in grads:
        shape = (groups, height, width)
        out, scratch = summer_shapes(shape, BF16, splits)
        sources.append(pltpu.VMEM(shape, BF16))
        out_shapes.append(out)
        more += scratch
    out_shapes.append(jax.ShapeDtypeStruct((16, width), F32))
    out_shapes += [jax.ShapeDtypeStruct((groups, length, width), BF16)] * 2
    small_copies = 1 + (groups // 2 - 1) + (splits - 1)
    scratch = sources + more + [
        pltpu.VMEM((4, 16, width), F32),
        pltpu.VMEM((small_copies, 16, width), F32),
        pltpu.SemaphoreType.DMA((2, small_copies)),
        pltpu.VMEM((2, groups, length, width), BF16),
        pltpu.SemaphoreType.DMA((2, 2, groups - 1)),
        pltpu.VMEM((back, tokens, width), BF16),
        pltpu.VMEM((back, tokens, width), BF16),
        pltpu.SemaphoreType.DMA((2, back)),
        pltpu.VMEM((tokens, width), F32),
        pltpu.VMEM((tokens, width), BF16),
        pltpu.VMEM((H, tokens, PAIR), BF16),
        pltpu.VMEM((H, tokens, PAIR), BF16),
        pltpu.VMEM((width, tokens), BF16),
        pltpu.VMEM((width, tokens), BF16),
        pltpu.VMEM((QB, span), F32),
        pltpu.VMEM((QB, span), F32),
        pltpu.VMEM((H // 2, 2, reach), F32),
        pltpu.VMEM((tokens, width), F32),
        pltpu.VMEM((PAIR, tokens), F32),
        pltpu.VMEM((PAIR, tokens), F32),
        pltpu.VMEM((tokens, 2 * width), BF16),
        pltpu.VMEM((width, 2 * width), F32),
        pltpu.VMEM((window, width), BF16),
        pltpu.VMEM((tokens, width), BF16),
        pltpu.VMEM((width, 3 * width), BF16),
        pltpu.VMEM((width, width), BF16),
        pltpu.VMEM((width, wup.shape[1]), BF16),
        pltpu.VMEM((wup.shape[1], width), BF16),
        pltpu.SemaphoreType.DMA((4, 2, groups - 1)),
        pltpu.SemaphoreType.DMA((4,)),
        pltpu.SemaphoreType.DMA((2, 2, groups - 1)),
        pltpu.SemaphoreType.DMA((2, back)),
        pltpu.VMEM((groups - 1, 16, width), BF16),
        pltpu.SemaphoreType.DMA((2, groups - 1)),
        pltpu.VMEM((8, width), F32),
        pltpu.VMEM((H // 2, 2, reach), F32),
        pltpu.VMEM((tokens, width), BF16),
        pltpu.VMEM((window, width), BF16),
        pltpu.VMEM((window, width), BF16),
        pltpu.VMEM((tokens, width), BF16),
        pltpu.VMEM((tokens, width), F32),
    ]
    vmem = pl.BlockSpec(memory_space=pltpu.VMEM)
    return pl.pallas_call(
        functools.partial(layer_kernel, back, maxlen),
        in_specs=[vmem, vmem, pl.BlockSpec(memory_space=pltpu.SMEM), vmem] + [pl.BlockSpec(memory_space=pl.ANY)] * 4 + [vmem] * 3,
        out_specs=[vmem] * len(out_shapes),
        out_shape=out_shapes,
        scratch_shapes=scratch,
        compiler_params=pltpu.CompilerParams(collective_id=1, has_side_effects=True, vmem_limit_bytes=VMEM_LIMIT),
        name="layer",
    )(tokens_in, cotangent, deal, small, wqkv, wout, wup, wdown, hot, qx, kx)


def finish_kernel(deal_ref, down, up, out, qkv, ret_out, ret_grad, *outs):
    o_out, o_grad, o_qkv, o_wout, o_up, o_down = outs
    length = ret_out.shape[1]
    for g in range(ret_out.shape[0]):
        piece = deal_ref[0, g]
        o_out[pl.ds(g * length, length), :] = ret_out[piece]
        o_grad[pl.ds(g * length, length), :] = ret_grad[piece]
    for source, target in ((down, o_down), (up, o_up), (out, o_wout), (qkv, o_qkv)):
        direct = source.shape[0] * source.shape[1] * source.shape[2] != target.shape[0] * target.shape[1]
        cols = source.shape[2]
        if direct:
            value = add_low(*[source[t] for t in range(source.shape[0])])
        else:
            value = source[...].reshape(-1, cols).astype(F32)
        height = target.shape[0]
        for c in range(target.shape[1] // cols):
            target[:, c * cols : (c + 1) * cols] = value[c * height : (c + 1) * height]


def finish(deal, sums, returned, shapes):
    return pl.pallas_call(
        finish_kernel,
        in_specs=[pl.BlockSpec(memory_space=pltpu.SMEM)] + [pl.BlockSpec(memory_space=pltpu.VMEM)] * 6,
        out_specs=[pl.BlockSpec(memory_space=pltpu.VMEM)] * len(shapes),
        out_shape=shapes,
        compiler_params=pltpu.CompilerParams(vmem_limit_bytes=VMEM_LIMIT),
        name="finish",
    )(deal, *sums, *returned)


def shards(
    tokens,
    cotangent,
    deal,
    lengths,
    buckets,
    ln1_gain,
    ln1_bias,
    w_qkv,
    w_out,
    rel_bias,
    ln2_gain,
    ln2_bias,
    w_up,
    w_down,
):
    groups = lax.axis_size("dp")
    splits = lax.axis_size("seq")
    tok_dev, width = tokens.shape
    maxlen = buckets.shape[0]
    back = -(-maxlen // tok_dev)
    window = (back + 1) * tok_dev
    span = back * tok_dev + QB
    chunk = lax.axis_index("seq")
    shard_rows = ln1_gain.shape[0]

    slice_of = lax.axis_index("dp")
    vectors = jnp.stack([jnp.tile(v, groups) for v in (ln1_gain, ln1_bias, ln2_gain, ln2_bias)])
    vectors = jnp.where(jnp.arange(width)[None, :] // shard_rows == slice_of, vectors, 0)
    rel_rows = rel_bias.shape[0]
    scores = jnp.tile(rel_bias.T, (1, groups))
    scores = jnp.where(jnp.arange(NBK)[None, :] // rel_rows == slice_of, scores, 0)
    small = jnp.concatenate([jnp.pad(vectors, ((0, 4), (0, 0))), jnp.pad(scores, ((0, 0), (0, width - NBK)))], axis=0)

    ends, so_far = [], 0
    for c in range(lengths.shape[1]):
        so_far = so_far + lengths[0, c]
        ends.append(so_far)
    lane = lax.rem(jnp.arange(PAIR, dtype=jnp.int32), HD)[None, :]
    key_pos = (chunk - back) * tok_dev + jnp.arange(window, dtype=jnp.int32)
    key_seg = sum((key_pos >= e).astype(jnp.int32) for e in ends)
    key_seg = jnp.where(key_pos < 0, len(ends), key_seg)[:, None]
    query_seg = key_seg[back * tok_dev :]
    kx = jnp.where((lane == key_seg) | (lane >= HD - 3), 1.0, 0.0).astype(BF16)
    qx = jnp.where((lane <= len(ends)) & (lane != query_seg), BIG, 0.0).astype(BF16)
    offset = jnp.arange(span + QB, dtype=jnp.int32) - QB
    distance = back * tok_dev - offset
    in_reach = (distance >= 0) & (distance < maxlen) & (offset >= 0)
    table_bucket = jnp.concatenate(
        [
            jnp.zeros((QB + back * tok_dev + 1 - maxlen,), jnp.int32),
            buckets[::-1],
            jnp.zeros((QB - 1,), jnp.int32),
        ]
    )
    hot = (table_bucket[:, None] == jnp.arange(PAIR, dtype=jnp.int32)[None, :]) & in_reach[:, None]
    hot = hot.astype(BF16)
    *sums, small_total, back_out, back_grad = layer(
        back, maxlen, tokens, cotangent, deal, small, w_qkv, w_out, w_up, w_down, hot, qx, kx
    )
    output, grad_tokens, total_qkv, total_out, total_up, total_down = finish(
        deal,
        sums,
        [back_out, back_grad],
        [
            jax.ShapeDtypeStruct((tok_dev, width), BF16),
            jax.ShapeDtypeStruct((tok_dev, width), BF16),
            jax.ShapeDtypeStruct(w_qkv.shape, F32),
            jax.ShapeDtypeStruct(w_out.shape, F32),
            jax.ShapeDtypeStruct(w_up.shape, F32),
            jax.ShapeDtypeStruct(w_down.shape, F32),
        ],
    )
    cut = [lax.dynamic_slice_in_dim(small_total[i], slice_of * shard_rows, shard_rows) for i in range(4)]
    total_rel = lax.dynamic_slice_in_dim(small_total[8 : 8 + H, :NBK].T, slice_of * rel_rows, rel_rows)
    return (
        output,
        grad_tokens,
        cut[0],
        cut[1],
        total_qkv,
        total_out,
        total_rel,
        cut[2],
        cut[3],
        total_up,
        total_down,
    )


def solution(mesh):
    by_all, by_dp = P(("seq", "dp"), None), P("dp", None)
    return jax.shard_map(
        shards,
        mesh=mesh,
        in_specs=(
            by_all, by_all, by_all, by_dp, P(), P("dp"), P("dp"), by_dp, by_dp, by_dp, P("dp"), P("dp"), by_dp, by_dp,
        ),
        out_specs=(by_all, by_all, P("dp"), P("dp"), by_dp, by_dp, by_dp, P("dp"), P("dp"), by_dp, by_dp),
        check_vma=False,
    )
```

```python
import functools

import jax
import jax.numpy as jnp
from jax import lax
from jax.experimental import pallas as pl
from jax.experimental.pallas import tpu as pltpu
from jax.sharding import PartitionSpec as P

H = 8
HD = 64
NBK = 32
QB = 256
PAIR = 2 * HD
BIG = -1e30
F32 = jnp.float32
BF16 = jnp.bfloat16
VMEM_LIMIT = 60 * 1024 * 1024

NT = (((1,), (1,)), ((), ()))
NN = (((1,), (0,)), ((), ()))


def dot_nt(a, b):
    return lax.dot_general(a, b, NT, preferred_element_type=F32)


def dot_nn(a, b):
    return lax.dot_general(a, b, NN, preferred_element_type=F32)


def toeplitz(row):
    width = row.shape[1]
    return pltpu.roll(jnp.broadcast_to(row, (QB, width)), 0, 1, stride=1, stride_axis=0)[:, QB:]


def add_low(first, *others):
    total = first.astype(F32)
    for other in others:
        total = total + other.astype(F32)
    return total


class Summer:
    def __init__(self, source, pair, recv2, mine, recv3, out, sems):
        self.source, self.pair, self.recv2 = source, pair, recv2
        self.mine, self.recv3, self.out, self.sems = mine, recv3, out, sems
        self.dp, self.seq = lax.axis_index("dp"), lax.axis_index("seq")
        self.pairs, self.splits = source.shape[0] // 2, lax.axis_size("seq")
        self.core, self.chip = lax.rem(self.dp, 2), self.dp // 2
        self.scatter = out.shape[1] < mine.shape[0]
        self.sent = []
        self.count = 0

    def send(self, src, dst, device):
        slot = self.count
        self.count += 1
        copy = pltpu.make_async_remote_copy(
            src_ref=src, dst_ref=dst, send_sem=self.sems.at[0, slot], recv_sem=self.sems.at[1, slot],
            device_id=device, device_id_type=pl.DeviceIdType.MESH,
        )
        copy.start()
        self.sent.append(copy)
        return copy

    def stage1(self):
        other = 1 - self.core
        self.first = [
            self.send(self.source.at[2 * k + other], self.pair.at[k], {"dp": self.dp + 1 - 2 * self.core})
            for k in range(self.pairs)
        ]

    def stage2(self):
        self.second = []
        for step in range(self.pairs):
            k = lax.rem(self.chip + 1 + step, self.pairs)
            if step == 0:
                for copy in self.first:
                    copy.wait_recv()
            self.pair[k] = add_low(self.source[2 * k + self.core], self.pair[k]).astype(self.pair.dtype)
            if step < self.pairs - 1:
                self.second.append(self.send(self.pair.at[k], self.recv2.at[step], {"dp": 2 * k + self.core}))

    def stage3(self):
        for copy in self.second:
            copy.wait_recv()
        total = add_low(self.pair[self.chip], *[self.recv2[step] for step in range(self.pairs - 1)])
        self.mine[...] = total.astype(self.mine.dtype)
        self.third = []
        rows = self.out.shape[1]
        for step in range(self.splits - 1):
            t = lax.rem(self.seq + 1 + step, self.splits)
            src = self.mine.at[pl.ds(pl.multiple_of(t * rows, rows), rows)] if self.scatter else self.mine
            dst = self.recv3.at[step] if self.scatter else self.out.at[self.seq]
            self.third.append(self.send(src, dst, {"seq": t}))
        if not self.scatter:
            self.out[self.seq] = self.mine[...]

    def stage4(self):
        for copy in self.third:
            copy.wait_recv()
        if not self.scatter:
            return
        rows = self.out.shape[1]
        own = self.mine[pl.ds(pl.multiple_of(self.seq * rows, rows), rows)]
        total = add_low(own, *[self.recv3[step] for step in range(self.splits - 1)])
        self.out[self.seq] = total.astype(self.out.dtype)
        self.fourth = [
            self.send(self.out.at[self.seq], self.out.at[self.seq], {"seq": lax.rem(self.seq + 1 + step, self.splits)})
            for step in range(self.splits - 1)
        ]

    def finish(self):
        if self.scatter:
            for copy in self.fourth:
                copy.wait_recv()
        for copy in self.sent:
            copy.wait_send()


def summer_shapes(shape, dtype, splits):
    groups, rows, cols = shape
    pairs = groups // 2
    scatter = rows % (16 * splits) == 0
    out = jax.ShapeDtypeStruct((splits, rows // splits if scatter else rows, cols), dtype)
    copies = pairs + (pairs - 1) + (splits - 1) * (2 if scatter else 1)
    scratch = [
        pltpu.VMEM((pairs, rows, cols), dtype),
        pltpu.VMEM((pairs - 1, rows, cols), dtype),
        pltpu.VMEM((rows, cols), dtype),
        pltpu.VMEM((splits - 1, out.shape[1] if scatter else 16, cols), dtype),
        pltpu.SemaphoreType.DMA((2, copies)),
    ]
    return out, scratch


def greet(peers):
    barrier = pltpu.get_barrier_semaphore()
    for device in peers:
        pl.semaphore_signal(barrier, inc=1, device_id=device, device_id_type=pl.DeviceIdType.MESH)
    pl.semaphore_wait(barrier, len(peers))


def others(axis):
    size, me = lax.axis_size(axis), lax.axis_index(axis)
    return [{axis: lax.rem(me + step, size)} for step in range(1, size)]


class SmallSummer:
    def __init__(self, ref, land, sems):
        self.ref, self.land, self.sems = ref, land, sems
        self.dp, self.seq = lax.axis_index("dp"), lax.axis_index("seq")
        self.pairs, self.splits = lax.axis_size("dp") // 2, lax.axis_size("seq")
        self.slot, self.copies, self.sent = 0, [], []

    def send(self, devices):
        self.copies = []
        for device in devices:
            copy = pltpu.make_async_remote_copy(
                src_ref=self.ref.at[len(self.sent)], dst_ref=self.land.at[self.slot],
                send_sem=self.sems.at[0, self.slot], recv_sem=self.sems.at[1, self.slot],
                device_id=device, device_id_type=pl.DeviceIdType.MESH,
            )
            copy.start()
            self.copies.append((self.slot, copy))
            self.slot += 1
        self.sent.append(self.copies)

    def take(self):
        stage = len(self.sent) - 1
        total = self.ref[stage]
        for slot, copy in self.copies:
            copy.wait_recv()
            total = total + self.land[slot]
        self.ref[stage + 1] = total

    def pair(self):
        self.send([{"dp": self.dp + 1 - 2 * lax.rem(self.dp, 2)}])

    def plane(self):
        core, chip = lax.rem(self.dp, 2), self.dp // 2
        self.send([{"dp": 2 * lax.rem(chip + step, self.pairs) + core} for step in range(1, self.pairs)])

    def along(self):
        self.send([{"seq": lax.rem(self.seq + step, self.splits)} for step in range(1, self.splits)])

    def finish(self):
        for copies in self.sent:
            for _, copy in copies:
                copy.wait_send()


def norm_stats(values):
    average = jnp.mean(values, axis=-1, keepdims=True)
    centred = values - average
    scale = lax.rsqrt(jnp.mean(centred * centred, axis=-1, keepdims=True) + 1e-05)
    return centred * scale, scale


def norm_back(grad, normal, scale):
    return scale * (
        grad - jnp.mean(grad, axis=-1, keepdims=True) - normal * jnp.mean(grad * normal, axis=-1, keepdims=True)
    )


def flip(values):
    return values.astype(F32).T.astype(BF16)


def phase_spans(back, per_chunk, tiles):
    spans = []
    for chunk in range(back + 1):
        jobs = [
            (kt, b, chunk * per_chunk + kt - b)
            for kt in range(per_chunk)
            for b in range(per_chunk)
            if 0 <= chunk * per_chunk + kt - b < tiles
        ]
        first, last = min(j[2] for j in jobs), max(j[2] for j in jobs)
        spans.append((chunk, first, last - first + 1, jobs))
    return spans


class Gather:
    def __init__(self, shard, full, sems, own_sem):
        self.shard, self.full, self.sems = shard, full, sems
        self.rows = shard.shape[0]
        self.dp = lax.axis_index("dp")
        self.pairs = lax.axis_size("dp") // 2
        self.core, self.chip = lax.rem(self.dp, 2), self.dp // 2
        self.sibling = {"dp": self.dp + 1 - 2 * self.core}
        self.own = pltpu.make_async_copy(shard, self.place(self.dp), own_sem)

    def place(self, owner):
        return self.full.at[pl.ds(pl.multiple_of(owner * self.rows, self.rows), self.rows)]

    def copy(self, src, owner, slot, device):
        return pltpu.make_async_remote_copy(
            src_ref=src, dst_ref=self.place(owner), send_sem=self.sems.at[0, slot], recv_sem=self.sems.at[1, slot],
            device_id=device, device_id_type=pl.DeviceIdType.MESH,
        )

    def start(self):
        self.sent = [
            self.copy(self.shard, self.dp, step, {"dp": 2 * lax.rem(self.chip + step, self.pairs) + self.core})
            for step in range(1, self.pairs)
        ]
        self.near = self.copy(self.shard, self.dp, 0, self.sibling)
        for copy in self.sent + [self.near]:
            copy.start()
        self.own.start()

    def relay(self):
        self.relayed = []
        for step in range(1, self.pairs):
            self.sent[step - 1].wait_recv()
            owner = 2 * lax.rem(self.chip + self.pairs - step, self.pairs) + self.core
            self.relayed.append(self.copy(self.place(owner), owner, self.pairs - 1 + step, self.sibling))
            self.relayed[-1].start()

    def arrive(self):
        self.own.wait()
        for copy in [self.near] + self.relayed:
            copy.wait_recv()

    def finish(self):
        for copy in self.sent + [self.near] + self.relayed:
            copy.wait_send()


def layer_kernel(back, maxlen, *refs):
    (
        tokens_ref, cotangent_ref, deal_ref, lengths_ref, buckets_ref, *vector_refs, rel_ref,
        wqkv_s, wout_s, wup_s, wdown_s,
    ) = refs[:14]
    sum_down, sum_up, sum_out, sum_qkv, small_out, ret_out, ret_grad = refs[14:21]
    it = iter(refs[21:])
    sources = [next(it) for _ in range(4)]
    summers = [
        Summer(source, *[next(it) for _ in range(4)], out, next(it))
        for source, out in zip(sources, (sum_down, sum_up, sum_out, sum_qkv))
    ]
    down, up, out_sum, qkv_sum = summers
    small_ref, small_land, small_sems = next(it), next(it), next(it)
    slots, ret_sems, halo_send, halo_land, halo_sems = (next(it) for _ in range(5))
    dres_ref, do_ref, qaug, doaug, q_t, do_t = (next(it) for _ in range(6))
    bias, dsum, dd, dq_acc, dkt, dvt, dkv, gkv = (next(it) for _ in range(8))
    xwin, g_ref, wqkv_ref, wout_ref, wup_ref, wdown_ref = (next(it) for _ in range(6))
    gather_sems, own_sems, deal_sems, row_sems, few_land, few_sems = (next(it) for _ in range(6))
    gains_ref, base_ref, q_ref, k_ref, v_ref, att_ref, lse_ref = (next(it) for _ in range(7))
    few_mine, rel_all, hot_ref, qx_ref, kx_ref = (next(it) for _ in range(5))
    dp, groups = lax.axis_index("dp"), lax.axis_size("dp")
    seq, splits = lax.axis_index("seq"), lax.axis_size("seq")
    tokens, width = tokens_ref.shape
    length = tokens // groups
    per_chunk = tokens // QB
    tiles = base_ref.shape[-1] // QB - 1
    spans = phase_spans(back, per_chunk, tiles)
    mesh_ids = pl.DeviceIdType.MESH
    greet(others("dp") + others("seq"))

    def deal_out(which, source, target, first_row):
        for j in range(groups):
            piece = source[:length, :]
            for k in range(1, groups):
                piece = jnp.where(deal_ref[0, k] == j, source[k * length : (k + 1) * length, :], piece)
            slots[which, j] = piece
        copies = []
        rows_here = pl.ds(pl.multiple_of(first_row + dp * length, length), length)
        for step in range(1, groups):
            peer = lax.rem(dp + step, groups)
            copy = pltpu.make_async_remote_copy(
                src_ref=slots.at[which, peer], dst_ref=target.at[rows_here],
                send_sem=deal_sems.at[0, which, step - 1], recv_sem=deal_sems.at[1, which, step - 1],
                device_id={"dp": peer}, device_id_type=mesh_ids,
            )
            copy.start()
            copies.append(copy)
        target[rows_here, :] = slots[which, dp]
        return copies

    own_first = back * tokens
    own_rows = pl.ds(own_first, tokens)
    dealt = deal_out(0, tokens_ref, xwin, own_first)
    shard_rows, rel_rows = vector_refs[0].shape[0], rel_ref.shape[0]
    few_mine[...] = jnp.zeros_like(few_mine)
    for i, vector in enumerate(vector_refs):
        few_mine[i : i + 1, :shard_rows] = vector[...].astype(F32).reshape(1, shard_rows)
    few_mine[8 : 8 + rel_rows, :H] = rel_ref[...].astype(F32)
    few = []
    for step in range(1, groups):
        copy = pltpu.make_async_remote_copy(
            src_ref=few_mine, dst_ref=few_land.at[dp],
            send_sem=few_sems.at[0, step - 1], recv_sem=few_sems.at[1, step - 1],
            device_id={"dp": lax.rem(dp + step, groups)}, device_id_type=mesh_ids,
        )
        copy.start()
        few.append(copy)
    few_land[dp] = few_mine[...]
    gathers = [
        Gather(shard, full, gather_sems.at[i], own_sems.at[i])
        for i, (shard, full) in enumerate(
            ((wqkv_s, wqkv_ref), (wout_s, wout_ref), (wup_s, wup_ref), (wdown_s, wdown_ref))
        )
    ]
    gathers[0].start()

    seqs = lengths_ref.shape[1]

    def segments(rows, first_pos):
        place = lax.broadcasted_iota(jnp.int32, (rows, PAIR), 0) + first_pos
        found, end = jnp.zeros((rows, PAIR), jnp.int32), 0
        for c in range(seqs):
            end = end + lengths_ref[0, c]
            found = found + (place >= end).astype(jnp.int32)
        return jnp.where(place < 0, seqs, found)

    window = kx_ref.shape[0]
    lane_w = lax.rem(lax.broadcasted_iota(jnp.int32, (window, PAIR), 1), HD)
    key_seg = segments(window, (seq - back) * tokens)
    kx_ref[...] = jnp.where((lane_w == key_seg) | (lane_w >= HD - 3), 1.0, 0.0).astype(BF16)
    lane_q = lane_w[:tokens]
    qx_ref[...] = jnp.where((lane_q <= seqs) & (lane_q != segments(tokens, seq * tokens)), BIG, 0.0).astype(BF16)

    level = lax.broadcasted_iota(jnp.int32, (NBK, PAIR), 0)
    below, up_to = jnp.zeros((NBK, PAIR), F32), jnp.zeros((NBK, PAIR), F32)
    for r in range(buckets_ref.shape[0]):
        row = buckets_ref[r : r + 1, :]
        below = below + (row < level).astype(F32)
        up_to = up_to + (row <= level).astype(F32)
    below = jnp.sum(below, axis=1, keepdims=True)
    up_to = jnp.sum(up_to, axis=1, keepdims=True)
    far = (back * tokens + QB - lax.broadcasted_iota(jnp.int32, hot_ref.shape, 1)).astype(F32)
    hot_ref[...] = jnp.where((far >= below) & (far < up_to), 1.0, 0.0).astype(BF16)
    for copy in dealt:
        copy.wait_recv()

    def row_copy(step):
        return pltpu.make_async_remote_copy(
            src_ref=xwin.at[pl.ds((back - step + 1) * tokens, tokens)],
            dst_ref=xwin.at[pl.ds((back - step) * tokens, tokens)],
            send_sem=row_sems.at[0, step - 1], recv_sem=row_sems.at[1, step - 1],
            device_id={"seq": lax.rem(seq + 1, splits)}, device_id_type=mesh_ids,
        )

    def row_send(step):
        @pl.when((seq + 1 < splits) & (seq + 1 >= step))
        def _():
            row_copy(step).start()

    def row_wait(step):
        @pl.when(seq >= step)
        def _():
            row_copy(step).wait_recv()

    row_send(1)
    for copy in few:
        copy.wait_recv()
    per_tile = PAIR // shard_rows
    for i in range(width // PAIR):
        tile = few_land[i * per_tile, :8, :]
        for o in range(1, per_tile):
            tile = tile + pltpu.roll(few_land[i * per_tile + o, :8, :], o * shard_rows, 1)
        gains_ref[:, i * PAIR : (i + 1) * PAIR] = tile
    for o in range(groups):
        rel_all[o * rel_rows : (o + 1) * rel_rows, :] = few_land[o, 8 : 8 + rel_rows, :]
    table = dot_nn(flip(rel_all[...])[:H], hot_ref[...])
    far = back * tokens + QB - lax.broadcasted_iota(jnp.int32, table.shape, 1)
    base_ref[...] = jnp.where((far >= 0) & (far < maxlen), table, BIG).reshape(base_ref.shape)

    def first_norm(chunk):
        normal, _ = norm_stats(xwin[chunk * tokens : (chunk + 1) * tokens, :].astype(F32))
        return (normal * gains_ref[0:1, :] + gains_ref[1:2, :]).astype(BF16)

    own_normed = first_norm(back)
    gathers[0].relay()
    gathers[1].start()
    gathers[2].start()
    gathers[0].arrive()
    q_ref[...] = (dot_nn(own_normed, wqkv_ref[:, :width])).astype(BF16) * jnp.asarray(HD**-0.5, BF16)
    k_ref[own_rows, :] = dot_nn(own_normed, wqkv_ref[:, width : 2 * width]).astype(BF16)
    v_ref[own_rows, :] = dot_nn(own_normed, wqkv_ref[:, 2 * width :]).astype(BF16)

    low_tile = lax.broadcasted_iota(jnp.int32, (QB, PAIR), 1) < HD

    def look(chunk, first, count, jobs):
        span = count * QB
        keys = pl.ds(chunk * tokens, tokens)
        started, last = chunk < back, chunk == 0

        def body(pair, _):
            cols = pl.ds(pl.multiple_of(pair * PAIR, PAIR), PAIR)
            k_pair, v_pair, kx = k_ref[keys, cols], v_ref[keys, cols], kx_ref[keys, :]
            low_k = lax.broadcasted_iota(jnp.int32, (tokens, PAIR), 1) < HD
            for h in range(2):
                mine_k = low_k if h == 0 else jnp.logical_not(low_k)
                mine = low_tile if h == 0 else jnp.logical_not(low_tile)
                bias[:, :span] = toeplitz(base_ref[pair, h : h + 1, first * QB : (first + count + 1) * QB])
                k_aug = jnp.where(mine_k, k_pair, kx)
                v_aug = jnp.where(mine_k, v_pair, jnp.ones_like(v_pair))
                held = pl.ds(pl.multiple_of((2 * pair + h) * PAIR, PAIR), PAIR)
                for b in range(per_chunk):
                    here = pl.ds(b * QB, QB)
                    work = [(kt, j - first) for kt, block, j in jobs if block == b]
                    q_aug = jnp.where(mine, q_ref[here, cols], qx_ref[here, :])
                    top = None
                    for kt, j in work:
                        over = pl.ds(j * QB, QB)
                        score = dot_nt(q_aug, k_aug[kt * QB : (kt + 1) * QB]) + bias[:, over]
                        dsum[:, over] = score
                        most = jnp.maximum(score[:, :128], score[:, 128:])
                        top = most if top is None else jnp.maximum(top, most)
                    top = jnp.max(top, axis=1, keepdims=True)
                    acc = None
                    if started:
                        lane_at = HD if h == 0 else 0
                        before = lse_ref[here, cols][:, lane_at : lane_at + 1]
                        top = jnp.maximum(top, before)
                        acc = gkv[here, held] * jnp.exp(before - top)
                    for kt, j in work:
                        p = jnp.exp(dsum[:, pl.ds(j * QB, QB)] - top).astype(BF16)
                        more = dot_nn(p, v_aug[kt * QB : (kt + 1) * QB])
                        acc = more if acc is None else acc + more
                    if last:
                        value = (acc / pltpu.roll(acc, HD, 1)).astype(BF16)
                        att_ref[here, cols] = value if h == 0 else jnp.where(mine, value, att_ref[here, cols])
                        stat = top + jnp.log(acc)
                    else:
                        gkv[here, held] = acc
                        stat = jnp.broadcast_to(top, (QB, PAIR))
                    lse_ref[here, cols] = jnp.where(mine, lse_ref[here, cols], stat)
            return _

        lax.fori_loop(0, H // 2, body, 0)

    for chunk, first, count, jobs in reversed(spans):
        step = back - chunk
        if step > 0:
            row_wait(step)
            if step < back:
                row_send(step + 1)
            normed = jnp.where(seq >= step, first_norm(chunk).astype(F32), 0.0).astype(BF16)
            here = pl.ds(chunk * tokens, tokens)
            k_ref[here, :] = dot_nn(normed, wqkv_ref[:, width : 2 * width]).astype(BF16)
            v_ref[here, :] = dot_nn(normed, wqkv_ref[:, 2 * width :]).astype(BF16)
        look(chunk, first, count, jobs)
        if step == 0:
            gathers[1].relay()
            dealt_grad = deal_out(1, cotangent_ref, g_ref, 0)
            gathers[3].start()
        if step == back - 1:
            gathers[2].relay()
    gathers[3].relay()
    for gather in gathers[1:]:
        gather.arrive()
    for copy in dealt_grad:
        copy.wait_recv()
    for copy in dealt + dealt_grad:
        copy.wait_send()

    returns = []

    def send_back(which, landed):
        landed[dp] = slots[which, dp]
        for step in range(1, groups):
            peer = lax.rem(dp + step, groups)
            copy = pltpu.make_async_remote_copy(
                src_ref=slots.at[which, peer], dst_ref=landed.at[dp],
                send_sem=ret_sems.at[0, which, step - 1], recv_sem=ret_sems.at[1, which, step - 1],
                device_id={"dp": peer}, device_id_type=mesh_ids,
            )
            copy.start()
            returns.append(copy)

    resid = xwin[own_rows, :].astype(F32) + dot_nn(att_ref[...], wout_ref[...])
    normal, scale = norm_stats(resid)
    gain_two = gains_ref[2:3, :]
    a2 = (normal * gain_two + gains_ref[3:4, :]).astype(BF16)
    a2_t = flip(a2)
    g = g_ref[...]
    y = resid
    da2 = jnp.zeros((tokens, width), F32)
    rows_up, rows_down = width // groups, wdown_ref.shape[0] // groups
    for c in range(wdown_ref.shape[0] // width):
        cols = pl.ds(c * width, width)
        upper = dot_nn(a2, wup_ref[:, cols])
        phi = 0.5 + 0.5 * lax.erf(upper * (0.5**0.5))
        act = (upper * phi).astype(BF16)
        y = y + dot_nn(act, wdown_ref[cols, :])
        slope = phi + upper * (jnp.exp(-0.5 * upper * upper) * 0.3989422804014327)
        dup = (dot_nt(g, wdown_ref[cols, :]) * slope).astype(BF16)
        da2 = da2 + dot_nt(dup, wup_ref[:, cols])
        grad_down = dot_nn(flip(act), g).astype(BF16)
        for o in range(width // rows_down):
            sources[0][c * (width // rows_down) + o] = grad_down[o * rows_down : (o + 1) * rows_down]
        grad_up = dot_nn(a2_t, dup).astype(BF16)
        for o in range(groups):
            sources[1][o, c * rows_up : (c + 1) * rows_up] = grad_up[o * rows_up : (o + 1) * rows_up]
    down.stage1()
    up.stage1()
    y = y.astype(BF16)
    for o in range(groups):
        slots[0, o] = y[o * length : (o + 1) * length]
    send_back(0, ret_out)
    small_ref[0, 2:3, :] = jnp.sum(da2 * normal, axis=0, keepdims=True)
    small_ref[0, 3:4, :] = jnp.sum(da2, axis=0, keepdims=True)
    dres = g.astype(F32) + norm_back(da2 * gain_two, normal, scale)
    dres_ref[...] = dres
    dbr = dres.astype(BF16)
    grad_out = dot_nn(flip(att_ref[...]), dbr).astype(BF16)
    rows_out = width // groups
    for o in range(groups):
        sources[2][o] = grad_out[o * rows_out : (o + 1) * rows_out]
    out_sum.stage1()
    do_ref[...] = dot_nt(dbr, wout_ref[...]).astype(BF16)
    q_t[...] = flip(q_ref[...])
    do_t[...] = flip(do_ref[...])

    lane = lax.broadcasted_iota(jnp.int32, (tokens, PAIR), 1)
    extra = lax.rem(lane, HD)
    low_half = lane < HD
    swap = (
        (lax.broadcasted_iota(jnp.int32, (PAIR, PAIR), 0) < HD)
        != (lax.broadcasted_iota(jnp.int32, (PAIR, PAIR), 1) < HD)
    ).astype(BF16)

    def prepare(pair, _):
        cols = pl.ds(pl.multiple_of(pair * PAIR, PAIR), PAIR)
        prod = do_ref[:, cols].astype(F32) * att_ref[:, cols].astype(F32)
        prod_hi = prod.astype(BF16)
        prod_lo = (prod - prod_hi.astype(F32)).astype(BF16)
        delta = -(dot_nn(prod_hi, swap) + dot_nn(prod_lo, swap))
        delta_hi = delta.astype(BF16).astype(F32)
        lse = -lse_ref[:, cols]
        lse_hi = lse.astype(BF16).astype(F32)
        lse_mid = (lse - lse_hi).astype(BF16).astype(F32)
        lse_lo = lse - lse_hi - lse_mid
        q_extra = jnp.where(
            extra == HD - 3,
            lse_hi,
            jnp.where(extra == HD - 2, lse_mid, jnp.where(extra == HD - 1, lse_lo, qx_ref[...].astype(F32))),
        ).astype(BF16)
        do_extra = jnp.where(extra == 0, delta_hi, jnp.where(extra == 1, delta - delta_hi, 0.0)).astype(BF16)
        qaug[2 * pair] = jnp.where(low_half, q_ref[:, cols], q_extra)
        qaug[2 * pair + 1] = jnp.where(low_half, q_extra, q_ref[:, cols])
        doaug[2 * pair] = jnp.where(low_half, do_ref[:, cols], do_extra)
        doaug[2 * pair + 1] = jnp.where(low_half, do_extra, do_ref[:, cols])
        return _

    lax.fori_loop(0, H // 2, prepare, 0)
    dd[...] = jnp.zeros_like(dd)
    dq_acc[...] = jnp.zeros_like(dq_acc)
    halo = []

    def attend(chunk, first, count, jobs):
        span = count * QB
        keys = pl.ds(chunk * tokens, tokens)
        fresh = set()

        def body(pair, _):
            cols = pl.ds(pl.multiple_of(pair * PAIR, PAIR), PAIR)
            k_pair, v_pair, kx = k_ref[keys, cols], v_ref[keys, cols], kx_ref[keys, :]
            for h in range(2):
                mine = low_half if h == 0 else jnp.logical_not(low_half)
                head = 2 * pair + h
                bias[:, :span] = toeplitz(base_ref[pair, h : h + 1, first * QB : (first + count + 1) * QB])
                k_aug = jnp.where(mine, k_pair, kx)
                v_aug = jnp.where(mine, v_pair, jnp.ones_like(v_pair))
                feat = pl.ds(pl.multiple_of(head * HD, HD), HD)
                spot = pl.ds(h * HD, HD)
                fresh.clear()
                dq = [None] * per_chunk
                for kt in range(per_chunk):
                    part = slice(kt * QB, (kt + 1) * QB)
                    dk_t = dv_t = None
                    for b in range(per_chunk):
                        if (kt, b, chunk * per_chunk + kt - b) not in jobs:
                            continue
                        j = chunk * per_chunk + kt - b - first
                        here = pl.ds(b * QB, QB)
                        over = pl.ds(j * QB, QB)
                        p = jnp.exp(dot_nt(qaug[head, here, :], k_aug[part]) + bias[:, over])
                        ds = p * dot_nt(doaug[head, here, :], v_aug[part])
                        ds_low = ds.astype(BF16)
                        more_v = dot_nn(do_t[feat, here], p.astype(BF16))
                        more_k = dot_nn(q_t[feat, here], ds_low)
                        more_q = dot_nn(ds_low, k_pair[part])
                        dv_t = more_v if dv_t is None else dv_t + more_v
                        dk_t = more_k if dk_t is None else dk_t + more_k
                        dq[b] = more_q if dq[b] is None else dq[b] + more_q
                        if j in fresh:
                            dsum[:, over] += ds
                        else:
                            fresh.add(j)
                            dsum[:, over] = ds
                    dkt[spot, part] = dk_t
                    dvt[spot, part] = dv_t
                for b in range(per_chunk):
                    if dq[b] is not None:
                        here = pl.ds(b * QB, QB)
                        dq_acc[here, cols] += jnp.where(mine[:QB], dq[b], 0.0)
                left = jnp.concatenate([jnp.zeros((QB, QB), F32), dsum[:, :span]], axis=1)
                half = QB // 2
                while half:
                    left = left[:half] + pltpu.roll(left[half:], span + QB - half, 1)
                    half //= 2
                dd[pair, h : h + 1, first * QB : (first + count + 1) * QB] += left
            dkv[:, cols] = dkt[...].T.astype(BF16)
            dkv[:, pl.ds(pl.multiple_of(width + pair * PAIR, PAIR), PAIR)] = dvt[...].T.astype(BF16)
            return _

        lax.fori_loop(0, H // 2, body, 0)

    def halo_copy(step):
        return pltpu.make_async_remote_copy(
            src_ref=halo_send.at[step - 1], dst_ref=halo_land.at[step - 1],
            send_sem=halo_sems.at[0, step - 1], recv_sem=halo_sems.at[1, step - 1],
            device_id={"seq": lax.rem(seq + splits - 1, splits)}, device_id_type=pl.DeviceIdType.MESH,
        )

    grad_normed = None
    for index, (chunk, first, count, jobs) in enumerate(spans):
        attend(chunk, first, count, jobs)
        step = back - chunk
        part = dot_nt(dkv[...], wqkv_ref[:, width:])
        rows_t = first_norm(chunk)
        if step > 0:
            rows_t = jnp.where(seq >= step, rows_t.astype(F32), 0.0)
        rows_t = flip(rows_t)
        if index == 0:
            gkv[...] = dot_nn(rows_t, dkv[...])
        else:
            gkv[...] += dot_nn(rows_t, dkv[...])
        if step == 0:
            dq_low = (dq_acc[...] * (HD**-0.5)).astype(BF16)
            grad_normed = part + dot_nt(dq_low, wqkv_ref[:, :width])
            grad_q = dot_nn(rows_t, dq_low).astype(BF16)
            for o in range(groups):
                take = slice(o * rows_up, (o + 1) * rows_up)
                sources[3][o, :rows_up] = grad_q[take]
                sources[3][o, rows_up : 2 * rows_up] = gkv[take, :width].astype(BF16)
                sources[3][o, 2 * rows_up :] = gkv[take, width:].astype(BF16)
            qkv_sum.stage1()
        else:
            if step < back:

                @pl.when((seq + 1 < splits) & (seq >= step))
                def _(step=step):
                    halo_copy(step + 1).wait_recv()

                arrived = jnp.where((seq + 1 < splits) & (seq >= step), halo_land[step].astype(F32), 0.0)
                part = part + arrived
            halo_send[step - 1] = part.astype(BF16)

            @pl.when(seq >= step)
            def _(step=step):
                halo_copy(step).start()

        if index == 0:
            down.stage2()
            up.stage2()
            out_sum.stage2()
        if index == back - 1 and back > 0:
            down.stage3()
    up.stage3()
    out_sum.stage3()
    qkv_sum.stage2()

    @pl.when(seq + 1 < splits)
    def _():
        halo_copy(1).wait_recv()

    grad_normed = grad_normed + jnp.where(seq + 1 < splits, halo_land[0].astype(F32), 0.0)
    normal, scale = norm_stats(xwin[own_rows, :].astype(F32))
    small_ref[0, 0:1, :] = jnp.sum(grad_normed * normal, axis=0, keepdims=True)
    small_ref[0, 1:2, :] = jnp.sum(grad_normed, axis=0, keepdims=True)
    small_ref[0, 4:8, :] = jnp.zeros((4, width), F32)
    dd_all = dd[...].reshape(H, dd.shape[-1])
    dd_hi = dd_all.astype(BF16)
    dd_mid = (dd_all - dd_hi.astype(F32)).astype(BF16)
    small_ref[0, 8:16, :] = jnp.zeros((8, width), F32)
    small_ref[0, 8:16, :NBK] = dot_nt(dd_hi, hot_ref[...]) + dot_nt(dd_mid, hot_ref[...])
    small = SmallSummer(small_ref, small_land, small_sems)
    small.pair()
    dx = (dres_ref[...] + norm_back(grad_normed * gains_ref[0:1, :], normal, scale)).astype(BF16)
    for o in range(groups):
        slots[1, o] = dx[o * length : (o + 1) * length]
    send_back(1, ret_grad)
    small.take()
    small.plane()
    down.stage4()
    up.stage4()
    qkv_sum.stage3()
    small.take()
    small.along()
    out_sum.stage4()
    qkv_sum.stage4()
    small.take()
    small_out[...] = small_ref[3]
    for summer in summers:
        summer.finish()
    small.finish()
    for copy in returns:
        copy.wait()
    for gather in gathers:
        gather.finish()
    for copy in few:
        copy.wait_send()
    for step in range(1, back + 1):

        @pl.when((seq + 1 < splits) & (seq + 1 >= step))
        def _(step=step):
            row_copy(step).wait_send()
    for step in range(1, back + 1):

        @pl.when(seq >= step)
        def _(step=step):
            halo_copy(step).wait_send()


def layer(back, tokens_in, cotangent, deal, lengths, buckets, vectors, rel, wqkv, wout, wup, wdown):
    splits, groups = lax.axis_size("seq"), lax.axis_size("dp")
    tokens, width = tokens_in.shape
    length = tokens // groups
    per_chunk = tokens // QB
    maxlen = buckets.shape[0]
    window, reach = (back + 1) * tokens, back * tokens + 2 * QB
    span = max(count for _, _, count, _ in phase_spans(back, per_chunk, reach // QB - 1)) * QB
    grads = [wdown.shape[0], wup.shape[0] * wup.shape[1] // width, width // groups, 3 * width // groups]
    out_shapes, more, sources = [], [], []
    for height in grads:
        shape = (groups, height, width)
        out, scratch = summer_shapes(shape, BF16, splits)
        sources.append(pltpu.VMEM(shape, BF16))
        out_shapes.append(out)
        more += scratch
    out_shapes.append(jax.ShapeDtypeStruct((16, width), F32))
    out_shapes += [jax.ShapeDtypeStruct((groups, length, width), BF16)] * 2
    small_copies = 1 + (groups // 2 - 1) + (splits - 1)
    scratch = sources + more + [
        pltpu.VMEM((4, 16, width), F32),
        pltpu.VMEM((small_copies, 16, width), F32),
        pltpu.SemaphoreType.DMA((2, small_copies)),
        pltpu.VMEM((2, groups, length, width), BF16),
        pltpu.SemaphoreType.DMA((2, 2, groups - 1)),
        pltpu.VMEM((back, tokens, width), BF16),
        pltpu.VMEM((back, tokens, width), BF16),
        pltpu.SemaphoreType.DMA((2, back)),
        pltpu.VMEM((tokens, width), F32),
        pltpu.VMEM((tokens, width), BF16),
        pltpu.VMEM((H, tokens, PAIR), BF16),
        pltpu.VMEM((H, tokens, PAIR), BF16),
        pltpu.VMEM((width, tokens), BF16),
        pltpu.VMEM((width, tokens), BF16),
        pltpu.VMEM((QB, span), F32),
        pltpu.VMEM((QB, span), F32),
        pltpu.VMEM((H // 2, 2, reach), F32),
        pltpu.VMEM((tokens, width), F32),
        pltpu.VMEM((PAIR, tokens), F32),
        pltpu.VMEM((PAIR, tokens), F32),
        pltpu.VMEM((tokens, 2 * width), BF16),
        pltpu.VMEM((width, 2 * width), F32),
        pltpu.VMEM((window, width), BF16),
        pltpu.VMEM((tokens, width), BF16),
        pltpu.VMEM((width, 3 * width), BF16),
        pltpu.VMEM((width, width), BF16),
        pltpu.VMEM((width, wup.shape[1]), BF16),
        pltpu.VMEM((wup.shape[1], width), BF16),
        pltpu.SemaphoreType.DMA((4, 2, groups - 1)),
        pltpu.SemaphoreType.DMA((4,)),
        pltpu.SemaphoreType.DMA((2, 2, groups - 1)),
        pltpu.SemaphoreType.DMA((2, back)),
        pltpu.VMEM((groups, 16, PAIR), F32),
        pltpu.SemaphoreType.DMA((2, groups - 1)),
        pltpu.VMEM((8, width), F32),
        pltpu.VMEM((H // 2, 2, reach), F32),
        pltpu.VMEM((tokens, width), BF16),
        pltpu.VMEM((window, width), BF16),
        pltpu.VMEM((window, width), BF16),
        pltpu.VMEM((tokens, width), BF16),
        pltpu.VMEM((tokens, width), F32),
        pltpu.VMEM((16, PAIR), F32),
        pltpu.VMEM((NBK, PAIR), F32),
        pltpu.VMEM((NBK, reach), BF16),
        pltpu.VMEM((tokens, PAIR), BF16),
        pltpu.VMEM((window, PAIR), BF16),
    ]
    vmem, smem = pl.BlockSpec(memory_space=pltpu.VMEM), pl.BlockSpec(memory_space=pltpu.SMEM)
    return pl.pallas_call(
        functools.partial(layer_kernel, back, maxlen),
        in_specs=[vmem] * 2 + [smem] * 2 + [vmem] * (2 + len(vectors)) + [pl.BlockSpec(memory_space=pl.ANY)] * 4,
        out_specs=[vmem] * len(out_shapes),
        out_shape=out_shapes,
        scratch_shapes=scratch,
        compiler_params=pltpu.CompilerParams(collective_id=1, has_side_effects=True, vmem_limit_bytes=VMEM_LIMIT),
        name="layer",
    )(tokens_in, cotangent, deal, lengths, buckets.reshape(-1, PAIR), *vectors, rel, wqkv, wout, wup, wdown)


def finish_kernel(deal_ref, down, up, out, qkv, small, ret_out, ret_grad, *outs):
    o_out, o_grad, o_qkv, o_wout, o_up, o_down, *o_vectors, o_rel = outs
    length = ret_out.shape[1]
    for g in range(ret_out.shape[0]):
        piece = deal_ref[0, g]
        o_out[pl.ds(g * length, length), :] = ret_out[piece]
        o_grad[pl.ds(g * length, length), :] = ret_grad[piece]
    for source, target in ((down, o_down), (up, o_up), (out, o_wout), (qkv, o_qkv)):
        direct = source.shape[0] * source.shape[1] * source.shape[2] != target.shape[0] * target.shape[1]
        cols = source.shape[2]
        if direct:
            value = add_low(*[source[t] for t in range(source.shape[0])])
        else:
            value = source[...].reshape(-1, cols).astype(F32)
        height = target.shape[0]
        for c in range(target.shape[1] // cols):
            target[:, c * cols : (c + 1) * cols] = value[c * height : (c + 1) * height]
    dp, groups = lax.axis_index("dp"), lax.axis_size("dp")
    for i, target in enumerate(o_vectors):
        size = target.shape[0]
        value = small[i : i + 1, :size]
        for o in range(1, groups):
            value = jnp.where(dp == o, small[i : i + 1, o * size : (o + 1) * size], value)
        target[...] = value.reshape(size)
    levels = small[8 : 8 + H, :PAIR].T
    size = o_rel.shape[0]
    value = levels[:size, :H]
    for o in range(1, groups):
        value = jnp.where(dp == o, levels[o * size : (o + 1) * size, :H], value)
    o_rel[...] = value


def finish(deal, sums, returned, shapes):
    return pl.pallas_call(
        finish_kernel,
        in_specs=[pl.BlockSpec(memory_space=pltpu.SMEM)] + [pl.BlockSpec(memory_space=pltpu.VMEM)] * 7,
        out_specs=[pl.BlockSpec(memory_space=pltpu.VMEM)] * len(shapes),
        out_shape=shapes,
        compiler_params=pltpu.CompilerParams(vmem_limit_bytes=VMEM_LIMIT),
        name="finish",
    )(deal, *sums, *returned)


def shards(
    tokens,
    cotangent,
    deal,
    lengths,
    buckets,
    ln1_gain,
    ln1_bias,
    w_qkv,
    w_out,
    rel_bias,
    ln2_gain,
    ln2_bias,
    w_up,
    w_down,
):
    tok_dev = tokens.shape[0]
    back = -(-buckets.shape[0] // tok_dev)
    *sums, small_total, back_out, back_grad = layer(
        back, tokens, cotangent, deal, lengths, buckets, (ln1_gain, ln1_bias, ln2_gain, ln2_bias), rel_bias,
        w_qkv, w_out, w_up, w_down,
    )
    output, grad_tokens, total_qkv, total_out, total_up, total_down, g_one, b_one, g_two, b_two, total_rel = finish(
        deal,
        [*sums, small_total],
        [back_out, back_grad],
        [jax.ShapeDtypeStruct(tokens.shape, BF16)] * 2
        + [
            jax.ShapeDtypeStruct(a.shape, F32)
            for a in (w_qkv, w_out, w_up, w_down, ln1_gain, ln1_bias, ln2_gain, ln2_bias, rel_bias)
        ],
    )
    return (
        output, grad_tokens, g_one, b_one, total_qkv, total_out, total_rel, g_two, b_two, total_up, total_down,
    )


def solution(mesh):
    by_all, by_dp = P(("seq", "dp"), None), P("dp", None)
    return jax.shard_map(
        shards,
        mesh=mesh,
        in_specs=(
            by_all, by_all, by_all, by_dp, P(), P("dp"), P("dp"), by_dp, by_dp, by_dp, P("dp"), P("dp"), by_dp, by_dp,
        ),
        out_specs=(by_all, by_all, P("dp"), P("dp"), by_dp, by_dp, by_dp, P("dp"), P("dp"), by_dp, by_dp),
        check_vma=False,
    )
```

```python
import functools

import jax
import jax.numpy as jnp
from jax import lax
from jax.experimental import pallas as pl
from jax.experimental.pallas import tpu as pltpu
from jax.sharding import PartitionSpec as P

H = 8
HD = 64
NBK = 32
QB = 256
PAIR = 2 * HD
BIG = -1e30
F32 = jnp.float32
BF16 = jnp.bfloat16
VMEM_LIMIT = 60 * 1024 * 1024

NT = (((1,), (1,)), ((), ()))
NN = (((1,), (0,)), ((), ()))


def dot_nt(a, b):
    return lax.dot_general(a, b, NT, preferred_element_type=F32)


def dot_nn(a, b):
    return lax.dot_general(a, b, NN, preferred_element_type=F32)


def toeplitz(row):
    width = row.shape[1]
    return pltpu.roll(jnp.broadcast_to(row, (QB, width)), 0, 1, stride=1, stride_axis=0)[:, QB:]


def add_low(first, *others):
    total = first.astype(F32)
    for other in others:
        total = total + other.astype(F32)
    return total


def square(chip):
    return chip + 1 - 2 * lax.rem(chip, 2), chip + 2 - 4 * (chip // 2), 3 - chip


class Summer:
    def __init__(self, source, pair, recv2, mine, recv3, out, sems):
        self.source, self.pair, self.recv2 = source, pair, recv2
        self.mine, self.recv3, self.out, self.sems = mine, recv3, out, sems
        self.dp, self.seq = lax.axis_index("dp"), lax.axis_index("seq")
        self.pairs, self.splits = source.shape[0] // 2, lax.axis_size("seq")
        self.core, self.chip = lax.rem(self.dp, 2), self.dp // 2
        self.rows = out.shape[1]
        self.scatter = self.rows < mine.shape[0]
        self.square = False
        self.hops2 = 6 if self.square else self.pairs - 1

    def copy(self, src, dst, slot, device):
        return pltpu.make_async_remote_copy(
            src_ref=src, dst_ref=dst, send_sem=self.sems.at[0, slot], recv_sem=self.sems.at[1, slot],
            device_id=device, device_id_type=pl.DeviceIdType.MESH,
        )

    def copy1(self, k):
        other = 1 - self.core
        return self.copy(self.source.at[2 * k + other], self.pair.at[k], k, {"dp": self.dp + 1 - 2 * self.core})

    def copy2(self, step):
        k = lax.rem(self.chip + 1 + step, self.pairs)
        return self.copy(self.pair.at[k], self.recv2.at[step], self.pairs + step, {"dp": 2 * k + self.core})

    def square2(self):
        across, along, far = square(self.chip)
        half = self.mine.shape[0] // 2
        copies = []
        for i, (one, two) in enumerate(((across, along), (along, across))):
            part = pl.ds(i * half, half)
            for j, owner in enumerate((one, far)):
                copies.append(
                    self.copy(
                        self.pair.at[owner, part], self.recv2.at[j, part], self.pairs + 2 * i + j,
                        {"dp": 2 * one + self.core},
                    )
                )
        late = []
        for i, two in enumerate((along, across)):
            part = pl.ds(i * half, half)
            late.append(
                self.copy(
                    self.pair.at[two, part], self.recv2.at[2, part], self.pairs + 4 + i, {"dp": 2 * two + self.core}
                )
            )
        return copies, late

    def copies2(self):
        if self.square:
            copies, late = self.square2()
            return copies + late
        return [self.copy2(step) for step in range(self.pairs - 1)]

    def copy3(self, step):
        t = lax.rem(self.seq + 1 + step, self.splits)
        src = self.mine.at[pl.ds(pl.multiple_of(t * self.rows, self.rows), self.rows)] if self.scatter else self.mine
        dst = self.recv3.at[step] if self.scatter else self.out.at[self.seq]
        return self.copy(src, dst, self.pairs + self.hops2 + step, {"seq": t})

    def copy4(self, step):
        t = lax.rem(self.seq + 1 + step, self.splits)
        slot = self.pairs + self.hops2 + self.splits - 1 + step
        return self.copy(self.out.at[self.seq], self.out.at[self.seq], slot, {"seq": t})

    def stage1(self, some=None):
        for k in range(self.pairs) if some is None else some:
            self.copy1(k).start()

    def stage2(self):
        for k in range(self.pairs):
            self.copy1(k).wait_recv()
        for step in range(self.pairs):
            k = lax.rem(self.chip + 1 + step, self.pairs)
            self.pair[k] = add_low(self.source[2 * k + self.core], self.pair[k]).astype(self.pair.dtype)
            if step < self.pairs - 1 and not self.square:
                self.copy2(step).start()
        if self.square:
            for copy in self.square2()[0]:
                copy.start()

    def stage2b(self):
        if not self.square:
            return
        across, along, _ = square(self.chip)
        copies, late = self.square2()
        half = self.mine.shape[0] // 2
        for copy in copies:
            copy.wait_recv()
        for i, two in enumerate((along, across)):
            part = pl.ds(i * half, half)
            self.pair[two, part] = add_low(self.pair[two, part], self.recv2[1, part]).astype(self.pair.dtype)
            late[i].start()

    def stage3(self):
        if self.square:
            for copy in self.square2()[1]:
                copy.wait_recv()
            total = add_low(self.pair[self.chip], self.recv2[0], self.recv2[2])
        else:
            for step in range(self.pairs - 1):
                self.copy2(step).wait_recv()
            total = add_low(self.pair[self.chip], *[self.recv2[step] for step in range(self.pairs - 1)])
        self.mine[...] = total.astype(self.mine.dtype)
        for step in range(self.splits - 1):
            self.copy3(step).start()
        if not self.scatter:
            self.out[self.seq] = self.mine[...]

    def stage4(self):
        for step in range(self.splits - 1):
            self.copy3(step).wait_recv()
        if not self.scatter:
            return
        own = self.mine[pl.ds(pl.multiple_of(self.seq * self.rows, self.rows), self.rows)]
        total = add_low(own, *[self.recv3[step] for step in range(self.splits - 1)])
        self.out[self.seq] = total.astype(self.out.dtype)
        for step in range(self.splits - 1):
            self.copy4(step).start()

    def finish(self):
        for k in range(self.pairs):
            self.copy1(k).wait_send()
        for copy in self.copies2():
            copy.wait_send()
        for step in range(self.splits - 1):
            self.copy3(step).wait_send()
        if self.scatter:
            for step in range(self.splits - 1):
                self.copy4(step).wait()


def summer_shapes(shape, dtype, splits):
    groups, rows, cols = shape
    pairs = groups // 2
    scatter = rows % (16 * splits) == 0
    out = jax.ShapeDtypeStruct((splits, rows // splits if scatter else rows, cols), dtype)
    copies = pairs + (6 if pairs == 4 else pairs - 1) + (splits - 1) * (2 if scatter else 1)
    scratch = [
        pltpu.VMEM((pairs, rows, cols), dtype),
        pltpu.VMEM((pairs - 1, rows, cols), dtype),
        pltpu.VMEM((rows, cols), dtype),
        pltpu.VMEM((splits - 1, out.shape[1] if scatter else 16, cols), dtype),
        pltpu.SemaphoreType.DMA((2, copies)),
    ]
    return out, scratch


def greet(peers):
    barrier = pltpu.get_barrier_semaphore()
    for device in peers:
        pl.semaphore_signal(barrier, inc=1, device_id=device, device_id_type=pl.DeviceIdType.MESH)
    pl.semaphore_wait(barrier, len(peers))


def others(axis):
    size, me = lax.axis_size(axis), lax.axis_index(axis)
    return [{axis: lax.rem(me + step, size)} for step in range(1, size)]


class SmallSummer:
    def __init__(self, ref, land, sems):
        self.ref, self.land, self.sems = ref, land, sems
        self.dp, self.seq = lax.axis_index("dp"), lax.axis_index("seq")
        self.pairs, self.splits = lax.axis_size("dp") // 2, lax.axis_size("seq")
        self.slot, self.copies, self.sent = 0, [], []

    def send(self, devices):
        self.copies = []
        for device in devices:
            copy = pltpu.make_async_remote_copy(
                src_ref=self.ref.at[len(self.sent)], dst_ref=self.land.at[self.slot],
                send_sem=self.sems.at[0, self.slot], recv_sem=self.sems.at[1, self.slot],
                device_id=device, device_id_type=pl.DeviceIdType.MESH,
            )
            copy.start()
            self.copies.append((self.slot, copy))
            self.slot += 1
        self.sent.append(self.copies)

    def take(self):
        stage = len(self.sent) - 1
        total = self.ref[stage]
        for slot, copy in self.copies:
            copy.wait_recv()
            total = total + self.land[slot]
        self.ref[stage + 1] = total

    def pair(self):
        self.send([{"dp": self.dp + 1 - 2 * lax.rem(self.dp, 2)}])

    def plane(self):
        core, chip = lax.rem(self.dp, 2), self.dp // 2
        self.send([{"dp": 2 * lax.rem(chip + step, self.pairs) + core} for step in range(1, self.pairs)])

    def along(self):
        self.send([{"seq": lax.rem(self.seq + step, self.splits)} for step in range(1, self.splits)])

    def finish(self):
        for copies in self.sent:
            for _, copy in copies:
                copy.wait_send()


def norm_stats(values):
    average = jnp.mean(values, axis=-1, keepdims=True)
    centred = values - average
    scale = lax.rsqrt(jnp.mean(centred * centred, axis=-1, keepdims=True) + 1e-05)
    return centred * scale, scale


def norm_back(grad, normal, scale):
    return scale * (
        grad - jnp.mean(grad, axis=-1, keepdims=True) - normal * jnp.mean(grad * normal, axis=-1, keepdims=True)
    )


def flip(values):
    return values.astype(F32).T.astype(BF16)


def phase_spans(back, per_chunk, tiles):
    spans = []
    for chunk in range(back + 1):
        jobs = [
            (kt, b, chunk * per_chunk + kt - b)
            for kt in range(per_chunk)
            for b in range(per_chunk)
            if 0 <= chunk * per_chunk + kt - b < tiles
        ]
        first, last = min(j[2] for j in jobs), max(j[2] for j in jobs)
        spans.append((chunk, first, last - first + 1, jobs))
    return spans


class Gather:
    def __init__(self, shard, full, sems, own_sem):
        self.shard, self.full, self.sems = shard, full, sems
        self.rows = shard.shape[0]
        self.dp = lax.axis_index("dp")
        self.pairs = lax.axis_size("dp") // 2
        self.square = self.pairs == 4
        self.core, self.chip = lax.rem(self.dp, 2), self.dp // 2
        self.sibling = {"dp": self.dp + 1 - 2 * self.core}
        self.own = pltpu.make_async_copy(shard, self.place(self.dp), own_sem)
        if self.square:
            self.around = square(self.chip)
        else:
            self.around = [lax.rem(self.chip + step, self.pairs) for step in range(1, self.pairs)]
            self.behind = [lax.rem(self.chip + self.pairs - step, self.pairs) for step in range(1, self.pairs)]

    def place(self, owner, first=0, rows=None):
        start = pl.multiple_of(owner * self.rows, self.rows)
        return self.full.at[pl.ds(start + first, self.rows if rows is None else rows)]

    def copy(self, src, dst, slot, device):
        return pltpu.make_async_remote_copy(
            src_ref=src, dst_ref=dst, send_sem=self.sems.at[0, slot], recv_sem=self.sems.at[1, slot],
            device_id=device, device_id_type=pl.DeviceIdType.MESH,
        )

    def mate(self, chip):
        return {"dp": 2 * chip + self.core}

    def start(self):
        reach = self.around[:2] if self.square else self.around
        self.sent = [self.copy(self.shard, self.place(self.dp), 1 + i, self.mate(c)) for i, c in enumerate(reach)]
        self.near = self.copy(self.shard, self.place(self.dp), 0, self.sibling)
        for copy in self.sent + [self.near]:
            copy.start()
        self.own.start()
        self.waiting = [self.near]

    def share(self, chip, slot):
        there = self.place(2 * chip + self.core)
        copy = self.copy(there, there, slot, self.sibling)
        copy.start()
        self.waiting.append(copy)
        self.sent.append(copy)

    def relay(self):
        for copy in self.sent:
            copy.wait_recv()
        if not self.square:
            for i, chip in enumerate(self.behind):
                self.share(chip, self.pairs + i)
            return
        across, along, _ = self.around
        half = self.rows // 2
        self.passed = []
        for i, (origin, target) in enumerate(((across, along), (along, across))):
            there = self.place(2 * origin + self.core, i * half, half)
            copy = self.copy(there, there, 3 + i, self.mate(target))
            copy.start()
            self.passed.append(copy)
        self.share(across, 5)
        self.share(along, 6)

    def relay_far(self):
        if not self.square:
            return
        for copy in self.passed:
            copy.wait_recv()
        self.share(self.around[2], 7)
        self.sent += self.passed

    def arrive(self):
        self.own.wait()
        for copy in self.waiting:
            copy.wait_recv()

    def finish(self):
        for copy in self.sent + [self.near]:
            copy.wait_send()


def layer_kernel(back, maxlen, *refs):
    (
        tokens_ref, cotangent_ref, deal_ref, lengths_ref, buckets_ref, *vector_refs, rel_ref,
        wqkv_s, wout_s, wup_s, wdown_s,
    ) = refs[:14]
    sum_down, sum_up, sum_out, sum_qkv, small_out, ret_out, ret_grad = refs[14:21]
    it = iter(refs[21:])
    sources = [next(it) for _ in range(4)]
    summers = [
        Summer(source, *[next(it) for _ in range(4)], out, next(it))
        for source, out in zip(sources, (sum_down, sum_up, sum_out, sum_qkv))
    ]
    down, up, out_sum, qkv_sum = summers
    small_ref, small_land, small_sems = next(it), next(it), next(it)
    slots, ret_sems, halo_send, halo_land, halo_sems = (next(it) for _ in range(5))
    dres_ref, do_ref, qaug, doaug, q_t, do_t = (next(it) for _ in range(6))
    bias, scores, kaug, vaug, dd, dq_acc, dkt, dvt, dkv, gkv = (next(it) for _ in range(10))
    dsum = scores.at[0]
    xwin, g_ref, wqkv_ref, wout_ref, wup_ref, wdown_ref = (next(it) for _ in range(6))
    gather_sems, own_sems, deal_sems, row_sems, few_land, few_sems = (next(it) for _ in range(6))
    gains_ref, base_ref, q_ref, k_ref, v_ref, att_ref, lse_ref = (next(it) for _ in range(7))
    few_mine, rel_all, hot_ref, qx_ref, kx_ref = (next(it) for _ in range(5))
    dp, groups = lax.axis_index("dp"), lax.axis_size("dp")
    seq, splits = lax.axis_index("seq"), lax.axis_size("seq")
    tokens, width = tokens_ref.shape
    length = tokens // groups
    per_chunk = tokens // QB
    tiles = base_ref.shape[-1] // QB - 1
    spans = phase_spans(back, per_chunk, tiles)
    mesh_ids = pl.DeviceIdType.MESH
    greet(others("dp") + others("seq"))

    def deal_out(which, source, target, first_row):
        for j in range(groups):
            piece = source[:length, :]
            for k in range(1, groups):
                piece = jnp.where(deal_ref[0, k] == j, source[k * length : (k + 1) * length, :], piece)
            slots[which, j] = piece
        copies = []
        rows_here = pl.ds(pl.multiple_of(first_row + dp * length, length), length)
        for step in range(1, groups):
            peer = lax.rem(dp + step, groups)
            copy = pltpu.make_async_remote_copy(
                src_ref=slots.at[which, peer], dst_ref=target.at[rows_here],
                send_sem=deal_sems.at[0, which, step - 1], recv_sem=deal_sems.at[1, which, step - 1],
                device_id={"dp": peer}, device_id_type=mesh_ids,
            )
            copy.start()
            copies.append(copy)
        target[rows_here, :] = slots[which, dp]
        return copies

    own_first = back * tokens
    own_rows = pl.ds(own_first, tokens)
    dealt = deal_out(0, tokens_ref, xwin, own_first)
    shard_rows, rel_rows = vector_refs[0].shape[0], rel_ref.shape[0]
    few_mine[...] = jnp.zeros_like(few_mine)
    for i, vector in enumerate(vector_refs):
        few_mine[i : i + 1, :shard_rows] = vector[...].astype(F32).reshape(1, shard_rows)
    few_mine[8 : 8 + rel_rows, :H] = rel_ref[...].astype(F32)
    few = []
    for step in range(1, groups):
        copy = pltpu.make_async_remote_copy(
            src_ref=few_mine, dst_ref=few_land.at[dp],
            send_sem=few_sems.at[0, step - 1], recv_sem=few_sems.at[1, step - 1],
            device_id={"dp": lax.rem(dp + step, groups)}, device_id_type=mesh_ids,
        )
        copy.start()
        few.append(copy)
    few_land[dp] = few_mine[...]
    gathers = [
        Gather(shard, full, gather_sems.at[i], own_sems.at[i])
        for i, (shard, full) in enumerate(
            ((wqkv_s, wqkv_ref), (wout_s, wout_ref), (wup_s, wup_ref), (wdown_s, wdown_ref))
        )
    ]
    gathers[0].start()
    gathers[1].start()

    seqs = lengths_ref.shape[1]

    def segments(rows, first_pos):
        place = lax.broadcasted_iota(jnp.int32, (rows, PAIR), 0) + first_pos
        found, end = jnp.zeros((rows, PAIR), jnp.int32), 0
        for c in range(seqs):
            end = end + lengths_ref[0, c]
            found = found + (place >= end).astype(jnp.int32)
        return jnp.where(place < 0, seqs, found)

    window = kx_ref.shape[0]
    lane_w = lax.rem(lax.broadcasted_iota(jnp.int32, (window, PAIR), 1), HD)
    key_seg = segments(window, (seq - back) * tokens)
    kx_ref[...] = jnp.where((lane_w == key_seg) | (lane_w >= HD - 3), 1.0, 0.0).astype(BF16)
    lane_q = lane_w[:tokens]
    qx_ref[...] = jnp.where((lane_q <= seqs) & (lane_q != segments(tokens, seq * tokens)), BIG, 0.0).astype(BF16)

    level = lax.broadcasted_iota(jnp.int32, (NBK, PAIR), 0)
    below, up_to = jnp.zeros((NBK, PAIR), F32), jnp.zeros((NBK, PAIR), F32)
    for r in range(buckets_ref.shape[0]):
        row = buckets_ref[r : r + 1, :]
        below = below + (row < level).astype(F32)
        up_to = up_to + (row <= level).astype(F32)
    below = jnp.sum(below, axis=1, keepdims=True)
    up_to = jnp.sum(up_to, axis=1, keepdims=True)
    far = (back * tokens + QB - lax.broadcasted_iota(jnp.int32, hot_ref.shape, 1)).astype(F32)
    hot_ref[...] = jnp.where((far >= below) & (far < up_to), 1.0, 0.0).astype(BF16)
    for copy in dealt:
        copy.wait_recv()

    def row_copy(step):
        return pltpu.make_async_remote_copy(
            src_ref=xwin.at[pl.ds((back - step + 1) * tokens, tokens)],
            dst_ref=xwin.at[pl.ds((back - step) * tokens, tokens)],
            send_sem=row_sems.at[0, step - 1], recv_sem=row_sems.at[1, step - 1],
            device_id={"seq": lax.rem(seq + 1, splits)}, device_id_type=mesh_ids,
        )

    def row_send(step):
        @pl.when((seq + 1 < splits) & (seq + 1 >= step))
        def _():
            row_copy(step).start()

    def row_wait(step):
        @pl.when(seq >= step)
        def _():
            row_copy(step).wait_recv()

    row_send(1)
    for copy in few:
        copy.wait_recv()
    per_tile = PAIR // shard_rows
    for i in range(width // PAIR):
        tile = few_land[i * per_tile, :8, :]
        for o in range(1, per_tile):
            tile = tile + pltpu.roll(few_land[i * per_tile + o, :8, :], o * shard_rows, 1)
        gains_ref[:, i * PAIR : (i + 1) * PAIR] = tile
    for o in range(groups):
        rel_all[o * rel_rows : (o + 1) * rel_rows, :] = few_land[o, 8 : 8 + rel_rows, :]
    table = dot_nn(flip(rel_all[...])[:H], hot_ref[...])
    far = back * tokens + QB - lax.broadcasted_iota(jnp.int32, table.shape, 1)
    base_ref[...] = jnp.where((far >= 0) & (far < maxlen), table, BIG).reshape(base_ref.shape)

    def first_norm(chunk):
        normal, _ = norm_stats(xwin[chunk * tokens : (chunk + 1) * tokens, :].astype(F32))
        return (normal * gains_ref[0:1, :] + gains_ref[1:2, :]).astype(BF16)

    own_normed = first_norm(back)
    gathers[0].relay()
    gathers[2].start()
    gathers[0].relay_far()
    gathers[0].arrive()
    q_ref[...] = (dot_nn(own_normed, wqkv_ref[:, :width])).astype(BF16) * jnp.asarray(HD**-0.5, BF16)
    k_ref[own_rows, :] = dot_nn(own_normed, wqkv_ref[:, width : 2 * width]).astype(BF16)
    v_ref[own_rows, :] = dot_nn(own_normed, wqkv_ref[:, 2 * width :]).astype(BF16)

    low_tile = lax.broadcasted_iota(jnp.int32, (QB, PAIR), 1) < HD

    def look(low, high, started, last):
        jobs = [(kt, b, kt - b) for kt in range(low, high) for b in range(per_chunk) if 0 <= kt - b < tiles]
        first = min(j for _, _, j in jobs)
        span = (max(j for _, _, j in jobs) + 1 - first) * QB
        keys = pl.ds(low * QB, (high - low) * QB)
        jobs = [(kt - low, b, j) for kt, b, j in jobs]

        def body(pair, _):
            cols = pl.ds(pl.multiple_of(pair * PAIR, PAIR), PAIR)
            k_pair, v_pair, kx = k_ref[keys, cols], v_ref[keys, cols], kx_ref[keys, :]
            low_k = lax.broadcasted_iota(jnp.int32, k_pair.shape, 1) < HD
            for h in range(2):
                mine_k = low_k if h == 0 else jnp.logical_not(low_k)
                mine = low_tile if h == 0 else jnp.logical_not(low_tile)
                bias[:, :span] = toeplitz(base_ref[pair, h : h + 1, first * QB : first * QB + span + QB])
                kaug[: (high - low) * QB] = jnp.where(mine_k, k_pair, kx)
                vaug[: (high - low) * QB] = jnp.where(mine_k, v_pair, jnp.ones_like(v_pair))
                held = pl.ds(pl.multiple_of((2 * pair + h) * PAIR, PAIR), PAIR)
                for b in range(per_chunk):
                    here = pl.ds(b * QB, QB)
                    q_aug = jnp.where(mine, q_ref[here, cols], qx_ref[here, :])
                    work = [(pl.ds(kt * QB, QB), pl.ds((j - first) * QB, QB)) for kt, block, j in jobs if block == b]
                    top = None
                    for part, over in work:
                        score = dot_nt(q_aug, kaug[part, :]) + bias[:, over]
                        scores[b % scores.shape[0], :, over] = score
                        most = jnp.maximum(score[:, :128], score[:, 128:])
                        top = most if top is None else jnp.maximum(top, most)
                    top = jnp.max(top, axis=1, keepdims=True)
                    acc = None
                    if started:
                        lane_at = HD if h == 0 else 0
                        before = lse_ref[here, cols][:, lane_at : lane_at + 1]
                        top = jnp.maximum(top, before)
                        acc = gkv[here, held] * jnp.exp(before - top)
                    for part, over in work:
                        p = jnp.exp(scores[b % scores.shape[0], :, over] - top).astype(BF16)
                        more = dot_nn(p, vaug[part, :])
                        acc = more if acc is None else acc + more
                    if last:
                        value = (acc / pltpu.roll(acc, HD, 1)).astype(BF16)
                        att_ref[here, cols] = value if h == 0 else jnp.where(mine, value, att_ref[here, cols])
                        stat = top + jnp.log(acc)
                    else:
                        gkv[here, held] = acc
                        stat = jnp.broadcast_to(top, (QB, PAIR))
                    lse_ref[here, cols] = jnp.where(mine, lse_ref[here, cols], stat)
            return _

        lax.fori_loop(0, H // 2, body, 0)

    def keys_of(chunk):
        normed = jnp.where(seq >= back - chunk, first_norm(chunk).astype(F32), 0.0).astype(BF16)
        here = pl.ds(chunk * tokens, tokens)
        k_ref[here, :] = dot_nn(normed, wqkv_ref[:, width : 2 * width]).astype(BF16)
        v_ref[here, :] = dot_nn(normed, wqkv_ref[:, 2 * width :]).astype(BF16)

    for step in range(1, back):
        row_wait(step)
        row_send(step + 1)
        if step == 1:
            dealt_grad = deal_out(1, cotangent_ref, g_ref, 0)
            gathers[3].start()
        keys_of(back - step)
        if step % 2:
            high = (back - step + 2) * per_chunk
            look((back - step) * per_chunk, high, step > 1, False)
    for gather in gathers[1:]:
        gather.relay()
    row_wait(back)
    keys_of(0)
    look(0, per_chunk, True, True)
    for gather in gathers[1:]:
        gather.relay_far()
    for gather in gathers[1:]:
        gather.arrive()
    for copy in dealt_grad:
        copy.wait_recv()
    for copy in dealt + dealt_grad:
        copy.wait_send()

    def ret_copy(which, step):
        peer = lax.rem(dp + step, groups)
        return pltpu.make_async_remote_copy(
            src_ref=slots.at[which, peer], dst_ref=(ret_out, ret_grad)[which].at[dp],
            send_sem=ret_sems.at[0, which, step - 1], recv_sem=ret_sems.at[1, which, step - 1],
            device_id={"dp": peer}, device_id_type=mesh_ids,
        )

    def send_back(which):
        for step in range(1, groups):
            ret_copy(which, step).start()
        (ret_out, ret_grad)[which][dp] = slots[which, dp]

    resid = xwin[own_rows, :].astype(F32) + dot_nn(att_ref[...], wout_ref[...])
    normal, scale = norm_stats(resid)
    gain_two = gains_ref[2:3, :]
    a2 = (normal * gain_two + gains_ref[3:4, :]).astype(BF16)
    a2_t = flip(a2)
    g = g_ref[...]
    y = resid
    da2 = jnp.zeros((tokens, width), F32)
    rows_up, rows_down = width // groups, wdown_ref.shape[0] // groups
    for c in range(wdown_ref.shape[0] // width):
        cols = pl.ds(c * width, width)
        upper = dot_nn(a2, wup_ref[:, cols])
        phi = 0.5 + 0.5 * lax.erf(upper * (0.5**0.5))
        act = (upper * phi).astype(BF16)
        y = y + dot_nn(act, wdown_ref[cols, :])
        slope = phi + upper * (jnp.exp(-0.5 * upper * upper) * 0.3989422804014327)
        dup = (dot_nt(g, wdown_ref[cols, :]) * slope).astype(BF16)
        da2 = da2 + dot_nt(dup, wup_ref[:, cols])
        grad_down = dot_nn(flip(act), g).astype(BF16)
        for o in range(width // rows_down):
            sources[0][c * (width // rows_down) + o] = grad_down[o * rows_down : (o + 1) * rows_down]
        per_step = width // rows_down // 2
        down.stage1(range(c * per_step, (c + 1) * per_step))
        grad_up = dot_nn(a2_t, dup).astype(BF16)
        for o in range(groups):
            sources[1][o, c * rows_up : (c + 1) * rows_up] = grad_up[o * rows_up : (o + 1) * rows_up]
    up.stage1()
    y = y.astype(BF16)
    for o in range(groups):
        slots[0, o] = y[o * length : (o + 1) * length]
    small_ref[0, 2:3, :] = jnp.sum(da2 * normal, axis=0, keepdims=True)
    small_ref[0, 3:4, :] = jnp.sum(da2, axis=0, keepdims=True)
    dres = g.astype(F32) + norm_back(da2 * gain_two, normal, scale)
    dres_ref[...] = dres
    dbr = dres.astype(BF16)
    grad_out = dot_nn(flip(att_ref[...]), dbr).astype(BF16)
    rows_out = width // groups
    for o in range(groups):
        sources[2][o] = grad_out[o * rows_out : (o + 1) * rows_out]
    out_sum.stage1()
    do_ref[...] = dot_nt(dbr, wout_ref[...]).astype(BF16)
    q_t[...] = flip(q_ref[...])
    do_t[...] = flip(do_ref[...])

    lane = lax.broadcasted_iota(jnp.int32, (tokens, PAIR), 1)
    extra = lax.rem(lane, HD)
    low_half = lane < HD
    swap = (
        (lax.broadcasted_iota(jnp.int32, (PAIR, PAIR), 0) < HD)
        != (lax.broadcasted_iota(jnp.int32, (PAIR, PAIR), 1) < HD)
    ).astype(BF16)

    def prepare(pair, _):
        cols = pl.ds(pl.multiple_of(pair * PAIR, PAIR), PAIR)
        prod = do_ref[:, cols].astype(F32) * att_ref[:, cols].astype(F32)
        prod_hi = prod.astype(BF16)
        prod_lo = (prod - prod_hi.astype(F32)).astype(BF16)
        delta = -(dot_nn(prod_hi, swap) + dot_nn(prod_lo, swap))
        delta_hi = delta.astype(BF16).astype(F32)
        lse = -lse_ref[:, cols]
        lse_hi = lse.astype(BF16).astype(F32)
        lse_mid = (lse - lse_hi).astype(BF16).astype(F32)
        lse_lo = lse - lse_hi - lse_mid
        q_extra = jnp.where(
            extra == HD - 3,
            lse_hi,
            jnp.where(extra == HD - 2, lse_mid, jnp.where(extra == HD - 1, lse_lo, qx_ref[...].astype(F32))),
        ).astype(BF16)
        do_extra = jnp.where(extra == 0, delta_hi, jnp.where(extra == 1, delta - delta_hi, 0.0)).astype(BF16)
        qaug[2 * pair] = jnp.where(low_half, q_ref[:, cols], q_extra)
        qaug[2 * pair + 1] = jnp.where(low_half, q_extra, q_ref[:, cols])
        doaug[2 * pair] = jnp.where(low_half, do_ref[:, cols], do_extra)
        doaug[2 * pair + 1] = jnp.where(low_half, do_extra, do_ref[:, cols])
        return _

    lax.fori_loop(0, H // 2, prepare, 0)
    down.stage2()
    up.stage2()
    out_sum.stage2()
    dd[...] = jnp.zeros_like(dd)
    dq_acc[...] = jnp.zeros_like(dq_acc)
    halo = []

    rounds = len(spans) * (H // 2)
    plan = {}
    for part, action in (
    ):
        plan.setdefault(part * rounds // 12, []).append(action)

    def attend(index, chunk, first, count, jobs):
        span = count * QB
        keys = pl.ds(chunk * tokens, tokens)
        fresh = set()

        def body(pair, _):
            for spot in range(H // 2):
                for action in plan.get(index * (H // 2) + spot, ()):
                    pl.when(pair == spot)(action)
            cols = pl.ds(pl.multiple_of(pair * PAIR, PAIR), PAIR)
            k_pair, v_pair, kx = k_ref[keys, cols], v_ref[keys, cols], kx_ref[keys, :]
            for h in range(2):
                mine = low_half if h == 0 else jnp.logical_not(low_half)
                head = 2 * pair + h
                bias[:, :span] = toeplitz(base_ref[pair, h : h + 1, first * QB : (first + count + 1) * QB])
                k_aug = jnp.where(mine, k_pair, kx)
                v_aug = jnp.where(mine, v_pair, jnp.ones_like(v_pair))
                feat = pl.ds(pl.multiple_of(head * HD, HD), HD)
                spot = pl.ds(h * HD, HD)
                fresh.clear()
                dq = [None] * per_chunk
                for kt in range(per_chunk):
                    part = slice(kt * QB, (kt + 1) * QB)
                    dk_t = dv_t = None
                    for b in range(per_chunk):
                        if (kt, b, chunk * per_chunk + kt - b) not in jobs:
                            continue
                        j = chunk * per_chunk + kt - b - first
                        here = pl.ds(b * QB, QB)
                        over = pl.ds(j * QB, QB)
                        p = jnp.exp(dot_nt(qaug[head, here, :], k_aug[part]) + bias[:, over])
                        ds = p * dot_nt(doaug[head, here, :], v_aug[part])
                        ds_low = ds.astype(BF16)
                        more_v = dot_nn(do_t[feat, here], p.astype(BF16))
                        more_k = dot_nn(q_t[feat, here], ds_low)
                        more_q = dot_nn(ds_low, k_pair[part])
                        dv_t = more_v if dv_t is None else dv_t + more_v
                        dk_t = more_k if dk_t is None else dk_t + more_k
                        dq[b] = more_q if dq[b] is None else dq[b] + more_q
                        if j in fresh:
                            dsum[:, over] += ds
                        else:
                            fresh.add(j)
                            dsum[:, over] = ds
                    dkt[spot, part] = dk_t
                    dvt[spot, part] = dv_t
                for b in range(per_chunk):
                    if dq[b] is not None:
                        here = pl.ds(b * QB, QB)
                        dq_acc[here, cols] += jnp.where(mine[:QB], dq[b], 0.0)
                left = jnp.concatenate([jnp.zeros((QB, QB), F32), dsum[:, :span]], axis=1)
                half = QB // 2
                while half:
                    left = left[:half] + pltpu.roll(left[half:], span + QB - half, 1)
                    half //= 2
                dd[pair, h : h + 1, first * QB : (first + count + 1) * QB] += left
            dkv[:, cols] = dkt[...].T.astype(BF16)
            dkv[:, pl.ds(pl.multiple_of(width + pair * PAIR, PAIR), PAIR)] = dvt[...].T.astype(BF16)
            return _

        lax.fori_loop(0, H // 2, body, 0)

    def halo_copy(step):
        return pltpu.make_async_remote_copy(
            src_ref=halo_send.at[(step - 1) % 2], dst_ref=halo_land.at[step - 1],
            send_sem=halo_sems.at[0, step - 1], recv_sem=halo_sems.at[1, step - 1],
            device_id={"seq": lax.rem(seq + splits - 1, splits)}, device_id_type=pl.DeviceIdType.MESH,
        )

    grad_normed = None
    for index, (chunk, first, count, jobs) in enumerate(spans):
        attend(index, chunk, first, count, jobs)
        step = back - chunk
        part = dot_nt(dkv[...], wqkv_ref[:, width:])
        rows_t = first_norm(chunk)
        if step > 0:
            rows_t = jnp.where(seq >= step, rows_t.astype(F32), 0.0)
        rows_t = flip(rows_t)
        if index == 0:
            gkv[...] = dot_nn(rows_t, dkv[...])
        else:
            gkv[...] += dot_nn(rows_t, dkv[...])
        if step == 0:
            dq_low = (dq_acc[...] * (HD**-0.5)).astype(BF16)
            grad_normed = part + dot_nt(dq_low, wqkv_ref[:, :width])
            grad_q = dot_nn(rows_t, dq_low).astype(BF16)
            for o in range(groups):
                take = slice(o * rows_up, (o + 1) * rows_up)
                sources[3][o, :rows_up] = grad_q[take]
                sources[3][o, rows_up : 2 * rows_up] = gkv[take, :width].astype(BF16)
                sources[3][o, 2 * rows_up :] = gkv[take, width:].astype(BF16)
            qkv_sum.stage1()
        else:
            if step < back:

                @pl.when((seq + 1 < splits) & (seq >= step))
                def _(step=step):
                    halo_copy(step + 1).wait_recv()

                arrived = jnp.where((seq + 1 < splits) & (seq >= step), halo_land[step].astype(F32), 0.0)
                part = part + arrived
            if step + 2 <= back:

                @pl.when(seq >= step + 2)
                def _(step=step):
                    halo_copy(step + 2).wait_send()

            halo_send[(step - 1) % 2] = part.astype(BF16)

            @pl.when(seq >= step)
            def _(step=step):
                halo_copy(step).start()

    down.stage3()
    up.stage3()
    out_sum.stage3()
    qkv_sum.stage2()
    send_back(0)
    down.stage4()

    @pl.when(seq + 1 < splits)
    def _():
        halo_copy(1).wait_recv()

    grad_normed = grad_normed + jnp.where(seq + 1 < splits, halo_land[0].astype(F32), 0.0)
    normal, scale = norm_stats(xwin[own_rows, :].astype(F32))
    small_ref[0, 0:1, :] = jnp.sum(grad_normed * normal, axis=0, keepdims=True)
    small_ref[0, 1:2, :] = jnp.sum(grad_normed, axis=0, keepdims=True)
    small_ref[0, 4:8, :] = jnp.zeros((4, width), F32)
    dd_all = dd[...].reshape(H, dd.shape[-1])
    dd_hi = dd_all.astype(BF16)
    dd_mid = (dd_all - dd_hi.astype(F32)).astype(BF16)
    small_ref[0, 8:16, :] = jnp.zeros((8, width), F32)
    small_ref[0, 8:16, :NBK] = dot_nt(dd_hi, hot_ref[...]) + dot_nt(dd_mid, hot_ref[...])
    small = SmallSummer(small_ref, small_land, small_sems)
    small.pair()
    dx = (dres_ref[...] + norm_back(grad_normed * gains_ref[0:1, :], normal, scale)).astype(BF16)
    for o in range(groups):
        slots[1, o] = dx[o * length : (o + 1) * length]
    send_back(1)
    qkv_sum.stage2b()
    small.take()
    small.plane()
    up.stage4()
    out_sum.stage4()
    qkv_sum.stage3()
    small.take()
    small.along()
    qkv_sum.stage4()
    small.take()
    small_out[...] = small_ref[3]
    for summer in summers:
        summer.finish()
    small.finish()
    for which in range(2):
        for step in range(1, groups):
            ret_copy(which, step).wait()
    for gather in gathers:
        gather.finish()
    for copy in few:
        copy.wait_send()
    for step in range(1, back + 1):

        @pl.when((seq + 1 < splits) & (seq + 1 >= step))
        def _(step=step):
            row_copy(step).wait_send()
    for step in range(1, min(back, 2) + 1):

        @pl.when(seq >= step)
        def _(step=step):
            halo_copy(step).wait_send()


def layer(back, tokens_in, cotangent, deal, lengths, buckets, vectors, rel, wqkv, wout, wup, wdown):
    splits, groups = lax.axis_size("seq"), lax.axis_size("dp")
    tokens, width = tokens_in.shape
    length = tokens // groups
    per_chunk = tokens // QB
    maxlen = buckets.shape[0]
    window, reach = (back + 1) * tokens, back * tokens + 2 * QB
    wide = min(2, back) * per_chunk
    span = min(wide + per_chunk - 1, reach // QB - 1) * QB
    grads = [wdown.shape[0], wup.shape[0] * wup.shape[1] // width, width // groups, 3 * width // groups]
    out_shapes, more, sources = [], [], []
    for height in grads:
        shape = (groups, height, width)
        out, scratch = summer_shapes(shape, BF16, splits)
        sources.append(pltpu.VMEM(shape, BF16))
        out_shapes.append(out)
        more += scratch
    out_shapes.append(jax.ShapeDtypeStruct((16, width), F32))
    out_shapes += [jax.ShapeDtypeStruct((groups, length, width), BF16)] * 2
    small_copies = 1 + (groups // 2 - 1) + (splits - 1)
    scratch = sources + more + [
        pltpu.VMEM((4, 16, width), F32),
        pltpu.VMEM((small_copies, 16, width), F32),
        pltpu.SemaphoreType.DMA((2, small_copies)),
        pltpu.VMEM((2, groups, length, width), BF16),
        pltpu.SemaphoreType.DMA((2, 2, groups - 1)),
        pltpu.VMEM((min(back, 2), tokens, width), BF16),
        pltpu.VMEM((back, tokens, width), BF16),
        pltpu.SemaphoreType.DMA((2, back)),
        pltpu.VMEM((tokens, width), F32),
        pltpu.VMEM((tokens, width), BF16),
        pltpu.VMEM((H, tokens, PAIR), BF16),
        pltpu.VMEM((H, tokens, PAIR), BF16),
        pltpu.VMEM((width, tokens), BF16),
        pltpu.VMEM((width, tokens), BF16),
        pltpu.VMEM((QB, span), F32),
        pltpu.VMEM((2 if span <= 1024 else 1, QB, span), F32),
        pltpu.VMEM((wide * QB, PAIR), BF16),
        pltpu.VMEM((wide * QB, PAIR), BF16),
        pltpu.VMEM((H // 2, 2, reach), F32),
        pltpu.VMEM((tokens, width), F32),
        pltpu.VMEM((PAIR, tokens), F32),
        pltpu.VMEM((PAIR, tokens), F32),
        pltpu.VMEM((tokens, 2 * width), BF16),
        pltpu.VMEM((width, 2 * width), F32),
        pltpu.VMEM((window, width), BF16),
        pltpu.VMEM((tokens, width), BF16),
        pltpu.VMEM((width, 3 * width), BF16),
        pltpu.VMEM((width, width), BF16),
        pltpu.VMEM((width, wup.shape[1]), BF16),
        pltpu.VMEM((wup.shape[1], width), BF16),
        pltpu.SemaphoreType.DMA((4, 2, max(8, groups - 1))),
        pltpu.SemaphoreType.DMA((4,)),
        pltpu.SemaphoreType.DMA((2, 2, groups - 1)),
        pltpu.SemaphoreType.DMA((2, back)),
        pltpu.VMEM((groups, 16, PAIR), F32),
        pltpu.SemaphoreType.DMA((2, groups - 1)),
        pltpu.VMEM((8, width), F32),
        pltpu.VMEM((H // 2, 2, reach), F32),
        pltpu.VMEM((tokens, width), BF16),
        pltpu.VMEM((window, width), BF16),
        pltpu.VMEM((window, width), BF16),
        pltpu.VMEM((tokens, width), BF16),
        pltpu.VMEM((tokens, width), F32),
        pltpu.VMEM((16, PAIR), F32),
        pltpu.VMEM((NBK, PAIR), F32),
        pltpu.VMEM((NBK, reach), BF16),
        pltpu.VMEM((tokens, PAIR), BF16),
        pltpu.VMEM((window, PAIR), BF16),
    ]
    vmem, smem = pl.BlockSpec(memory_space=pltpu.VMEM), pl.BlockSpec(memory_space=pltpu.SMEM)
    return pl.pallas_call(
        functools.partial(layer_kernel, back, maxlen),
        in_specs=[vmem] * 2 + [smem] * 2 + [vmem] * (2 + len(vectors)) + [pl.BlockSpec(memory_space=pl.ANY)] * 4,
        out_specs=[vmem] * len(out_shapes),
        out_shape=out_shapes,
        scratch_shapes=scratch,
        compiler_params=pltpu.CompilerParams(collective_id=1, has_side_effects=True, vmem_limit_bytes=VMEM_LIMIT),
        name="layer",
    )(tokens_in, cotangent, deal, lengths, buckets.reshape(-1, PAIR), *vectors, rel, wqkv, wout, wup, wdown)


def finish_kernel(deal_ref, down, up, out, qkv, small, ret_out, ret_grad, *outs):
    o_out, o_grad, o_qkv, o_wout, o_up, o_down, *o_vectors, o_rel = outs
    length = ret_out.shape[1]
    for g in range(ret_out.shape[0]):
        piece = deal_ref[0, g]
        o_out[pl.ds(g * length, length), :] = ret_out[piece]
        o_grad[pl.ds(g * length, length), :] = ret_grad[piece]
    for source, target in ((down, o_down), (up, o_up), (out, o_wout), (qkv, o_qkv)):
        direct = source.shape[0] * source.shape[1] * source.shape[2] != target.shape[0] * target.shape[1]
        cols = source.shape[2]
        if direct:
            value = add_low(*[source[t] for t in range(source.shape[0])])
        else:
            value = source[...].reshape(-1, cols).astype(F32)
        height = target.shape[0]
        for c in range(target.shape[1] // cols):
            target[:, c * cols : (c + 1) * cols] = value[c * height : (c + 1) * height]
    dp, groups = lax.axis_index("dp"), lax.axis_size("dp")
    for i, target in enumerate(o_vectors):
        size = target.shape[0]
        value = small[i : i + 1, :size]
        for o in range(1, groups):
            value = jnp.where(dp == o, small[i : i + 1, o * size : (o + 1) * size], value)
        target[...] = value.reshape(size)
    levels = small[8 : 8 + H, :PAIR].T
    size = o_rel.shape[0]
    value = levels[:size, :H]
    for o in range(1, groups):
        value = jnp.where(dp == o, levels[o * size : (o + 1) * size, :H], value)
    o_rel[...] = value


def finish(deal, sums, returned, shapes):
    return pl.pallas_call(
        finish_kernel,
        in_specs=[pl.BlockSpec(memory_space=pltpu.SMEM)] + [pl.BlockSpec(memory_space=pltpu.VMEM)] * 7,
        out_specs=[pl.BlockSpec(memory_space=pltpu.VMEM)] * len(shapes),
        out_shape=shapes,
        compiler_params=pltpu.CompilerParams(vmem_limit_bytes=VMEM_LIMIT),
        name="finish",
    )(deal, *sums, *returned)


def shards(
    tokens,
    cotangent,
    deal,
    lengths,
    buckets,
    ln1_gain,
    ln1_bias,
    w_qkv,
    w_out,
    rel_bias,
    ln2_gain,
    ln2_bias,
    w_up,
    w_down,
):
    tok_dev = tokens.shape[0]
    back = -(-buckets.shape[0] // tok_dev)
    *sums, small_total, back_out, back_grad = layer(
        back, tokens, cotangent, deal, lengths, buckets, (ln1_gain, ln1_bias, ln2_gain, ln2_bias), rel_bias,
        w_qkv, w_out, w_up, w_down,
    )
    output, grad_tokens, total_qkv, total_out, total_up, total_down, g_one, b_one, g_two, b_two, total_rel = finish(
        deal,
        [*sums, small_total],
        [back_out, back_grad],
        [jax.ShapeDtypeStruct(tokens.shape, BF16)] * 2
        + [
            jax.ShapeDtypeStruct(a.shape, F32)
            for a in (w_qkv, w_out, w_up, w_down, ln1_gain, ln1_bias, ln2_gain, ln2_bias, rel_bias)
        ],
    )
    return (
        output, grad_tokens, g_one, b_one, total_qkv, total_out, total_rel, g_two, b_two, total_up, total_down,
    )


def solution(mesh):
    by_all, by_dp = P(("seq", "dp"), None), P("dp", None)
    return jax.shard_map(
        shards,
        mesh=mesh,
        in_specs=(
            by_all, by_all, by_all, by_dp, P(), P("dp"), P("dp"), by_dp, by_dp, by_dp, P("dp"), P("dp"), by_dp, by_dp,
        ),
        out_specs=(by_all, by_all, P("dp"), P("dp"), by_dp, by_dp, by_dp, P("dp"), P("dp"), by_dp, by_dp),
        check_vma=False,
    )
```

```python
import functools

import jax
import jax.numpy as jnp
from jax import lax
from jax.experimental import pallas as pl
from jax.experimental.pallas import tpu as pltpu
from jax.sharding import PartitionSpec as P

H = 8
HD = 64
NBK = 32
QB = 256
PAIR = 2 * HD
BIG = -1e30
F32 = jnp.float32
BF16 = jnp.bfloat16
VMEM_LIMIT = 60 * 1024 * 1024

NT = (((1,), (1,)), ((), ()))
NN = (((1,), (0,)), ((), ()))


def dot_nt(a, b):
    return lax.dot_general(a, b, NT, preferred_element_type=F32)


def dot_nn(a, b):
    return lax.dot_general(a, b, NN, preferred_element_type=F32)


def toeplitz(row):
    width = row.shape[1]
    return pltpu.roll(jnp.broadcast_to(row, (QB, width)), 0, 1, stride=1, stride_axis=0)[:, QB:]


def add_low(first, *others):
    total = first.astype(F32)
    for other in others:
        total = total + other.astype(F32)
    return total


def square(chip):
    return chip + 1 - 2 * lax.rem(chip, 2), chip + 2 - 4 * (chip // 2), 3 - chip


class Summer:
    def __init__(self, source, pair, recv2, mine, recv3, out, sems, halving):
        self.source, self.pair, self.recv2 = source, pair, recv2
        self.mine, self.recv3, self.out, self.sems = mine, recv3, out, sems
        self.dp, self.seq = lax.axis_index("dp"), lax.axis_index("seq")
        self.pairs, self.splits = source.shape[0] // 2, lax.axis_size("seq")
        self.core, self.chip = lax.rem(self.dp, 2), self.dp // 2
        self.rows = out.shape[1]
        self.scatter = self.rows < mine.shape[0]
        self.halving = halving and self.scatter
        self.rounds = (self.splits - 1).bit_length() if self.halving else 1
        self.hops2 = self.pairs - 1

    def copy(self, src, dst, slot, device):
        return pltpu.make_async_remote_copy(
            src_ref=src, dst_ref=dst, send_sem=self.sems.at[0, slot], recv_sem=self.sems.at[1, slot],
            device_id=device, device_id_type=pl.DeviceIdType.MESH,
        )

    def copy1(self, k):
        other = 1 - self.core
        return self.copy(self.source.at[2 * k + other], self.pair.at[k], k, {"dp": self.dp + 1 - 2 * self.core})

    def copy2(self, step):
        k = lax.rem(self.chip + 1 + step, self.pairs)
        return self.copy(self.pair.at[k], self.recv2.at[step], self.pairs + step, {"dp": 2 * k + self.core})

    def copy3(self, step):
        t = lax.rem(self.seq + 1 + step, self.splits)
        src = self.mine.at[pl.ds(pl.multiple_of(t * self.rows, self.rows), self.rows)] if self.scatter else self.mine
        dst = self.recv3.at[step] if self.scatter else self.out.at[self.seq]
        return self.copy(src, dst, self.pairs + self.hops2 + step, {"seq": t})

    def copy4(self, step):
        t = lax.rem(self.seq + 1 + step, self.splits)
        slot = self.pairs + self.hops2 + self.splits - 1 + step
        return self.copy(self.out.at[self.seq], self.out.at[self.seq], slot, {"seq": t})

    def exchange(self, back, turn):
        low, stride = 2**turn, 2 ** (turn + 1)
        bit = lax.rem(self.seq // low, 2)
        partner = self.seq + low - 2 * low * bit
        kept, given = lax.rem(self.seq, stride), lax.rem(partner, stride)
        count = self.splits // stride
        base = self.splits - self.splits // low
        slot = self.pairs + self.hops2 + base + (self.splits - 1 if back else 0)
        moves = []
        for i in range(count):
            mine, theirs = kept + i * stride, given + i * stride
            src = self.out.at[mine] if back else self.mine.at[self.part(theirs)]
            dst = self.out.at[mine] if back else self.recv3.at[base + i]
            moves.append((self.copy(src, dst, slot + i, {"seq": partner}), mine, base + i))
        return moves

    def part(self, t):
        return pl.ds(pl.multiple_of(t * self.rows, self.rows), self.rows)

    def turn(self, turn):
        if not self.halving:
            return
        for copy, kept, slot in self.exchange(False, turn - 1):
            copy.wait_recv()
            self.mine[self.part(kept)] = add_low(self.mine[self.part(kept)], self.recv3[slot]).astype(self.mine.dtype)
        if turn < self.rounds:
            for copy, _, _ in self.exchange(False, turn):
                copy.start()
        else:
            self.out[self.seq] = self.mine[self.part(self.seq)]
            for copy, _, _ in self.exchange(True, turn - 1):
                copy.start()

    def turn_back(self, turn):
        if not self.halving:
            return
        for copy, _, _ in self.exchange(True, turn):
            copy.wait_recv()
        if turn > 0:
            for copy, _, _ in self.exchange(True, turn - 1):
                copy.start()

    def stage1(self, some=None):
        for k in range(self.pairs) if some is None else some:
            self.copy1(k).start()

    def stage2(self):
        for k in range(self.pairs):
            self.copy1(k).wait_recv()
        for step in range(self.pairs):
            k = lax.rem(self.chip + 1 + step, self.pairs)
            self.pair[k] = add_low(self.source[2 * k + self.core], self.pair[k]).astype(self.pair.dtype)
            if step < self.pairs - 1:
                self.copy2(step).start()

    def stage3(self):
        for step in range(self.pairs - 1):
            self.copy2(step).wait_recv()
        total = add_low(self.pair[self.chip], *[self.recv2[step] for step in range(self.pairs - 1)])
        self.mine[...] = total.astype(self.mine.dtype)
        if self.halving:
            for copy, _, _ in self.exchange(False, 0):
                copy.start()
            return
        for step in range(self.splits - 1):
            self.copy3(step).start()
        if not self.scatter:
            self.out[self.seq] = self.mine[...]

    def stage4(self):
        if self.halving:
            return
        for step in range(self.splits - 1):
            self.copy3(step).wait_recv()
        if not self.scatter:
            return
        own = self.mine[pl.ds(pl.multiple_of(self.seq * self.rows, self.rows), self.rows)]
        total = add_low(own, *[self.recv3[step] for step in range(self.splits - 1)])
        self.out[self.seq] = total.astype(self.out.dtype)
        for step in range(self.splits - 1):
            self.copy4(step).start()

    def finish(self):
        for k in range(self.pairs):
            self.copy1(k).wait_send()
        for step in range(self.pairs - 1):
            self.copy2(step).wait_send()
        if self.halving:
            for turn in range(self.rounds):
                for back in (False, True):
                    for copy, _, _ in self.exchange(back, turn):
                        copy.wait_send()
            return
        for step in range(self.splits - 1):
            self.copy3(step).wait_send()
        if self.scatter:
            for step in range(self.splits - 1):
                self.copy4(step).wait()


def summer_shapes(shape, dtype, splits):
    groups, rows, cols = shape
    pairs = groups // 2
    scatter = rows % (16 * splits) == 0
    out = jax.ShapeDtypeStruct((splits, rows // splits if scatter else rows, cols), dtype)
    copies = pairs + (pairs - 1) + (splits - 1) * (2 if scatter else 1)
    scratch = [
        pltpu.VMEM((pairs, rows, cols), dtype),
        pltpu.VMEM((pairs - 1, rows, cols), dtype),
        pltpu.VMEM((rows, cols), dtype),
        pltpu.VMEM((splits - 1, out.shape[1] if scatter else 16, cols), dtype),
        pltpu.SemaphoreType.DMA((2, copies)),
    ]
    return out, scratch


def greet(peers):
    barrier = pltpu.get_barrier_semaphore()
    for device in peers:
        pl.semaphore_signal(barrier, inc=1, device_id=device, device_id_type=pl.DeviceIdType.MESH)
    pl.semaphore_wait(barrier, len(peers))


def others(axis):
    size, me = lax.axis_size(axis), lax.axis_index(axis)
    return [{axis: lax.rem(me + step, size)} for step in range(1, size)]


class SmallSummer:
    def __init__(self, ref, land, sems):
        self.ref, self.land, self.sems = ref, land, sems
        self.dp, self.seq = lax.axis_index("dp"), lax.axis_index("seq")
        self.pairs, self.splits = lax.axis_size("dp") // 2, lax.axis_size("seq")
        self.slot, self.copies, self.sent = 0, [], []

    def send(self, devices):
        self.copies = []
        for device in devices:
            copy = pltpu.make_async_remote_copy(
                src_ref=self.ref.at[len(self.sent)], dst_ref=self.land.at[self.slot],
                send_sem=self.sems.at[0, self.slot], recv_sem=self.sems.at[1, self.slot],
                device_id=device, device_id_type=pl.DeviceIdType.MESH,
            )
            copy.start()
            self.copies.append((self.slot, copy))
            self.slot += 1
        self.sent.append(self.copies)

    def take(self):
        stage = len(self.sent) - 1
        total = self.ref[stage]
        for slot, copy in self.copies:
            copy.wait_recv()
            total = total + self.land[slot]
        self.ref[stage + 1] = total

    def pair(self):
        self.send([{"dp": self.dp + 1 - 2 * lax.rem(self.dp, 2)}])

    def plane(self):
        core, chip = lax.rem(self.dp, 2), self.dp // 2
        self.send([{"dp": 2 * lax.rem(chip + step, self.pairs) + core} for step in range(1, self.pairs)])

    def along(self):
        self.send([{"seq": lax.rem(self.seq + step, self.splits)} for step in range(1, self.splits)])

    def finish(self):
        for copies in self.sent:
            for _, copy in copies:
                copy.wait_send()


def norm_stats(values):
    average = jnp.mean(values, axis=-1, keepdims=True)
    centred = values - average
    scale = lax.rsqrt(jnp.mean(centred * centred, axis=-1, keepdims=True) + 1e-05)
    return centred * scale, scale


def norm_back(grad, normal, scale):
    return scale * (
        grad - jnp.mean(grad, axis=-1, keepdims=True) - normal * jnp.mean(grad * normal, axis=-1, keepdims=True)
    )


def flip(values):
    return values.astype(F32).T.astype(BF16)


def phase_spans(back, per_chunk, tiles):
    spans = []
    for chunk in range(back + 1):
        jobs = [
            (kt, b, chunk * per_chunk + kt - b)
            for kt in range(per_chunk)
            for b in range(per_chunk)
            if 0 <= chunk * per_chunk + kt - b < tiles
        ]
        first, last = min(j[2] for j in jobs), max(j[2] for j in jobs)
        spans.append((chunk, first, last - first + 1, jobs))
    return spans


class Gather:
    def __init__(self, shard, full, sems, own_sem):
        self.shard, self.full, self.sems = shard, full, sems
        self.rows = shard.shape[0]
        self.dp = lax.axis_index("dp")
        self.pairs = lax.axis_size("dp") // 2
        self.square = self.pairs == 4
        self.core, self.chip = lax.rem(self.dp, 2), self.dp // 2
        self.sibling = {"dp": self.dp + 1 - 2 * self.core}
        self.own = pltpu.make_async_copy(shard, self.place(self.dp), own_sem)
        if self.square:
            self.around = square(self.chip)
        else:
            self.around = [lax.rem(self.chip + step, self.pairs) for step in range(1, self.pairs)]
            self.behind = [lax.rem(self.chip + self.pairs - step, self.pairs) for step in range(1, self.pairs)]

    def place(self, owner, first=0, rows=None):
        start = pl.multiple_of(owner * self.rows, self.rows)
        return self.full.at[pl.ds(start + first, self.rows if rows is None else rows)]

    def copy(self, src, dst, slot, device):
        return pltpu.make_async_remote_copy(
            src_ref=src, dst_ref=dst, send_sem=self.sems.at[0, slot], recv_sem=self.sems.at[1, slot],
            device_id=device, device_id_type=pl.DeviceIdType.MESH,
        )

    def mate(self, chip):
        return {"dp": 2 * chip + self.core}

    def start(self):
        reach = self.around[:2] if self.square else self.around
        self.sent = [self.copy(self.shard, self.place(self.dp), 1 + i, self.mate(c)) for i, c in enumerate(reach)]
        self.near = self.copy(self.shard, self.place(self.dp), 0, self.sibling)
        for copy in self.sent + [self.near]:
            copy.start()
        self.own.start()
        self.waiting = [self.near]

    def share(self, chip, slot):
        there = self.place(2 * chip + self.core)
        copy = self.copy(there, there, slot, self.sibling)
        copy.start()
        self.waiting.append(copy)
        self.sent.append(copy)

    def relay(self):
        for copy in self.sent:
            copy.wait_recv()
        if not self.square:
            for i, chip in enumerate(self.behind):
                self.share(chip, self.pairs + i)
            return
        across, along, _ = self.around
        half = self.rows // 2
        self.passed = []
        for i, (origin, target) in enumerate(((across, along), (along, across))):
            there = self.place(2 * origin + self.core, i * half, half)
            copy = self.copy(there, there, 3 + i, self.mate(target))
            copy.start()
            self.passed.append(copy)
        self.share(across, 5)
        self.share(along, 6)

    def relay_far(self):
        if not self.square:
            return
        for copy in self.passed:
            copy.wait_recv()
        self.share(self.around[2], 7)
        self.sent += self.passed

    def arrive(self):
        self.own.wait()
        for copy in self.waiting:
            copy.wait_recv()

    def finish(self):
        for copy in self.sent + [self.near]:
            copy.wait_send()


def layer_kernel(back, maxlen, *refs):
    (
        tokens_ref, cotangent_ref, deal_ref, lengths_ref, buckets_ref, *vector_refs, rel_ref,
        wqkv_s, wout_s, wup_s, wdown_s,
    ) = refs[:14]
    *sums, small_out, ret_out, ret_grad = refs[14:23]
    it = iter(refs[23:])
    sources = [next(it) for _ in range(6)]
    summers = [
        Summer(source, *[next(it) for _ in range(4)], out, next(it), halving)
        for source, out, halving in zip(sources, sums, (True, True, True, False, False, False))
    ]
    down, up, out_sum, *qkv_sums = summers
    small_ref, small_land, small_sems = next(it), next(it), next(it)
    slots, ret_sems, halo_send, halo_land, halo_sems = (next(it) for _ in range(5))
    dres_ref, do_ref, qaug, doaug, q_t, do_t = (next(it) for _ in range(6))
    bias, scores, kaug, vaug, dd, dq_acc, dkt, dvt, dkv, gkv = (next(it) for _ in range(10))
    dsum = scores.at[0]
    xwin, g_ref, wqkv_ref, wout_ref, wup_ref, wdown_ref = (next(it) for _ in range(6))
    gather_sems, own_sems, deal_sems, row_sems, few_land, few_sems = (next(it) for _ in range(6))
    gains_ref, base_ref, q_ref, k_ref, v_ref, att_ref, lse_ref = (next(it) for _ in range(7))
    few_mine, rel_all, hot_ref, qx_ref, kx_ref = (next(it) for _ in range(5))
    dp, groups = lax.axis_index("dp"), lax.axis_size("dp")
    seq, splits = lax.axis_index("seq"), lax.axis_size("seq")
    tokens, width = tokens_ref.shape
    length = tokens // groups
    per_chunk = tokens // QB
    tiles = base_ref.shape[-1] // QB - 1
    spans = phase_spans(back, per_chunk, tiles)
    mesh_ids = pl.DeviceIdType.MESH
    greet(others("dp") + others("seq"))

    def deal_out(which, source, target, first_row):
        for j in range(groups):
            piece = source[:length, :]
            for k in range(1, groups):
                piece = jnp.where(deal_ref[0, k] == j, source[k * length : (k + 1) * length, :], piece)
            slots[which, j] = piece
        copies = []
        rows_here = pl.ds(pl.multiple_of(first_row + dp * length, length), length)
        for step in range(1, groups):
            peer = lax.rem(dp + step, groups)
            copy = pltpu.make_async_remote_copy(
                src_ref=slots.at[which, peer], dst_ref=target.at[rows_here],
                send_sem=deal_sems.at[0, which, step - 1], recv_sem=deal_sems.at[1, which, step - 1],
                device_id={"dp": peer}, device_id_type=mesh_ids,
            )
            copy.start()
            copies.append(copy)
        target[rows_here, :] = slots[which, dp]
        return copies

    own_first = back * tokens
    own_rows = pl.ds(own_first, tokens)
    dealt = deal_out(0, tokens_ref, xwin, own_first)
    shard_rows, rel_rows = vector_refs[0].shape[0], rel_ref.shape[0]
    few_mine[...] = jnp.zeros_like(few_mine)
    for i, vector in enumerate(vector_refs):
        few_mine[i : i + 1, :shard_rows] = vector[...].astype(F32).reshape(1, shard_rows)
    few_mine[8 : 8 + rel_rows, :H] = rel_ref[...].astype(F32)
    few = []
    for step in range(1, groups):
        copy = pltpu.make_async_remote_copy(
            src_ref=few_mine, dst_ref=few_land.at[dp],
            send_sem=few_sems.at[0, step - 1], recv_sem=few_sems.at[1, step - 1],
            device_id={"dp": lax.rem(dp + step, groups)}, device_id_type=mesh_ids,
        )
        copy.start()
        few.append(copy)
    few_land[dp] = few_mine[...]
    gathers = [
        Gather(shard, full, gather_sems.at[i], own_sems.at[i])
        for i, (shard, full) in enumerate(
            ((wqkv_s, wqkv_ref), (wout_s, wout_ref), (wup_s, wup_ref), (wdown_s, wdown_ref))
        )
    ]
    gathers[0].start()
    gathers[1].start()

    seqs = lengths_ref.shape[1]

    def segments(rows, first_pos):
        place = lax.broadcasted_iota(jnp.int32, (rows, PAIR), 0) + first_pos
        found, end = jnp.zeros((rows, PAIR), jnp.int32), 0
        for c in range(seqs):
            end = end + lengths_ref[0, c]
            found = found + (place >= end).astype(jnp.int32)
        return jnp.where(place < 0, seqs, found)

    window = kx_ref.shape[0]
    lane_w = lax.rem(lax.broadcasted_iota(jnp.int32, (window, PAIR), 1), HD)
    key_seg = segments(window, (seq - back) * tokens)
    kx_ref[...] = jnp.where((lane_w == key_seg) | (lane_w >= HD - 3), 1.0, 0.0).astype(BF16)
    lane_q = lane_w[:tokens]
    qx_ref[...] = jnp.where((lane_q <= seqs) & (lane_q != segments(tokens, seq * tokens)), BIG, 0.0).astype(BF16)

    level = lax.broadcasted_iota(jnp.int32, (NBK, PAIR), 0)
    below, up_to = jnp.zeros((NBK, PAIR), F32), jnp.zeros((NBK, PAIR), F32)
    for r in range(buckets_ref.shape[0]):
        row = buckets_ref[r : r + 1, :]
        below = below + (row < level).astype(F32)
        up_to = up_to + (row <= level).astype(F32)
    below = jnp.sum(below, axis=1, keepdims=True)
    up_to = jnp.sum(up_to, axis=1, keepdims=True)
    far = (back * tokens + QB - lax.broadcasted_iota(jnp.int32, hot_ref.shape, 1)).astype(F32)
    hot_ref[...] = jnp.where((far >= below) & (far < up_to), 1.0, 0.0).astype(BF16)
    for copy in dealt:
        copy.wait_recv()

    def row_copy(step):
        return pltpu.make_async_remote_copy(
            src_ref=xwin.at[pl.ds((back - step + 1) * tokens, tokens)],
            dst_ref=xwin.at[pl.ds((back - step) * tokens, tokens)],
            send_sem=row_sems.at[0, step - 1], recv_sem=row_sems.at[1, step - 1],
            device_id={"seq": lax.rem(seq + 1, splits)}, device_id_type=mesh_ids,
        )

    def row_send(step):
        @pl.when((seq + 1 < splits) & (seq + 1 >= step))
        def _():
            row_copy(step).start()

    def row_wait(step):
        @pl.when(seq >= step)
        def _():
            row_copy(step).wait_recv()

    row_send(1)
    for copy in few:
        copy.wait_recv()
    per_tile = PAIR // shard_rows
    for i in range(width // PAIR):
        tile = few_land[i * per_tile, :8, :]
        for o in range(1, per_tile):
            tile = tile + pltpu.roll(few_land[i * per_tile + o, :8, :], o * shard_rows, 1)
        gains_ref[:, i * PAIR : (i + 1) * PAIR] = tile
    for o in range(groups):
        rel_all[o * rel_rows : (o + 1) * rel_rows, :] = few_land[o, 8 : 8 + rel_rows, :]
    table = dot_nn(flip(rel_all[...])[:H], hot_ref[...])
    far = back * tokens + QB - lax.broadcasted_iota(jnp.int32, table.shape, 1)
    base_ref[...] = jnp.where((far >= 0) & (far < maxlen), table, BIG).reshape(base_ref.shape)

    def first_norm(chunk):
        normal, _ = norm_stats(xwin[chunk * tokens : (chunk + 1) * tokens, :].astype(F32))
        return (normal * gains_ref[0:1, :] + gains_ref[1:2, :]).astype(BF16)

    own_normed = first_norm(back)
    gathers[0].relay()
    gathers[2].start()
    gathers[3].start()
    gathers[0].relay_far()
    gathers[0].arrive()
    q_ref[...] = (dot_nn(own_normed, wqkv_ref[:, :width])).astype(BF16) * jnp.asarray(HD**-0.5, BF16)
    k_ref[own_rows, :] = dot_nn(own_normed, wqkv_ref[:, width : 2 * width]).astype(BF16)
    v_ref[own_rows, :] = dot_nn(own_normed, wqkv_ref[:, 2 * width :]).astype(BF16)

    low_tile = lax.broadcasted_iota(jnp.int32, (QB, PAIR), 1) < HD

    def look(low, high, started, last):
        jobs = [(kt, b, kt - b) for kt in range(low, high) for b in range(per_chunk) if 0 <= kt - b < tiles]
        first = min(j for _, _, j in jobs)
        span = (max(j for _, _, j in jobs) + 1 - first) * QB
        keys = pl.ds(low * QB, (high - low) * QB)
        jobs = [(kt - low, b, j) for kt, b, j in jobs]

        def body(pair, _):
            cols = pl.ds(pl.multiple_of(pair * PAIR, PAIR), PAIR)
            k_pair, v_pair, kx = k_ref[keys, cols], v_ref[keys, cols], kx_ref[keys, :]
            low_k = lax.broadcasted_iota(jnp.int32, k_pair.shape, 1) < HD
            for h in range(2):
                mine_k = low_k if h == 0 else jnp.logical_not(low_k)
                mine = low_tile if h == 0 else jnp.logical_not(low_tile)
                bias[:, :span] = toeplitz(base_ref[pair, h : h + 1, first * QB : first * QB + span + QB])
                kaug[: (high - low) * QB] = jnp.where(mine_k, k_pair, kx)
                vaug[: (high - low) * QB] = jnp.where(mine_k, v_pair, jnp.ones_like(v_pair))
                held = pl.ds(pl.multiple_of((2 * pair + h) * PAIR, PAIR), PAIR)
                for b in range(per_chunk):
                    here = pl.ds(b * QB, QB)
                    q_aug = jnp.where(mine, q_ref[here, cols], qx_ref[here, :])
                    work = [(pl.ds(kt * QB, QB), pl.ds((j - first) * QB, QB)) for kt, block, j in jobs if block == b]
                    top = None
                    for part, over in work:
                        score = dot_nt(q_aug, kaug[part, :]) + bias[:, over]
                        scores[b % scores.shape[0], :, over] = score
                        most = jnp.maximum(score[:, :128], score[:, 128:])
                        top = most if top is None else jnp.maximum(top, most)
                    top = jnp.max(top, axis=1, keepdims=True)
                    acc = None
                    if started:
                        lane_at = HD if h == 0 else 0
                        before = lse_ref[here, cols][:, lane_at : lane_at + 1]
                        top = jnp.maximum(top, before)
                        acc = gkv[here, held] * jnp.exp(before - top)
                    for part, over in work:
                        p = jnp.exp(scores[b % scores.shape[0], :, over] - top).astype(BF16)
                        more = dot_nn(p, vaug[part, :])
                        acc = more if acc is None else acc + more
                    if last:
                        value = (acc / pltpu.roll(acc, HD, 1)).astype(BF16)
                        att_ref[here, cols] = value if h == 0 else jnp.where(mine, value, att_ref[here, cols])
                        stat = top + jnp.log(acc)
                    else:
                        gkv[here, held] = acc
                        stat = jnp.broadcast_to(top, (QB, PAIR))
                    lse_ref[here, cols] = jnp.where(mine, lse_ref[here, cols], stat)
            return _

        lax.fori_loop(0, H // 2, body, 0)

    def keys_of(chunk):
        normed = jnp.where(seq >= back - chunk, first_norm(chunk).astype(F32), 0.0).astype(BF16)
        here = pl.ds(chunk * tokens, tokens)
        k_ref[here, :] = dot_nn(normed, wqkv_ref[:, width : 2 * width]).astype(BF16)
        v_ref[here, :] = dot_nn(normed, wqkv_ref[:, 2 * width :]).astype(BF16)

    for step in range(1, back):
        row_wait(step)
        row_send(step + 1)
        if step == 1:
            gathers[1].relay()
            gathers[2].relay()
            dealt_grad = deal_out(1, cotangent_ref, g_ref, 0)
        keys_of(back - step)
        if step % 2:
            high = (back - step + 2) * per_chunk
            look((back - step) * per_chunk, high, step > 1, False)
    gathers[3].relay()
    gathers[1].relay_far()
    gathers[2].relay_far()
    row_wait(back)
    keys_of(0)
    look(0, per_chunk, True, True)
    gathers[3].relay_far()
    for gather in gathers[1:]:
        gather.arrive()
    for copy in dealt_grad:
        copy.wait_recv()
    for copy in dealt + dealt_grad:
        copy.wait_send()

    def ret_copy(which, step):
        peer = lax.rem(dp + step, groups)
        return pltpu.make_async_remote_copy(
            src_ref=slots.at[which, peer], dst_ref=(ret_out, ret_grad)[which].at[dp],
            send_sem=ret_sems.at[0, which, step - 1], recv_sem=ret_sems.at[1, which, step - 1],
            device_id={"dp": peer}, device_id_type=mesh_ids,
        )

    def send_back(which):
        for step in range(1, groups):
            ret_copy(which, step).start()
        (ret_out, ret_grad)[which][dp] = slots[which, dp]

    resid = xwin[own_rows, :].astype(F32) + dot_nn(att_ref[...], wout_ref[...])
    normal, scale = norm_stats(resid)
    gain_two = gains_ref[2:3, :]
    a2 = (normal * gain_two + gains_ref[3:4, :]).astype(BF16)
    a2_t = flip(a2)
    g = g_ref[...]
    y = resid
    da2 = jnp.zeros((tokens, width), F32)
    rows_up, rows_down = width // groups, wdown_ref.shape[0] // groups
    for c in range(wdown_ref.shape[0] // width):
        cols = pl.ds(c * width, width)
        upper = dot_nn(a2, wup_ref[:, cols])
        phi = 0.5 + 0.5 * lax.erf(upper * (0.5**0.5))
        act = (upper * phi).astype(BF16)
        y = y + dot_nn(act, wdown_ref[cols, :])
        slope = phi + upper * (jnp.exp(-0.5 * upper * upper) * 0.3989422804014327)
        dup = (dot_nt(g, wdown_ref[cols, :]) * slope).astype(BF16)
        da2 = da2 + dot_nt(dup, wup_ref[:, cols])
        grad_down = dot_nn(flip(act), g).astype(BF16)
        for o in range(width // rows_down):
            sources[0][c * (width // rows_down) + o] = grad_down[o * rows_down : (o + 1) * rows_down]
        per_step = width // rows_down // 2
        down.stage1(range(c * per_step, (c + 1) * per_step))
        grad_up = dot_nn(a2_t, dup).astype(BF16)
        for o in range(groups):
            sources[1][o, c * rows_up : (c + 1) * rows_up] = grad_up[o * rows_up : (o + 1) * rows_up]
    up.stage1()
    y = y.astype(BF16)
    for o in range(groups):
        slots[0, o] = y[o * length : (o + 1) * length]
    small_ref[0, 2:3, :] = jnp.sum(da2 * normal, axis=0, keepdims=True)
    small_ref[0, 3:4, :] = jnp.sum(da2, axis=0, keepdims=True)
    dres = g.astype(F32) + norm_back(da2 * gain_two, normal, scale)
    dres_ref[...] = dres
    dbr = dres.astype(BF16)
    grad_out = dot_nn(flip(att_ref[...]), dbr).astype(BF16)
    rows_out = width // groups
    for o in range(groups):
        sources[2][o] = grad_out[o * rows_out : (o + 1) * rows_out]
    out_sum.stage1()
    do_ref[...] = dot_nt(dbr, wout_ref[...]).astype(BF16)
    q_t[...] = flip(q_ref[...])
    do_t[...] = flip(do_ref[...])

    lane = lax.broadcasted_iota(jnp.int32, (tokens, PAIR), 1)
    extra = lax.rem(lane, HD)
    low_half = lane < HD
    swap = (
        (lax.broadcasted_iota(jnp.int32, (PAIR, PAIR), 0) < HD)
        != (lax.broadcasted_iota(jnp.int32, (PAIR, PAIR), 1) < HD)
    ).astype(BF16)

    def prepare(pair, _):
        cols = pl.ds(pl.multiple_of(pair * PAIR, PAIR), PAIR)
        prod = do_ref[:, cols].astype(F32) * att_ref[:, cols].astype(F32)
        prod_hi = prod.astype(BF16)
        prod_lo = (prod - prod_hi.astype(F32)).astype(BF16)
        delta = -(dot_nn(prod_hi, swap) + dot_nn(prod_lo, swap))
        delta_hi = delta.astype(BF16).astype(F32)
        lse = -lse_ref[:, cols]
        lse_hi = lse.astype(BF16).astype(F32)
        lse_mid = (lse - lse_hi).astype(BF16).astype(F32)
        lse_lo = lse - lse_hi - lse_mid
        q_extra = jnp.where(
            extra == HD - 3,
            lse_hi,
            jnp.where(extra == HD - 2, lse_mid, jnp.where(extra == HD - 1, lse_lo, qx_ref[...].astype(F32))),
        ).astype(BF16)
        do_extra = jnp.where(extra == 0, delta_hi, jnp.where(extra == 1, delta - delta_hi, 0.0)).astype(BF16)
        qaug[2 * pair] = jnp.where(low_half, q_ref[:, cols], q_extra)
        qaug[2 * pair + 1] = jnp.where(low_half, q_extra, q_ref[:, cols])
        doaug[2 * pair] = jnp.where(low_half, do_ref[:, cols], do_extra)
        doaug[2 * pair + 1] = jnp.where(low_half, do_extra, do_ref[:, cols])
        return _

    lax.fori_loop(0, H // 2, prepare, 0)
    down.stage2()
    up.stage2()
    out_sum.stage2()
    dd[...] = jnp.zeros_like(dd)
    dq_acc[...] = jnp.zeros_like(dq_acc)
    halo = []

    rounds = len(spans) * (H // 2)
    plan = {}
    for part, action in ((8, lambda: send_back(0)),):
        plan.setdefault(part * rounds // 12, []).append(action)

    def attend(index, chunk, first, count, jobs):
        span = count * QB
        keys = pl.ds(chunk * tokens, tokens)
        fresh = set()

        def body(pair, _):
            for spot in range(H // 2):
                for action in plan.get(index * (H // 2) + spot, ()):
                    pl.when(pair == spot)(action)
            cols = pl.ds(pl.multiple_of(pair * PAIR, PAIR), PAIR)
            k_pair, v_pair, kx = k_ref[keys, cols], v_ref[keys, cols], kx_ref[keys, :]
            for h in range(2):
                mine = low_half if h == 0 else jnp.logical_not(low_half)
                head = 2 * pair + h
                bias[:, :span] = toeplitz(base_ref[pair, h : h + 1, first * QB : (first + count + 1) * QB])
                k_aug = jnp.where(mine, k_pair, kx)
                v_aug = jnp.where(mine, v_pair, jnp.ones_like(v_pair))
                feat = pl.ds(pl.multiple_of(head * HD, HD), HD)
                spot = pl.ds(h * HD, HD)
                fresh.clear()
                dq = [None] * per_chunk
                for kt in range(per_chunk):
                    part = slice(kt * QB, (kt + 1) * QB)
                    dk_t = dv_t = None
                    for b in range(per_chunk):
                        if (kt, b, chunk * per_chunk + kt - b) not in jobs:
                            continue
                        j = chunk * per_chunk + kt - b - first
                        here = pl.ds(b * QB, QB)
                        over = pl.ds(j * QB, QB)
                        p = jnp.exp(dot_nt(qaug[head, here, :], k_aug[part]) + bias[:, over])
                        ds = p * dot_nt(doaug[head, here, :], v_aug[part])
                        ds_low = ds.astype(BF16)
                        more_v = dot_nn(do_t[feat, here], p.astype(BF16))
                        more_k = dot_nn(q_t[feat, here], ds_low)
                        more_q = dot_nn(ds_low, k_pair[part])
                        dv_t = more_v if dv_t is None else dv_t + more_v
                        dk_t = more_k if dk_t is None else dk_t + more_k
                        dq[b] = more_q if dq[b] is None else dq[b] + more_q
                        if j in fresh:
                            dsum[:, over] += ds
                        else:
                            fresh.add(j)
                            dsum[:, over] = ds
                    dkt[spot, part] = dk_t
                    dvt[spot, part] = dv_t
                for b in range(per_chunk):
                    if dq[b] is not None:
                        here = pl.ds(b * QB, QB)
                        dq_acc[here, cols] += jnp.where(mine[:QB], dq[b], 0.0)
                left = jnp.concatenate([jnp.zeros((QB, QB), F32), dsum[:, :span]], axis=1)
                half = QB // 2
                while half:
                    left = left[:half] + pltpu.roll(left[half:], span + QB - half, 1)
                    half //= 2
                dd[pair, h : h + 1, first * QB : (first + count + 1) * QB] += left
            dkv[:, cols] = dkt[...].T.astype(BF16)
            dkv[:, pl.ds(pl.multiple_of(width + pair * PAIR, PAIR), PAIR)] = dvt[...].T.astype(BF16)
            return _

        lax.fori_loop(0, H // 2, body, 0)

    def halo_copy(step):
        return pltpu.make_async_remote_copy(
            src_ref=halo_send.at[(step - 1) % 2], dst_ref=halo_land.at[step - 1],
            send_sem=halo_sems.at[0, step - 1], recv_sem=halo_sems.at[1, step - 1],
            device_id={"seq": lax.rem(seq + splits - 1, splits)}, device_id_type=pl.DeviceIdType.MESH,
        )

    grad_normed = None
    for index, (chunk, first, count, jobs) in enumerate(spans):
        attend(index, chunk, first, count, jobs)
        step = back - chunk
        part = dot_nt(dkv[...], wqkv_ref[:, width:])
        rows_t = first_norm(chunk)
        if step > 0:
            rows_t = jnp.where(seq >= step, rows_t.astype(F32), 0.0)
        rows_t = flip(rows_t)
        if index == 0:
            gkv[...] = dot_nn(rows_t, dkv[...])
        else:
            gkv[...] += dot_nn(rows_t, dkv[...])
        if step == 0:
            dq_low = (dq_acc[...] * (HD**-0.5)).astype(BF16)
            grad_normed = part + dot_nt(dq_low, wqkv_ref[:, :width])
            grads = (dot_nn(rows_t, dq_low).astype(BF16), gkv[:, :width].astype(BF16), gkv[:, width:].astype(BF16))
            for i, grad in enumerate(grads):
                for o in range(groups):
                    sources[3 + i][o] = grad[o * rows_up : (o + 1) * rows_up]
                qkv_sums[i].stage1()
        else:
            if step < back:

                @pl.when((seq + 1 < splits) & (seq >= step))
                def _(step=step):
                    halo_copy(step + 1).wait_recv()

                arrived = jnp.where((seq + 1 < splits) & (seq >= step), halo_land[step].astype(F32), 0.0)
                part = part + arrived
            if step + 2 <= back:

                @pl.when(seq >= step + 2)
                def _(step=step):
                    halo_copy(step + 2).wait_send()

            halo_send[(step - 1) % 2] = part.astype(BF16)

            @pl.when(seq >= step)
            def _(step=step):
                halo_copy(step).start()

            if index == back - 1:
                down.stage3()
    up.stage3()
    out_sum.stage3()
    for summer in qkv_sums:
        summer.stage2()
    wide = (down, up, out_sum)
    for summer in wide:
        summer.turn(1)

    @pl.when(seq + 1 < splits)
    def _():
        halo_copy(1).wait_recv()

    grad_normed = grad_normed + jnp.where(seq + 1 < splits, halo_land[0].astype(F32), 0.0)
    normal, scale = norm_stats(xwin[own_rows, :].astype(F32))
    small_ref[0, 0:1, :] = jnp.sum(grad_normed * normal, axis=0, keepdims=True)
    small_ref[0, 1:2, :] = jnp.sum(grad_normed, axis=0, keepdims=True)
    small_ref[0, 4:8, :] = jnp.zeros((4, width), F32)
    dd_all = dd[...].reshape(H, dd.shape[-1])
    dd_hi = dd_all.astype(BF16)
    dd_mid = (dd_all - dd_hi.astype(F32)).astype(BF16)
    small_ref[0, 8:16, :] = jnp.zeros((8, width), F32)
    small_ref[0, 8:16, :NBK] = dot_nt(dd_hi, hot_ref[...]) + dot_nt(dd_mid, hot_ref[...])
    small = SmallSummer(small_ref, small_land, small_sems)
    small.pair()
    dx = (dres_ref[...] + norm_back(grad_normed * gains_ref[0:1, :], normal, scale)).astype(BF16)
    for o in range(groups):
        slots[1, o] = dx[o * length : (o + 1) * length]
    send_back(1)
    small.take()
    small.plane()
    for turn in range(2, down.rounds + 1):
        for summer in wide:
            summer.turn(turn)
    for summer in qkv_sums:
        summer.stage3()
    small.take()
    small.along()
    for turn in reversed(range(1, down.rounds)):
        for summer in wide:
            summer.turn_back(turn)
    for summer in summers:
        summer.stage4()
    for summer in wide:
        summer.turn_back(0)
    small.take()
    small_out[...] = small_ref[3]
    for summer in summers:
        summer.finish()
    small.finish()
    for which in range(2):
        for step in range(1, groups):
            ret_copy(which, step).wait()
    for gather in gathers:
        gather.finish()
    for copy in few:
        copy.wait_send()
    for step in range(1, back + 1):

        @pl.when((seq + 1 < splits) & (seq + 1 >= step))
        def _(step=step):
            row_copy(step).wait_send()
    for step in range(1, min(back, 2) + 1):

        @pl.when(seq >= step)
        def _(step=step):
            halo_copy(step).wait_send()


def layer(back, tokens_in, cotangent, deal, lengths, buckets, vectors, rel, wqkv, wout, wup, wdown):
    splits, groups = lax.axis_size("seq"), lax.axis_size("dp")
    tokens, width = tokens_in.shape
    length = tokens // groups
    per_chunk = tokens // QB
    maxlen = buckets.shape[0]
    window, reach = (back + 1) * tokens, back * tokens + 2 * QB
    wide = min(2, back) * per_chunk
    span = min(wide + per_chunk - 1, reach // QB - 1) * QB
    grads = [wdown.shape[0], wup.shape[0] * wup.shape[1] // width, *[width // groups] * 4]
    out_shapes, more, sources = [], [], []
    for height in grads:
        shape = (groups, height, width)
        out, scratch = summer_shapes(shape, BF16, splits)
        sources.append(pltpu.VMEM(shape, BF16))
        out_shapes.append(out)
        more += scratch
    out_shapes.append(jax.ShapeDtypeStruct((16, width), F32))
    out_shapes += [jax.ShapeDtypeStruct((groups, length, width), BF16)] * 2
    small_copies = 1 + (groups // 2 - 1) + (splits - 1)
    scratch = sources + more + [
        pltpu.VMEM((4, 16, width), F32),
        pltpu.VMEM((small_copies, 16, width), F32),
        pltpu.SemaphoreType.DMA((2, small_copies)),
        pltpu.VMEM((2, groups, length, width), BF16),
        pltpu.SemaphoreType.DMA((2, 2, groups - 1)),
        pltpu.VMEM((min(back, 2), tokens, width), BF16),
        pltpu.VMEM((back, tokens, width), BF16),
        pltpu.SemaphoreType.DMA((2, back)),
        pltpu.VMEM((tokens, width), F32),
        pltpu.VMEM((tokens, width), BF16),
        pltpu.VMEM((H, tokens, PAIR), BF16),
        pltpu.VMEM((H, tokens, PAIR), BF16),
        pltpu.VMEM((width, tokens), BF16),
        pltpu.VMEM((width, tokens), BF16),
        pltpu.VMEM((QB, span), F32),
        pltpu.VMEM((2 if span <= 1024 else 1, QB, span), F32),
        pltpu.VMEM((wide * QB, PAIR), BF16),
        pltpu.VMEM((wide * QB, PAIR), BF16),
        pltpu.VMEM((H // 2, 2, reach), F32),
        pltpu.VMEM((tokens, width), F32),
        pltpu.VMEM((PAIR, tokens), F32),
        pltpu.VMEM((PAIR, tokens), F32),
        pltpu.VMEM((tokens, 2 * width), BF16),
        pltpu.VMEM((width, 2 * width), F32),
        pltpu.VMEM((window, width), BF16),
        pltpu.VMEM((tokens, width), BF16),
        pltpu.VMEM((width, 3 * width), BF16),
        pltpu.VMEM((width, width), BF16),
        pltpu.VMEM((width, wup.shape[1]), BF16),
        pltpu.VMEM((wup.shape[1], width), BF16),
        pltpu.SemaphoreType.DMA((4, 2, max(8, groups - 1))),
        pltpu.SemaphoreType.DMA((4,)),
        pltpu.SemaphoreType.DMA((2, 2, groups - 1)),
        pltpu.SemaphoreType.DMA((2, back)),
        pltpu.VMEM((groups, 16, PAIR), F32),
        pltpu.SemaphoreType.DMA((2, groups - 1)),
        pltpu.VMEM((8, width), F32),
        pltpu.VMEM((H // 2, 2, reach), F32),
        pltpu.VMEM((tokens, width), BF16),
        pltpu.VMEM((window, width), BF16),
        pltpu.VMEM((window, width), BF16),
        pltpu.VMEM((tokens, width), BF16),
        pltpu.VMEM((tokens, width), F32),
        pltpu.VMEM((16, PAIR), F32),
        pltpu.VMEM((NBK, PAIR), F32),
        pltpu.VMEM((NBK, reach), BF16),
        pltpu.VMEM((tokens, PAIR), BF16),
        pltpu.VMEM((window, PAIR), BF16),
    ]
    vmem, smem = pl.BlockSpec(memory_space=pltpu.VMEM), pl.BlockSpec(memory_space=pltpu.SMEM)
    return pl.pallas_call(
        functools.partial(layer_kernel, back, maxlen),
        in_specs=[vmem] * 2 + [smem] * 2 + [vmem] * (2 + len(vectors)) + [pl.BlockSpec(memory_space=pl.ANY)] * 4,
        out_specs=[vmem] * len(out_shapes),
        out_shape=out_shapes,
        scratch_shapes=scratch,
        compiler_params=pltpu.CompilerParams(collective_id=1, has_side_effects=True, vmem_limit_bytes=VMEM_LIMIT),
        name="layer",
    )(tokens_in, cotangent, deal, lengths, buckets.reshape(-1, PAIR), *vectors, rel, wqkv, wout, wup, wdown)


def finish_kernel(deal_ref, down, up, out, q, k, v, small, ret_out, ret_grad, *outs):
    o_out, o_grad, o_qkv, o_wout, o_up, o_down, *o_vectors, o_rel = outs
    length = ret_out.shape[1]
    for g in range(ret_out.shape[0]):
        piece = deal_ref[0, g]
        o_out[pl.ds(g * length, length), :] = ret_out[piece]
        o_grad[pl.ds(g * length, length), :] = ret_grad[piece]
    def collect(source, rows):
        parts, height, cols = source.shape
        if height == rows:
            return add_low(*[source[t] for t in range(parts)])
        return source[...].reshape(-1, cols).astype(F32)

    width = down.shape[2]
    for source, target in ((down, o_down), (up, o_up), (out, o_wout)):
        height, columns = target.shape[0], target.shape[1] // width
        value = collect(source, height * columns)
        for c in range(columns):
            target[:, c * width : (c + 1) * width] = value[c * height : (c + 1) * height]
    for c, source in enumerate((q, k, v)):
        o_qkv[:, c * width : (c + 1) * width] = collect(source, o_qkv.shape[0])
    dp, groups = lax.axis_index("dp"), lax.axis_size("dp")
    for i, target in enumerate(o_vectors):
        size = target.shape[0]
        value = small[i : i + 1, :size]
        for o in range(1, groups):
            value = jnp.where(dp == o, small[i : i + 1, o * size : (o + 1) * size], value)
        target[...] = value.reshape(size)
    levels = small[8 : 8 + H, :PAIR].T
    size = o_rel.shape[0]
    value = levels[:size, :H]
    for o in range(1, groups):
        value = jnp.where(dp == o, levels[o * size : (o + 1) * size, :H], value)
    o_rel[...] = value


def finish(deal, sums, returned, shapes):
    return pl.pallas_call(
        finish_kernel,
        in_specs=[pl.BlockSpec(memory_space=pltpu.SMEM)] + [pl.BlockSpec(memory_space=pltpu.VMEM)] * 9,
        out_specs=[pl.BlockSpec(memory_space=pltpu.VMEM)] * len(shapes),
        out_shape=shapes,
        compiler_params=pltpu.CompilerParams(vmem_limit_bytes=VMEM_LIMIT),
        name="finish",
    )(deal, *sums, *returned)


def shards(
    tokens,
    cotangent,
    deal,
    lengths,
    buckets,
    ln1_gain,
    ln1_bias,
    w_qkv,
    w_out,
    rel_bias,
    ln2_gain,
    ln2_bias,
    w_up,
    w_down,
):
    tok_dev = tokens.shape[0]
    back = -(-buckets.shape[0] // tok_dev)
    *sums, small_total, back_out, back_grad = layer(
        back, tokens, cotangent, deal, lengths, buckets, (ln1_gain, ln1_bias, ln2_gain, ln2_bias), rel_bias,
        w_qkv, w_out, w_up, w_down,
    )
    output, grad_tokens, total_qkv, total_out, total_up, total_down, g_one, b_one, g_two, b_two, total_rel = finish(
        deal,
        [*sums, small_total],
        [back_out, back_grad],
        [jax.ShapeDtypeStruct(tokens.shape, BF16)] * 2
        + [
            jax.ShapeDtypeStruct(a.shape, F32)
            for a in (w_qkv, w_out, w_up, w_down, ln1_gain, ln1_bias, ln2_gain, ln2_bias, rel_bias)
        ],
    )
    return (
        output, grad_tokens, g_one, b_one, total_qkv, total_out, total_rel, g_two, b_two, total_up, total_down,
    )


def solution(mesh):
    by_all, by_dp = P(("seq", "dp"), None), P("dp", None)
    return jax.shard_map(
        shards,
        mesh=mesh,
        in_specs=(
            by_all, by_all, by_all, by_dp, P(), P("dp"), P("dp"), by_dp, by_dp, by_dp, P("dp"), P("dp"), by_dp, by_dp,
        ),
        out_specs=(by_all, by_all, P("dp"), P("dp"), by_dp, by_dp, by_dp, P("dp"), P("dp"), by_dp, by_dp),
        check_vma=False,
    )
```

```python
import functools

import jax
import jax.numpy as jnp
from jax import lax
from jax.experimental import pallas as pl
from jax.experimental.pallas import tpu as pltpu
from jax.sharding import PartitionSpec as P

H = 8
HD = 64
NBK = 32
QB = 256
PAIR = 2 * HD
BIG = -1e30
F32 = jnp.float32
BF16 = jnp.bfloat16
VMEM_LIMIT = 60 * 1024 * 1024

NT = (((1,), (1,)), ((), ()))
NN = (((1,), (0,)), ((), ()))


def dot_nt(a, b):
    return lax.dot_general(a, b, NT, preferred_element_type=F32)


def dot_nn(a, b):
    return lax.dot_general(a, b, NN, preferred_element_type=F32)


def toeplitz(row):
    width = row.shape[1]
    return pltpu.roll(jnp.broadcast_to(row, (QB, width)), 0, 1, stride=1, stride_axis=0)[:, QB:]


def add_low(first, *others):
    total = first.astype(F32)
    for other in others:
        total = total + other.astype(F32)
    return total


def square(chip):
    return chip + 1 - 2 * lax.rem(chip, 2), chip + 2 - 4 * (chip // 2), 3 - chip


class Summer:
    def __init__(self, source, pair, recv2, mine, recv3, out, sems, halving):
        self.source, self.pair, self.recv2 = source, pair, recv2
        self.mine, self.recv3, self.out, self.sems = mine, recv3, out, sems
        self.dp, self.seq = lax.axis_index("dp"), lax.axis_index("seq")
        self.pairs, self.splits = source.shape[0] // 2, lax.axis_size("seq")
        self.core, self.chip = lax.rem(self.dp, 2), self.dp // 2
        self.rows = out.shape[1]
        self.scatter = self.rows < mine.shape[0]
        self.halving = halving and self.scatter
        self.rounds = (self.splits - 1).bit_length() if self.halving else 1
        self.hops2 = self.pairs - 1

    def copy(self, src, dst, slot, device):
        return pltpu.make_async_remote_copy(
            src_ref=src, dst_ref=dst, send_sem=self.sems.at[0, slot], recv_sem=self.sems.at[1, slot],
            device_id=device, device_id_type=pl.DeviceIdType.MESH,
        )

    def copy1(self, k):
        other = 1 - self.core
        return self.copy(self.source.at[2 * k + other], self.pair.at[k], k, {"dp": self.dp + 1 - 2 * self.core})

    def copy2(self, step):
        k = lax.rem(self.chip + 1 + step, self.pairs)
        return self.copy(self.pair.at[k], self.recv2.at[step], self.pairs + step, {"dp": 2 * k + self.core})

    def copy3(self, step):
        t = lax.rem(self.seq + 1 + step, self.splits)
        src = self.mine.at[pl.ds(pl.multiple_of(t * self.rows, self.rows), self.rows)] if self.scatter else self.mine
        dst = self.recv3.at[step] if self.scatter else self.out.at[self.seq]
        return self.copy(src, dst, self.pairs + self.hops2 + step, {"seq": t})

    def copy4(self, step):
        t = lax.rem(self.seq + 1 + step, self.splits)
        slot = self.pairs + self.hops2 + self.splits - 1 + step
        return self.copy(self.out.at[self.seq], self.out.at[self.seq], slot, {"seq": t})

    def exchange(self, back, turn):
        low, stride = 2**turn, 2 ** (turn + 1)
        bit = lax.rem(self.seq // low, 2)
        partner = self.seq + low - 2 * low * bit
        kept, given = lax.rem(self.seq, stride), lax.rem(partner, stride)
        count = self.splits // stride
        base = self.splits - self.splits // low
        slot = self.pairs + self.hops2 + base + (self.splits - 1 if back else 0)
        moves = []
        for i in range(count):
            mine, theirs = kept + i * stride, given + i * stride
            src = self.out.at[mine] if back else self.mine.at[self.part(theirs)]
            dst = self.out.at[mine] if back else self.recv3.at[base + i]
            moves.append((self.copy(src, dst, slot + i, {"seq": partner}), mine, base + i))
        return moves

    def part(self, t):
        return pl.ds(pl.multiple_of(t * self.rows, self.rows), self.rows)

    def turn(self, turn):
        if not self.halving:
            return
        for copy, kept, slot in self.exchange(False, turn - 1):
            copy.wait_recv()
            self.mine[self.part(kept)] = add_low(self.mine[self.part(kept)], self.recv3[slot]).astype(self.mine.dtype)
        if turn < self.rounds:
            for copy, _, _ in self.exchange(False, turn):
                copy.start()
        else:
            self.out[self.seq] = self.mine[self.part(self.seq)]
            for copy, _, _ in self.exchange(True, turn - 1):
                copy.start()

    def turn_back(self, turn):
        if not self.halving:
            return
        for copy, _, _ in self.exchange(True, turn):
            copy.wait_recv()
        if turn > 0:
            for copy, _, _ in self.exchange(True, turn - 1):
                copy.start()

    def stage1(self, some=None):
        for k in range(self.pairs) if some is None else some:
            self.copy1(k).start()

    def stage2(self):
        for k in range(self.pairs):
            self.copy1(k).wait_recv()
        for step in range(self.pairs):
            k = lax.rem(self.chip + 1 + step, self.pairs)
            self.pair[k] = add_low(self.source[2 * k + self.core], self.pair[k]).astype(self.pair.dtype)
            if step < self.pairs - 1:
                self.copy2(step).start()

    def stage3(self):
        for step in range(self.pairs - 1):
            self.copy2(step).wait_recv()
        total = add_low(self.pair[self.chip], *[self.recv2[step] for step in range(self.pairs - 1)])
        self.mine[...] = total.astype(self.mine.dtype)
        if self.halving:
            for copy, _, _ in self.exchange(False, 0):
                copy.start()
            return
        for step in range(self.splits - 1):
            self.copy3(step).start()
        if not self.scatter:
            self.out[self.seq] = self.mine[...]

    def stage4(self):
        if self.halving:
            return
        for step in range(self.splits - 1):
            self.copy3(step).wait_recv()
        if not self.scatter:
            return
        own = self.mine[pl.ds(pl.multiple_of(self.seq * self.rows, self.rows), self.rows)]
        total = add_low(own, *[self.recv3[step] for step in range(self.splits - 1)])
        self.out[self.seq] = total.astype(self.out.dtype)
        for step in range(self.splits - 1):
            self.copy4(step).start()

    def finish(self):
        for k in range(self.pairs):
            self.copy1(k).wait_send()
        for step in range(self.pairs - 1):
            self.copy2(step).wait_send()
        if self.halving:
            for turn in range(self.rounds):
                for back in (False, True):
                    for copy, _, _ in self.exchange(back, turn):
                        copy.wait_send()
            return
        for step in range(self.splits - 1):
            self.copy3(step).wait_send()
        if self.scatter:
            for step in range(self.splits - 1):
                self.copy4(step).wait()


def summer_shapes(shape, dtype, splits):
    groups, rows, cols = shape
    pairs = groups // 2
    scatter = rows % (16 * splits) == 0
    out = jax.ShapeDtypeStruct((splits, rows // splits if scatter else rows, cols), dtype)
    copies = pairs + (pairs - 1) + (splits - 1) * (2 if scatter else 1)
    scratch = [
        pltpu.VMEM((pairs, rows, cols), dtype),
        pltpu.VMEM((pairs - 1, rows, cols), dtype),
        pltpu.VMEM((rows, cols), dtype),
        pltpu.VMEM((splits - 1, out.shape[1] if scatter else 16, cols), dtype),
        pltpu.SemaphoreType.DMA((2, copies)),
    ]
    return out, scratch


def greet(peers):
    barrier = pltpu.get_barrier_semaphore()
    for device in peers:
        pl.semaphore_signal(barrier, inc=1, device_id=device, device_id_type=pl.DeviceIdType.MESH)
    pl.semaphore_wait(barrier, len(peers))


def others(axis):
    size, me = lax.axis_size(axis), lax.axis_index(axis)
    return [{axis: lax.rem(me + step, size)} for step in range(1, size)]


class SmallSummer:
    def __init__(self, ref, land, sems):
        self.ref, self.land, self.sems = ref, land, sems
        self.dp, self.seq = lax.axis_index("dp"), lax.axis_index("seq")
        self.pairs, self.splits = lax.axis_size("dp") // 2, lax.axis_size("seq")
        self.slot, self.copies, self.sent = 0, [], []

    def send(self, devices):
        self.copies = []
        for device in devices:
            copy = pltpu.make_async_remote_copy(
                src_ref=self.ref.at[len(self.sent)], dst_ref=self.land.at[self.slot],
                send_sem=self.sems.at[0, self.slot], recv_sem=self.sems.at[1, self.slot],
                device_id=device, device_id_type=pl.DeviceIdType.MESH,
            )
            copy.start()
            self.copies.append((self.slot, copy))
            self.slot += 1
        self.sent.append(self.copies)

    def take(self):
        stage = len(self.sent) - 1
        total = self.ref[stage]
        for slot, copy in self.copies:
            copy.wait_recv()
            total = total + self.land[slot]
        self.ref[stage + 1] = total

    def plane(self):
        groups = 2 * self.pairs
        self.send([{"dp": lax.rem(self.dp + step, groups)} for step in range(1, groups)])

    def along(self):
        self.send([{"seq": lax.rem(self.seq + step, self.splits)} for step in range(1, self.splits)])

    def finish(self):
        for copies in self.sent:
            for _, copy in copies:
                copy.wait_send()


def norm_stats(values):
    average = jnp.mean(values, axis=-1, keepdims=True)
    centred = values - average
    scale = lax.rsqrt(jnp.mean(centred * centred, axis=-1, keepdims=True) + 1e-05)
    return centred * scale, scale


def norm_back(grad, normal, scale):
    return scale * (
        grad - jnp.mean(grad, axis=-1, keepdims=True) - normal * jnp.mean(grad * normal, axis=-1, keepdims=True)
    )


def flip(values):
    return values.astype(BF16).T


def phase_spans(back, per_chunk, tiles):
    spans = []
    for chunk in range(back + 1):
        jobs = [
            (kt, b, chunk * per_chunk + kt - b)
            for kt in range(per_chunk)
            for b in range(per_chunk)
            if 0 <= chunk * per_chunk + kt - b < tiles
        ]
        first, last = min(j[2] for j in jobs), max(j[2] for j in jobs)
        spans.append((chunk, first, last - first + 1, jobs))
    return spans


class Gather:
    def __init__(self, shard, full, sems, own_sem):
        self.shard, self.full, self.sems = shard, full, sems
        self.rows = shard.shape[0]
        self.dp = lax.axis_index("dp")
        self.pairs = lax.axis_size("dp") // 2
        self.square = self.pairs == 4
        self.core, self.chip = lax.rem(self.dp, 2), self.dp // 2
        self.sibling = {"dp": self.dp + 1 - 2 * self.core}
        self.own = pltpu.make_async_copy(shard, self.place(self.dp), own_sem)
        if self.square:
            self.around = square(self.chip)
        else:
            self.around = [lax.rem(self.chip + step, self.pairs) for step in range(1, self.pairs)]
            self.behind = [lax.rem(self.chip + self.pairs - step, self.pairs) for step in range(1, self.pairs)]

    def place(self, owner, first=0, rows=None):
        start = pl.multiple_of(owner * self.rows, self.rows)
        return self.full.at[pl.ds(start + first, self.rows if rows is None else rows)]

    def copy(self, src, dst, slot, device):
        return pltpu.make_async_remote_copy(
            src_ref=src, dst_ref=dst, send_sem=self.sems.at[0, slot], recv_sem=self.sems.at[1, slot],
            device_id=device, device_id_type=pl.DeviceIdType.MESH,
        )

    def mate(self, chip):
        return {"dp": 2 * chip + self.core}

    def start(self):
        reach = self.around[:2] if self.square else self.around
        self.sent = [self.copy(self.shard, self.place(self.dp), 1 + i, self.mate(c)) for i, c in enumerate(reach)]
        self.near = self.copy(self.shard, self.place(self.dp), 0, self.sibling)
        for copy in self.sent + [self.near]:
            copy.start()
        self.own.start()
        self.waiting = [self.near]

    def share(self, chip, slot):
        there = self.place(2 * chip + self.core)
        copy = self.copy(there, there, slot, self.sibling)
        copy.start()
        self.waiting.append(copy)
        self.sent.append(copy)

    def relay(self):
        for copy in self.sent:
            copy.wait_recv()
        if not self.square:
            for i, chip in enumerate(self.behind):
                self.share(chip, self.pairs + i)
            return
        across, along, _ = self.around
        half = self.rows // 2
        self.passed = []
        for i, (origin, target) in enumerate(((across, along), (along, across))):
            there = self.place(2 * origin + self.core, i * half, half)
            copy = self.copy(there, there, 3 + i, self.mate(target))
            copy.start()
            self.passed.append(copy)
        self.share(across, 5)
        self.share(along, 6)

    def relay_far(self):
        if not self.square:
            return
        for copy in self.passed:
            copy.wait_recv()
        self.share(self.around[2], 7)
        self.sent += self.passed

    def arrive(self):
        self.own.wait()
        for copy in self.waiting:
            copy.wait_recv()

    def finish(self):
        for copy in self.sent + [self.near]:
            copy.wait_send()


def layer_kernel(back, maxlen, *refs):
    (
        tokens_ref, cotangent_ref, deal_ref, lengths_ref, buckets_ref, *vector_refs, rel_ref,
        wqkv_s, wout_s, wup_s, wdown_s,
    ) = refs[:14]
    *sums, small_out, ret_out, ret_grad = refs[14:23]
    it = iter(refs[23:])
    sources = [next(it) for _ in range(6)]
    summers = [
        Summer(source, *[next(it) for _ in range(4)], out, next(it), halving)
        for source, out, halving in zip(sources, sums, (True, True, True, False, False, False))
    ]
    down, up, out_sum, *qkv_sums = summers
    small_ref, small_land, small_sems = next(it), next(it), next(it)
    slots, ret_sems, halo_send, halo_land, halo_sems = (next(it) for _ in range(5))
    dres_ref, do_ref, qaug, doaug, q_t, do_t = (next(it) for _ in range(6))
    bias, scores, kaug, vaug, dd, dq_acc, dkt, dvt, dkv, gkv = (next(it) for _ in range(10))
    dsum = scores.at[0]
    xwin, g_ref, wqkv_ref, wout_ref, wup_ref, wdown_ref = (next(it) for _ in range(6))
    gather_sems, own_sems, deal_sems, row_sems, few_land, few_sems = (next(it) for _ in range(6))
    gains_ref, base_ref, q_ref, k_ref, v_ref, att_ref, lse_ref = (next(it) for _ in range(7))
    few_mine, rel_all, hot_ref, qx_ref, kx_ref = (next(it) for _ in range(5))
    dp, groups = lax.axis_index("dp"), lax.axis_size("dp")
    seq, splits = lax.axis_index("seq"), lax.axis_size("seq")
    tokens, width = tokens_ref.shape
    length = tokens // groups
    per_chunk = tokens // QB
    tiles = base_ref.shape[-1] // QB - 1
    spans = phase_spans(back, per_chunk, tiles)
    mesh_ids = pl.DeviceIdType.MESH
    greet(others("dp") + others("seq"))

    def deal_out(which, source, target, first_row):
        for j in range(groups):
            piece = source[:length, :]
            for k in range(1, groups):
                piece = jnp.where(deal_ref[0, k] == j, source[k * length : (k + 1) * length, :], piece)
            slots[which, j] = piece
        copies = []
        rows_here = pl.ds(pl.multiple_of(first_row + dp * length, length), length)
        for step in range(1, groups):
            peer = lax.rem(dp + step, groups)
            copy = pltpu.make_async_remote_copy(
                src_ref=slots.at[which, peer], dst_ref=target.at[rows_here],
                send_sem=deal_sems.at[0, which, step - 1], recv_sem=deal_sems.at[1, which, step - 1],
                device_id={"dp": peer}, device_id_type=mesh_ids,
            )
            copy.start()
            copies.append(copy)
        target[rows_here, :] = slots[which, dp]
        return copies

    own_first = back * tokens
    own_rows = pl.ds(own_first, tokens)
    dealt = deal_out(0, tokens_ref, xwin, own_first)
    shard_rows, rel_rows = vector_refs[0].shape[0], rel_ref.shape[0]
    few_mine[...] = jnp.zeros_like(few_mine)
    for i, vector in enumerate(vector_refs):
        few_mine[i : i + 1, :shard_rows] = vector[...].astype(F32).reshape(1, shard_rows)
    few_mine[8 : 8 + rel_rows, :H] = rel_ref[...].astype(F32)
    few = []
    for step in range(1, groups):
        copy = pltpu.make_async_remote_copy(
            src_ref=few_mine, dst_ref=few_land.at[dp],
            send_sem=few_sems.at[0, step - 1], recv_sem=few_sems.at[1, step - 1],
            device_id={"dp": lax.rem(dp + step, groups)}, device_id_type=mesh_ids,
        )
        copy.start()
        few.append(copy)
    few_land[dp] = few_mine[...]
    gathers = [
        Gather(shard, full, gather_sems.at[i], own_sems.at[i])
        for i, (shard, full) in enumerate(
            ((wqkv_s, wqkv_ref), (wout_s, wout_ref), (wup_s, wup_ref), (wdown_s, wdown_ref))
        )
    ]
    gathers[0].start()
    gathers[1].start()

    seqs = lengths_ref.shape[1]

    def segments(rows, first_pos):
        place = lax.broadcasted_iota(jnp.int32, (rows, PAIR), 0) + first_pos
        found, end = jnp.zeros((rows, PAIR), jnp.int32), 0
        for c in range(seqs):
            end = end + lengths_ref[0, c]
            found = found + (place >= end).astype(jnp.int32)
        return jnp.where(place < 0, seqs, found)

    window = kx_ref.shape[0]
    lane_w = lax.rem(lax.broadcasted_iota(jnp.int32, (window, PAIR), 1), HD)
    key_seg = segments(window, (seq - back) * tokens)
    kx_ref[...] = jnp.where((lane_w == key_seg) | (lane_w >= HD - 3), 1.0, 0.0).astype(BF16)
    lane_q = lane_w[:tokens]
    qx_ref[...] = jnp.where((lane_q <= seqs) & (lane_q != segments(tokens, seq * tokens)), BIG, 0.0).astype(BF16)

    level = lax.broadcasted_iota(jnp.int32, (NBK, PAIR), 0)
    below, up_to = jnp.zeros((NBK, PAIR), F32), jnp.zeros((NBK, PAIR), F32)
    for r in range(buckets_ref.shape[0]):
        row = buckets_ref[r : r + 1, :]
        below = below + (row < level).astype(F32)
        up_to = up_to + (row <= level).astype(F32)
    below = jnp.sum(below, axis=1, keepdims=True)
    up_to = jnp.sum(up_to, axis=1, keepdims=True)
    far = (back * tokens + QB - lax.broadcasted_iota(jnp.int32, hot_ref.shape, 1)).astype(F32)
    hot_ref[...] = jnp.where((far >= below) & (far < up_to), 1.0, 0.0).astype(BF16)
    for copy in dealt:
        copy.wait_recv()

    def row_copy(step):
        return pltpu.make_async_remote_copy(
            src_ref=xwin.at[pl.ds((back - step + 1) * tokens, tokens)],
            dst_ref=xwin.at[pl.ds((back - step) * tokens, tokens)],
            send_sem=row_sems.at[0, step - 1], recv_sem=row_sems.at[1, step - 1],
            device_id={"seq": lax.rem(seq + 1, splits)}, device_id_type=mesh_ids,
        )

    def row_send(step):
        @pl.when((seq + 1 < splits) & (seq + 1 >= step))
        def _():
            row_copy(step).start()

    def row_wait(step):
        @pl.when(seq >= step)
        def _():
            row_copy(step).wait_recv()

    row_send(1)
    for copy in few:
        copy.wait_recv()
    per_tile = PAIR // shard_rows
    for i in range(width // PAIR):
        tile = few_land[i * per_tile, :8, :]
        for o in range(1, per_tile):
            tile = tile + pltpu.roll(few_land[i * per_tile + o, :8, :], o * shard_rows, 1)
        gains_ref[:, i * PAIR : (i + 1) * PAIR] = tile
    for o in range(groups):
        rel_all[o * rel_rows : (o + 1) * rel_rows, :] = few_land[o, 8 : 8 + rel_rows, :]
    table = dot_nn(flip(rel_all[...])[:H], hot_ref[...])
    far = back * tokens + QB - lax.broadcasted_iota(jnp.int32, table.shape, 1)
    base_ref[...] = jnp.where((far >= 0) & (far < maxlen), table, BIG).reshape(base_ref.shape)

    def first_norm(chunk):
        normal, _ = norm_stats(xwin[chunk * tokens : (chunk + 1) * tokens, :].astype(F32))
        return (normal * gains_ref[0:1, :] + gains_ref[1:2, :]).astype(BF16)

    own_normed = first_norm(back)
    gathers[0].relay()
    gathers[2].start()
    gathers[3].start()
    gathers[0].relay_far()
    gathers[0].arrive()
    q_ref[...] = (dot_nn(own_normed, wqkv_ref[:, :width])).astype(BF16) * jnp.asarray(HD**-0.5, BF16)
    k_ref[own_rows, :] = dot_nn(own_normed, wqkv_ref[:, width : 2 * width]).astype(BF16)
    v_ref[own_rows, :] = dot_nn(own_normed, wqkv_ref[:, 2 * width :]).astype(BF16)

    low_tile = lax.broadcasted_iota(jnp.int32, (QB, PAIR), 1) < HD

    def look(low, high, started, last):
        jobs = [(kt, b, kt - b) for kt in range(low, high) for b in range(per_chunk) if 0 <= kt - b < tiles]
        first = min(j for _, _, j in jobs)
        span = (max(j for _, _, j in jobs) + 1 - first) * QB
        keys = pl.ds(low * QB, (high - low) * QB)
        jobs = [(kt - low, b, j) for kt, b, j in jobs]

        def body(pair, _):
            cols = pl.ds(pl.multiple_of(pair * PAIR, PAIR), PAIR)
            k_pair, v_pair, kx = k_ref[keys, cols], v_ref[keys, cols], kx_ref[keys, :]
            low_k = lax.broadcasted_iota(jnp.int32, k_pair.shape, 1) < HD
            for h in range(2):
                mine_k = low_k if h == 0 else jnp.logical_not(low_k)
                mine = low_tile if h == 0 else jnp.logical_not(low_tile)
                bias[:, :span] = toeplitz(base_ref[pair, h : h + 1, first * QB : first * QB + span + QB])
                kaug[: (high - low) * QB] = jnp.where(mine_k, k_pair, kx)
                vaug[: (high - low) * QB] = jnp.where(mine_k, v_pair, jnp.ones_like(v_pair))
                held = pl.ds(pl.multiple_of((2 * pair + h) * PAIR, PAIR), PAIR)
                for b in range(per_chunk):
                    here = pl.ds(b * QB, QB)
                    q_aug = jnp.where(mine, q_ref[here, cols], qx_ref[here, :])
                    work = [(pl.ds(kt * QB, QB), pl.ds((j - first) * QB, QB)) for kt, block, j in jobs if block == b]
                    top = None
                    for part, over in work:
                        score = dot_nt(q_aug, kaug[part, :]) + bias[:, over]
                        scores[b % scores.shape[0], :, over] = score
                        most = jnp.maximum(score[:, :128], score[:, 128:])
                        top = most if top is None else jnp.maximum(top, most)
                    top = jnp.max(top, axis=1, keepdims=True)
                    acc = None
                    if started:
                        lane_at = HD if h == 0 else 0
                        before = lse_ref[here, cols][:, lane_at : lane_at + 1]
                        top = jnp.maximum(top, before)
                        acc = gkv[here, held] * jnp.exp(before - top)
                    for part, over in work:
                        p = jnp.exp(scores[b % scores.shape[0], :, over] - top).astype(BF16)
                        more = dot_nn(p, vaug[part, :])
                        acc = more if acc is None else acc + more
                    if last:
                        value = (acc / pltpu.roll(acc, HD, 1)).astype(BF16)
                        att_ref[here, cols] = value if h == 0 else jnp.where(mine, value, att_ref[here, cols])
                        stat = top + jnp.log(acc)
                    else:
                        gkv[here, held] = acc
                        stat = jnp.broadcast_to(top, (QB, PAIR))
                    lse_ref[here, cols] = jnp.where(mine, lse_ref[here, cols], stat)
            return _

        lax.fori_loop(0, H // 2, body, 0)

    def keys_of(chunk):
        normed = jnp.where(seq >= back - chunk, first_norm(chunk).astype(F32), 0.0).astype(BF16)
        here = pl.ds(chunk * tokens, tokens)
        k_ref[here, :] = dot_nn(normed, wqkv_ref[:, width : 2 * width]).astype(BF16)
        v_ref[here, :] = dot_nn(normed, wqkv_ref[:, 2 * width :]).astype(BF16)

    for step in range(1, back):
        row_wait(step)
        row_send(step + 1)
        if step == 1:
            gathers[1].relay()
            gathers[2].relay()
            dealt_grad = deal_out(1, cotangent_ref, g_ref, 0)
        keys_of(back - step)
        if step % 2:
            high = (back - step + 2) * per_chunk
            look((back - step) * per_chunk, high, step > 1, False)
    gathers[3].relay()
    gathers[1].relay_far()
    gathers[2].relay_far()
    row_wait(back)
    keys_of(0)
    look(0, per_chunk, True, True)
    gathers[3].relay_far()
    for gather in gathers[1:]:
        gather.arrive()
    for copy in dealt_grad:
        copy.wait_recv()
    for copy in dealt + dealt_grad:
        copy.wait_send()

    def ret_copy(which, step):
        peer = lax.rem(dp + step, groups)
        return pltpu.make_async_remote_copy(
            src_ref=slots.at[which, peer], dst_ref=(ret_out, ret_grad)[which].at[dp],
            send_sem=ret_sems.at[0, which, step - 1], recv_sem=ret_sems.at[1, which, step - 1],
            device_id={"dp": peer}, device_id_type=mesh_ids,
        )

    def send_back(which):
        for step in range(1, groups):
            ret_copy(which, step).start()
        (ret_out, ret_grad)[which][dp] = slots[which, dp]

    resid = xwin[own_rows, :].astype(F32) + dot_nn(att_ref[...], wout_ref[...])
    normal, scale = norm_stats(resid)
    gain_two = gains_ref[2:3, :]
    a2 = (normal * gain_two + gains_ref[3:4, :]).astype(BF16)
    a2_t = flip(a2)
    g = g_ref[...]
    y = resid
    da2 = jnp.zeros((tokens, width), F32)
    rows_up, rows_down = width // groups, wdown_ref.shape[0] // groups
    for c in range(wdown_ref.shape[0] // width):
        cols = pl.ds(c * width, width)
        upper = dot_nn(a2, wup_ref[:, cols])
        phi = 0.5 + 0.5 * lax.erf(upper * (0.5**0.5))
        act = (upper * phi).astype(BF16)
        y = y + dot_nn(act, wdown_ref[cols, :])
        slope = phi + upper * (jnp.exp(-0.5 * upper * upper) * 0.3989422804014327)
        dup = (dot_nt(g, wdown_ref[cols, :]) * slope).astype(BF16)
        da2 = da2 + dot_nt(dup, wup_ref[:, cols])
        grad_down = dot_nn(flip(act), g).astype(BF16)
        for o in range(width // rows_down):
            sources[0][c * (width // rows_down) + o] = grad_down[o * rows_down : (o + 1) * rows_down]
        per_step = width // rows_down // 2
        down.stage1(range(c * per_step, (c + 1) * per_step))
        grad_up = dot_nn(a2_t, dup).astype(BF16)
        for o in range(groups):
            sources[1][o, c * rows_up : (c + 1) * rows_up] = grad_up[o * rows_up : (o + 1) * rows_up]
    up.stage1()
    y = y.astype(BF16)
    for o in range(groups):
        slots[0, o] = y[o * length : (o + 1) * length]
    small_ref[0, 2:3, :] = jnp.sum(da2 * normal, axis=0, keepdims=True)
    small_ref[0, 3:4, :] = jnp.sum(da2, axis=0, keepdims=True)
    dres = g.astype(F32) + norm_back(da2 * gain_two, normal, scale)
    dres_ref[...] = dres
    dbr = dres.astype(BF16)
    grad_out = dot_nn(flip(att_ref[...]), dbr).astype(BF16)
    rows_out = width // groups
    for o in range(groups):
        sources[2][o] = grad_out[o * rows_out : (o + 1) * rows_out]
    out_sum.stage1()
    do_ref[...] = dot_nt(dbr, wout_ref[...]).astype(BF16)
    q_t[...] = flip(q_ref[...])
    do_t[...] = flip(do_ref[...])

    lane = lax.broadcasted_iota(jnp.int32, (tokens, PAIR), 1)
    extra = lax.rem(lane, HD)
    low_half = lane < HD
    swap = (
        (lax.broadcasted_iota(jnp.int32, (PAIR, PAIR), 0) < HD)
        != (lax.broadcasted_iota(jnp.int32, (PAIR, PAIR), 1) < HD)
    ).astype(BF16)

    def prepare(pair, _):
        cols = pl.ds(pl.multiple_of(pair * PAIR, PAIR), PAIR)
        prod = do_ref[:, cols].astype(F32) * att_ref[:, cols].astype(F32)
        prod_hi = prod.astype(BF16)
        prod_lo = (prod - prod_hi.astype(F32)).astype(BF16)
        delta = -(dot_nn(prod_hi, swap) + dot_nn(prod_lo, swap))
        delta_hi = delta.astype(BF16).astype(F32)
        lse = -lse_ref[:, cols]
        lse_hi = lse.astype(BF16).astype(F32)
        lse_mid = (lse - lse_hi).astype(BF16).astype(F32)
        lse_lo = lse - lse_hi - lse_mid
        q_extra = jnp.where(
            extra == HD - 3,
            lse_hi,
            jnp.where(extra == HD - 2, lse_mid, jnp.where(extra == HD - 1, lse_lo, qx_ref[...].astype(F32))),
        ).astype(BF16)
        do_extra = jnp.where(extra == 0, delta_hi, jnp.where(extra == 1, delta - delta_hi, 0.0)).astype(BF16)
        qaug[2 * pair] = jnp.where(low_half, q_ref[:, cols], q_extra)
        qaug[2 * pair + 1] = jnp.where(low_half, q_extra, q_ref[:, cols])
        doaug[2 * pair] = jnp.where(low_half, do_ref[:, cols], do_extra)
        doaug[2 * pair + 1] = jnp.where(low_half, do_extra, do_ref[:, cols])
        return _

    lax.fori_loop(0, H // 2, prepare, 0)
    down.stage2()
    up.stage2()
    out_sum.stage2()
    dd[...] = jnp.zeros_like(dd)
    dq_acc[...] = jnp.zeros_like(dq_acc)
    halo = []

    rounds = len(spans) * (H // 2)
    plan = {}
    for part, action in ((8, lambda: send_back(0)),):
        plan.setdefault(part * rounds // 12, []).append(action)

    def attend(index, chunk, first, count, jobs):
        span = count * QB
        keys = pl.ds(chunk * tokens, tokens)
        fresh = set()

        def body(pair, _):
            for spot in range(H // 2):
                for action in plan.get(index * (H // 2) + spot, ()):
                    pl.when(pair == spot)(action)
            cols = pl.ds(pl.multiple_of(pair * PAIR, PAIR), PAIR)
            k_pair, v_pair, kx = k_ref[keys, cols], v_ref[keys, cols], kx_ref[keys, :]
            for h in range(2):
                mine = low_half if h == 0 else jnp.logical_not(low_half)
                head = 2 * pair + h
                bias[:, :span] = toeplitz(base_ref[pair, h : h + 1, first * QB : (first + count + 1) * QB])
                k_aug = jnp.where(mine, k_pair, kx)
                v_aug = jnp.where(mine, v_pair, jnp.ones_like(v_pair))
                feat = pl.ds(pl.multiple_of(head * HD, HD), HD)
                spot = pl.ds(h * HD, HD)
                fresh.clear()
                dq = [None] * per_chunk
                for kt in range(per_chunk):
                    part = slice(kt * QB, (kt + 1) * QB)
                    dk_t = dv_t = None
                    for b in range(per_chunk):
                        if (kt, b, chunk * per_chunk + kt - b) not in jobs:
                            continue
                        j = chunk * per_chunk + kt - b - first
                        here = pl.ds(b * QB, QB)
                        over = pl.ds(j * QB, QB)
                        p = jnp.exp(dot_nt(qaug[head, here, :], k_aug[part]) + bias[:, over])
                        ds = p * dot_nt(doaug[head, here, :], v_aug[part])
                        ds_low = ds.astype(BF16)
                        more_v = dot_nn(do_t[feat, here], p.astype(BF16))
                        more_k = dot_nn(q_t[feat, here], ds_low)
                        more_q = dot_nn(ds_low, k_pair[part])
                        dv_t = more_v if dv_t is None else dv_t + more_v
                        dk_t = more_k if dk_t is None else dk_t + more_k
                        dq[b] = more_q if dq[b] is None else dq[b] + more_q
                        if j in fresh:
                            dsum[:, over] += ds
                        else:
                            fresh.add(j)
                            dsum[:, over] = ds
                    dkt[spot, part] = dk_t
                    dvt[spot, part] = dv_t
                for b in range(per_chunk):
                    if dq[b] is not None:
                        here = pl.ds(b * QB, QB)
                        dq_acc[here, cols] += jnp.where(mine[:QB], dq[b], 0.0)
                left = jnp.concatenate([jnp.zeros((QB, QB), F32), dsum[:, :span]], axis=1)
                half = QB // 2
                while half:
                    left = left[:half] + pltpu.roll(left[half:], span + QB - half, 1)
                    half //= 2
                dd[pair, h : h + 1, first * QB : (first + count + 1) * QB] += left
            dkv[:, cols] = dkt[...].astype(BF16).T
            dkv[:, pl.ds(pl.multiple_of(width + pair * PAIR, PAIR), PAIR)] = dvt[...].astype(BF16).T
            return _

        lax.fori_loop(0, H // 2, body, 0)

    def halo_copy(step):
        return pltpu.make_async_remote_copy(
            src_ref=halo_send.at[(step - 1) % 2], dst_ref=halo_land.at[step - 1],
            send_sem=halo_sems.at[0, step - 1], recv_sem=halo_sems.at[1, step - 1],
            device_id={"seq": lax.rem(seq + splits - 1, splits)}, device_id_type=pl.DeviceIdType.MESH,
        )

    grad_normed = None
    for index, (chunk, first, count, jobs) in enumerate(spans):
        attend(index, chunk, first, count, jobs)
        step = back - chunk
        part = dot_nt(dkv[...], wqkv_ref[:, width:])
        rows_t = first_norm(chunk)
        if step > 0:
            rows_t = jnp.where(seq >= step, rows_t.astype(F32), 0.0)
        rows_t = flip(rows_t)
        if index == 0:
            gkv[...] = dot_nn(rows_t, dkv[...])
        else:
            gkv[...] += dot_nn(rows_t, dkv[...])
        if step == 0:
            dq_low = (dq_acc[...] * (HD**-0.5)).astype(BF16)
            grad_normed = part + dot_nt(dq_low, wqkv_ref[:, :width])
            grads = (dot_nn(rows_t, dq_low).astype(BF16), gkv[:, :width].astype(BF16), gkv[:, width:].astype(BF16))
            for i, grad in enumerate(grads):
                for o in range(groups):
                    sources[3 + i][o] = grad[o * rows_up : (o + 1) * rows_up]
                qkv_sums[i].stage1()
        else:
            if step < back:

                @pl.when((seq + 1 < splits) & (seq >= step))
                def _(step=step):
                    halo_copy(step + 1).wait_recv()

                arrived = jnp.where((seq + 1 < splits) & (seq >= step), halo_land[step].astype(F32), 0.0)
                part = part + arrived
            if step + 2 <= back:

                @pl.when(seq >= step + 2)
                def _(step=step):
                    halo_copy(step + 2).wait_send()

            halo_send[(step - 1) % 2] = part.astype(BF16)

            @pl.when(seq >= step)
            def _(step=step):
                halo_copy(step).start()

            if index == back - 1:
                down.stage3()
    up.stage3()
    out_sum.stage3()
    for summer in qkv_sums:
        summer.stage2()
    wide = (down, up, out_sum)
    for summer in wide:
        summer.turn(1)

    @pl.when(seq + 1 < splits)
    def _():
        halo_copy(1).wait_recv()

    grad_normed = grad_normed + jnp.where(seq + 1 < splits, halo_land[0].astype(F32), 0.0)
    normal, scale = norm_stats(xwin[own_rows, :].astype(F32))
    small_ref[0, 0:1, :] = jnp.sum(grad_normed * normal, axis=0, keepdims=True)
    small_ref[0, 1:2, :] = jnp.sum(grad_normed, axis=0, keepdims=True)
    small_ref[0, 4:8, :] = jnp.zeros((4, width), F32)
    dd_all = dd[...].reshape(H, dd.shape[-1])
    dd_hi = dd_all.astype(BF16)
    dd_mid = (dd_all - dd_hi.astype(F32)).astype(BF16)
    small_ref[0, 8:16, :] = jnp.zeros((8, width), F32)
    small_ref[0, 8:16, :NBK] = dot_nt(dd_hi, hot_ref[...]) + dot_nt(dd_mid, hot_ref[...])
    small = SmallSummer(small_ref, small_land, small_sems)
    small.plane()
    dx = (dres_ref[...] + norm_back(grad_normed * gains_ref[0:1, :], normal, scale)).astype(BF16)
    for o in range(groups):
        slots[1, o] = dx[o * length : (o + 1) * length]
    send_back(1)
    for turn in range(2, down.rounds + 1):
        for summer in wide:
            summer.turn(turn)
    for summer in qkv_sums:
        summer.stage3()
    small.take()
    small.along()
    for turn in reversed(range(1, down.rounds)):
        for summer in wide:
            summer.turn_back(turn)
    for summer in summers:
        summer.stage4()
    for summer in wide:
        summer.turn_back(0)
    small.take()
    small_out[...] = small_ref[2]
    for summer in summers:
        summer.finish()
    small.finish()
    for which in range(2):
        for step in range(1, groups):
            ret_copy(which, step).wait()
    for gather in gathers:
        gather.finish()
    for copy in few:
        copy.wait_send()
    for step in range(1, back + 1):

        @pl.when((seq + 1 < splits) & (seq + 1 >= step))
        def _(step=step):
            row_copy(step).wait_send()
    for step in range(1, min(back, 2) + 1):

        @pl.when(seq >= step)
        def _(step=step):
            halo_copy(step).wait_send()


def layer(back, tokens_in, cotangent, deal, lengths, buckets, vectors, rel, wqkv, wout, wup, wdown):
    splits, groups = lax.axis_size("seq"), lax.axis_size("dp")
    tokens, width = tokens_in.shape
    length = tokens // groups
    per_chunk = tokens // QB
    maxlen = buckets.shape[0]
    window, reach = (back + 1) * tokens, back * tokens + 2 * QB
    wide = min(2, back) * per_chunk
    span = min(wide + per_chunk - 1, reach // QB - 1) * QB
    grads = [wdown.shape[0], wup.shape[0] * wup.shape[1] // width, *[width // groups] * 4]
    out_shapes, more, sources = [], [], []
    for height in grads:
        shape = (groups, height, width)
        out, scratch = summer_shapes(shape, BF16, splits)
        sources.append(pltpu.VMEM(shape, BF16))
        out_shapes.append(out)
        more += scratch
    out_shapes.append(jax.ShapeDtypeStruct((16, width), F32))
    out_shapes += [jax.ShapeDtypeStruct((groups, length, width), BF16)] * 2
    small_copies = (groups - 1) + (splits - 1)
    scratch = sources + more + [
        pltpu.VMEM((4, 16, width), F32),
        pltpu.VMEM((small_copies, 16, width), F32),
        pltpu.SemaphoreType.DMA((2, small_copies)),
        pltpu.VMEM((2, groups, length, width), BF16),
        pltpu.SemaphoreType.DMA((2, 2, groups - 1)),
        pltpu.VMEM((min(back, 2), tokens, width), BF16),
        pltpu.VMEM((back, tokens, width), BF16),
        pltpu.SemaphoreType.DMA((2, back)),
        pltpu.VMEM((tokens, width), F32),
        pltpu.VMEM((tokens, width), BF16),
        pltpu.VMEM((H, tokens, PAIR), BF16),
        pltpu.VMEM((H, tokens, PAIR), BF16),
        pltpu.VMEM((width, tokens), BF16),
        pltpu.VMEM((width, tokens), BF16),
        pltpu.VMEM((QB, span), F32),
        pltpu.VMEM((2 if span <= 1024 else 1, QB, span), F32),
        pltpu.VMEM((wide * QB, PAIR), BF16),
        pltpu.VMEM((wide * QB, PAIR), BF16),
        pltpu.VMEM((H // 2, 2, reach), F32),
        pltpu.VMEM((tokens, width), F32),
        pltpu.VMEM((PAIR, tokens), F32),
        pltpu.VMEM((PAIR, tokens), F32),
        pltpu.VMEM((tokens, 2 * width), BF16),
        pltpu.VMEM((width, 2 * width), F32),
        pltpu.VMEM((window, width), BF16),
        pltpu.VMEM((tokens, width), BF16),
        pltpu.VMEM((width, 3 * width), BF16),
        pltpu.VMEM((width, width), BF16),
        pltpu.VMEM((width, wup.shape[1]), BF16),
        pltpu.VMEM((wup.shape[1], width), BF16),
        pltpu.SemaphoreType.DMA((4, 2, max(8, groups - 1))),
        pltpu.SemaphoreType.DMA((4,)),
        pltpu.SemaphoreType.DMA((2, 2, groups - 1)),
        pltpu.SemaphoreType.DMA((2, back)),
        pltpu.VMEM((groups, 16, PAIR), F32),
        pltpu.SemaphoreType.DMA((2, groups - 1)),
        pltpu.VMEM((8, width), F32),
        pltpu.VMEM((H // 2, 2, reach), F32),
        pltpu.VMEM((tokens, width), BF16),
        pltpu.VMEM((window, width), BF16),
        pltpu.VMEM((window, width), BF16),
        pltpu.VMEM((tokens, width), BF16),
        pltpu.VMEM((tokens, width), F32),
        pltpu.VMEM((16, PAIR), F32),
        pltpu.VMEM((NBK, PAIR), F32),
        pltpu.VMEM((NBK, reach), BF16),
        pltpu.VMEM((tokens, PAIR), BF16),
        pltpu.VMEM((window, PAIR), BF16),
    ]
    vmem, smem = pl.BlockSpec(memory_space=pltpu.VMEM), pl.BlockSpec(memory_space=pltpu.SMEM)
    return pl.pallas_call(
        functools.partial(layer_kernel, back, maxlen),
        in_specs=[vmem] * 2 + [smem] * 2 + [vmem] * (2 + len(vectors)) + [pl.BlockSpec(memory_space=pl.ANY)] * 4,
        out_specs=[vmem] * len(out_shapes),
        out_shape=out_shapes,
        scratch_shapes=scratch,
        compiler_params=pltpu.CompilerParams(collective_id=1, has_side_effects=True, vmem_limit_bytes=VMEM_LIMIT),
        name="layer",
    )(tokens_in, cotangent, deal, lengths, buckets.reshape(-1, PAIR), *vectors, rel, wqkv, wout, wup, wdown)


def finish_kernel(deal_ref, down, up, out, q, k, v, small, ret_out, ret_grad, *outs):
    o_out, o_grad, o_qkv, o_wout, o_up, o_down, *o_vectors, o_rel = outs
    length = ret_out.shape[1]
    for g in range(ret_out.shape[0]):
        piece = deal_ref[0, g]
        o_out[pl.ds(g * length, length), :] = ret_out[piece]
        o_grad[pl.ds(g * length, length), :] = ret_grad[piece]
    def collect(source, rows):
        parts, height, cols = source.shape
        if height == rows:
            return add_low(*[source[t] for t in range(parts)])
        return source[...].reshape(-1, cols).astype(F32)

    width = down.shape[2]
    for source, target in ((down, o_down), (up, o_up), (out, o_wout)):
        height, columns = target.shape[0], target.shape[1] // width
        value = collect(source, height * columns)
        for c in range(columns):
            target[:, c * width : (c + 1) * width] = value[c * height : (c + 1) * height]
    for c, source in enumerate((q, k, v)):
        o_qkv[:, c * width : (c + 1) * width] = collect(source, o_qkv.shape[0])
    dp, groups = lax.axis_index("dp"), lax.axis_size("dp")
    for i, target in enumerate(o_vectors):
        size = target.shape[0]
        value = small[i : i + 1, :size]
        for o in range(1, groups):
            value = jnp.where(dp == o, small[i : i + 1, o * size : (o + 1) * size], value)
        target[...] = value.reshape(size)
    levels = small[8 : 8 + H, :PAIR].T
    size = o_rel.shape[0]
    value = levels[:size, :H]
    for o in range(1, groups):
        value = jnp.where(dp == o, levels[o * size : (o + 1) * size, :H], value)
    o_rel[...] = value


def finish(deal, sums, returned, shapes):
    return pl.pallas_call(
        finish_kernel,
        in_specs=[pl.BlockSpec(memory_space=pltpu.SMEM)] + [pl.BlockSpec(memory_space=pltpu.VMEM)] * 9,
        out_specs=[pl.BlockSpec(memory_space=pltpu.VMEM)] * len(shapes),
        out_shape=shapes,
        compiler_params=pltpu.CompilerParams(vmem_limit_bytes=VMEM_LIMIT),
        name="finish",
    )(deal, *sums, *returned)


def shards(
    tokens,
    cotangent,
    deal,
    lengths,
    buckets,
    ln1_gain,
    ln1_bias,
    w_qkv,
    w_out,
    rel_bias,
    ln2_gain,
    ln2_bias,
    w_up,
    w_down,
):
    tok_dev = tokens.shape[0]
    back = -(-buckets.shape[0] // tok_dev)
    *sums, small_total, back_out, back_grad = layer(
        back, tokens, cotangent, deal, lengths, buckets, (ln1_gain, ln1_bias, ln2_gain, ln2_bias), rel_bias,
        w_qkv, w_out, w_up, w_down,
    )
    output, grad_tokens, total_qkv, total_out, total_up, total_down, g_one, b_one, g_two, b_two, total_rel = finish(
        deal,
        [*sums, small_total],
        [back_out, back_grad],
        [jax.ShapeDtypeStruct(tokens.shape, BF16)] * 2
        + [
            jax.ShapeDtypeStruct(a.shape, F32)
            for a in (w_qkv, w_out, w_up, w_down, ln1_gain, ln1_bias, ln2_gain, ln2_bias, rel_bias)
        ],
    )
    return (
        output, grad_tokens, g_one, b_one, total_qkv, total_out, total_rel, g_two, b_two, total_up, total_down,
    )


def solution(mesh):
    by_all, by_dp = P(("seq", "dp"), None), P("dp", None)
    return jax.shard_map(
        shards,
        mesh=mesh,
        in_specs=(
            by_all, by_all, by_all, by_dp, P(), P("dp"), P("dp"), by_dp, by_dp, by_dp, P("dp"), P("dp"), by_dp, by_dp,
        ),
        out_specs=(by_all, by_all, P("dp"), P("dp"), by_dp, by_dp, by_dp, P("dp"), P("dp"), by_dp, by_dp),
        check_vma=False,
    )
```

```python
import functools

import jax
import jax.numpy as jnp
from jax import lax
from jax.experimental import pallas as pl
from jax.experimental.pallas import tpu as pltpu
from jax.sharding import PartitionSpec as P

H = 8
HD = 64
NBK = 32
QB = 256
PAIR = 2 * HD
BIG = -1e30
F32 = jnp.float32
BF16 = jnp.bfloat16
VMEM_LIMIT = 60 * 1024 * 1024

NT = (((1,), (1,)), ((), ()))
NN = (((1,), (0,)), ((), ()))


def dot_nt(a, b):
    return lax.dot_general(a, b, NT, preferred_element_type=F32)


def dot_nn(a, b):
    return lax.dot_general(a, b, NN, preferred_element_type=F32)


def toeplitz(row):
    width = row.shape[1]
    return pltpu.roll(jnp.broadcast_to(row, (QB, width)), 0, 1, stride=1, stride_axis=0)[:, QB:]


def add_low(first, *others):
    total = first.astype(F32)
    for other in others:
        total = total + other.astype(F32)
    return total


def square(chip):
    return chip + 1 - 2 * lax.rem(chip, 2), chip + 2 - 4 * (chip // 2), 3 - chip


class Summer:
    def __init__(self, source, pair, recv2, mine, recv3, out, sems, halving):
        self.source, self.pair, self.recv2 = source, pair, recv2
        self.mine, self.recv3, self.out, self.sems = mine, recv3, out, sems
        self.dp, self.seq = lax.axis_index("dp"), lax.axis_index("seq")
        self.pairs, self.splits = source.shape[0] // 2, lax.axis_size("seq")
        self.core, self.chip = lax.rem(self.dp, 2), self.dp // 2
        self.rows = out.shape[1]
        self.scatter = self.rows < mine.shape[0]
        self.halving = halving and self.scatter
        self.rounds = (self.splits - 1).bit_length() if self.halving else 1
        self.hops2 = self.pairs - 1

    def copy(self, src, dst, slot, device):
        return pltpu.make_async_remote_copy(
            src_ref=src, dst_ref=dst, send_sem=self.sems.at[0, slot], recv_sem=self.sems.at[1, slot],
            device_id=device, device_id_type=pl.DeviceIdType.MESH,
        )

    def copy1(self, k):
        other = 1 - self.core
        return self.copy(self.source.at[2 * k + other], self.pair.at[k], k, {"dp": self.dp + 1 - 2 * self.core})

    def copy2(self, step):
        k = lax.rem(self.chip + 1 + step, self.pairs)
        return self.copy(self.pair.at[k], self.recv2.at[step], self.pairs + step, {"dp": 2 * k + self.core})

    def copy3(self, step):
        t = lax.rem(self.seq + 1 + step, self.splits)
        src = self.mine.at[pl.ds(pl.multiple_of(t * self.rows, self.rows), self.rows)] if self.scatter else self.mine
        dst = self.recv3.at[step] if self.scatter else self.out.at[self.seq]
        return self.copy(src, dst, self.pairs + self.hops2 + step, {"seq": t})

    def copy4(self, step):
        t = lax.rem(self.seq + 1 + step, self.splits)
        slot = self.pairs + self.hops2 + self.splits - 1 + step
        return self.copy(self.out.at[self.seq], self.out.at[self.seq], slot, {"seq": t})

    def exchange(self, back, turn):
        low, stride = 2**turn, 2 ** (turn + 1)
        bit = lax.rem(self.seq // low, 2)
        partner = self.seq + low - 2 * low * bit
        kept, given = lax.rem(self.seq, stride), lax.rem(partner, stride)
        count = self.splits // stride
        base = self.splits - self.splits // low
        slot = self.pairs + self.hops2 + base + (self.splits - 1 if back else 0)
        moves = []
        for i in range(count):
            mine, theirs = kept + i * stride, given + i * stride
            src = self.out.at[mine] if back else self.mine.at[self.part(theirs)]
            dst = self.out.at[mine] if back else self.recv3.at[base + i]
            moves.append((self.copy(src, dst, slot + i, {"seq": partner}), mine, base + i))
        return moves

    def part(self, t):
        return pl.ds(pl.multiple_of(t * self.rows, self.rows), self.rows)

    def turn(self, turn):
        if not self.halving:
            return
        for copy, kept, slot in self.exchange(False, turn - 1):
            copy.wait_recv()
            self.mine[self.part(kept)] = add_low(self.mine[self.part(kept)], self.recv3[slot]).astype(self.mine.dtype)
        if turn < self.rounds:
            for copy, _, _ in self.exchange(False, turn):
                copy.start()
        else:
            self.out[self.seq] = self.mine[self.part(self.seq)]
            for copy, _, _ in self.exchange(True, turn - 1):
                copy.start()

    def turn_back(self, turn):
        if not self.halving:
            return
        for copy, _, _ in self.exchange(True, turn):
            copy.wait_recv()
        if turn > 0:
            for copy, _, _ in self.exchange(True, turn - 1):
                copy.start()

    def stage1(self, some=None):
        for k in range(self.pairs) if some is None else some:
            self.copy1(k).start()

    def stage2(self):
        for k in range(self.pairs):
            self.copy1(k).wait_recv()
        for step in range(self.pairs):
            k = lax.rem(self.chip + 1 + step, self.pairs)
            self.pair[k] = add_low(self.source[2 * k + self.core], self.pair[k]).astype(self.pair.dtype)
            if step < self.pairs - 1:
                self.copy2(step).start()

    def stage3(self):
        for step in range(self.pairs - 1):
            self.copy2(step).wait_recv()
        total = add_low(self.pair[self.chip], *[self.recv2[step] for step in range(self.pairs - 1)])
        self.mine[...] = total.astype(self.mine.dtype)
        if self.halving:
            for copy, _, _ in self.exchange(False, 0):
                copy.start()
            return
        for step in range(self.splits - 1):
            self.copy3(step).start()
        if not self.scatter:
            self.out[self.seq] = self.mine[...]

    def stage4(self):
        if self.halving:
            return
        for step in range(self.splits - 1):
            self.copy3(step).wait_recv()
        if not self.scatter:
            return
        own = self.mine[pl.ds(pl.multiple_of(self.seq * self.rows, self.rows), self.rows)]
        total = add_low(own, *[self.recv3[step] for step in range(self.splits - 1)])
        self.out[self.seq] = total.astype(self.out.dtype)
        for step in range(self.splits - 1):
            self.copy4(step).start()

    def finish(self):
        for k in range(self.pairs):
            self.copy1(k).wait_send()
        for step in range(self.pairs - 1):
            self.copy2(step).wait_send()
        if self.halving:
            for turn in range(self.rounds):
                for back in (False, True):
                    for copy, _, _ in self.exchange(back, turn):
                        copy.wait_send()
            return
        for step in range(self.splits - 1):
            self.copy3(step).wait_send()
        if self.scatter:
            for step in range(self.splits - 1):
                self.copy4(step).wait()


def summer_shapes(shape, dtype, splits):
    groups, rows, cols = shape
    pairs = groups // 2
    scatter = rows % (16 * splits) == 0
    out = jax.ShapeDtypeStruct((splits, rows // splits if scatter else rows, cols), dtype)
    copies = pairs + (pairs - 1) + (splits - 1) * (2 if scatter else 1)
    scratch = [
        pltpu.VMEM((pairs, rows, cols), dtype),
        pltpu.VMEM((pairs - 1, rows, cols), dtype),
        pltpu.VMEM((rows, cols), dtype),
        pltpu.VMEM((splits - 1, out.shape[1] if scatter else 16, cols), dtype),
        pltpu.SemaphoreType.DMA((2, copies)),
    ]
    return out, scratch


def greet(peers):
    barrier = pltpu.get_barrier_semaphore()
    for device in peers:
        pl.semaphore_signal(barrier, inc=1, device_id=device, device_id_type=pl.DeviceIdType.MESH)
    pl.semaphore_wait(barrier, len(peers))


def others(axis):
    size, me = lax.axis_size(axis), lax.axis_index(axis)
    return [{axis: lax.rem(me + step, size)} for step in range(1, size)]


class SmallSummer:
    def __init__(self, ref, land, sems):
        self.ref, self.land, self.sems = ref, land, sems
        self.dp, self.seq = lax.axis_index("dp"), lax.axis_index("seq")
        self.pairs, self.splits = lax.axis_size("dp") // 2, lax.axis_size("seq")
        self.slot, self.copies, self.sent = 0, [], []

    def send(self, devices):
        self.copies = []
        for device in devices:
            copy = pltpu.make_async_remote_copy(
                src_ref=self.ref.at[len(self.sent)], dst_ref=self.land.at[self.slot],
                send_sem=self.sems.at[0, self.slot], recv_sem=self.sems.at[1, self.slot],
                device_id=device, device_id_type=pl.DeviceIdType.MESH,
            )
            copy.start()
            self.copies.append((self.slot, copy))
            self.slot += 1
        self.sent.append(self.copies)

    def take(self):
        stage = len(self.sent) - 1
        total = self.ref[stage]
        for slot, copy in self.copies:
            copy.wait_recv()
            total = total + self.land[slot]
        self.ref[stage + 1] = total

    def plane(self):
        groups = 2 * self.pairs
        self.send([{"dp": lax.rem(self.dp + step, groups)} for step in range(1, groups)])

    def along(self):
        self.send([{"seq": lax.rem(self.seq + step, self.splits)} for step in range(1, self.splits)])

    def finish(self):
        for copies in self.sent:
            for _, copy in copies:
                copy.wait_send()


def norm_stats(values):
    average = jnp.mean(values, axis=-1, keepdims=True)
    centred = values - average
    scale = lax.rsqrt(jnp.mean(centred * centred, axis=-1, keepdims=True) + 1e-05)
    return centred * scale, scale


def norm_back(grad, normal, scale):
    return scale * (
        grad - jnp.mean(grad, axis=-1, keepdims=True) - normal * jnp.mean(grad * normal, axis=-1, keepdims=True)
    )


def flip(values):
    return values.astype(BF16).T


def phase_spans(back, per_chunk, tiles):
    spans = []
    for chunk in range(back + 1):
        jobs = [
            (kt, b, chunk * per_chunk + kt - b)
            for kt in range(per_chunk)
            for b in range(per_chunk)
            if 0 <= chunk * per_chunk + kt - b < tiles
        ]
        first, last = min(j[2] for j in jobs), max(j[2] for j in jobs)
        spans.append((chunk, first, last - first + 1, jobs))
    return spans


class Gather:
    def __init__(self, shard, full, sems, own_sem):
        self.shard, self.full, self.sems = shard, full, sems
        self.rows = shard.shape[0]
        self.dp = lax.axis_index("dp")
        self.pairs = lax.axis_size("dp") // 2
        self.square = self.pairs == 4
        self.core, self.chip = lax.rem(self.dp, 2), self.dp // 2
        self.sibling = {"dp": self.dp + 1 - 2 * self.core}
        self.own = pltpu.make_async_copy(shard, self.place(self.dp), own_sem)
        if self.square:
            self.around = square(self.chip)
        else:
            self.around = [lax.rem(self.chip + step, self.pairs) for step in range(1, self.pairs)]
            self.behind = [lax.rem(self.chip + self.pairs - step, self.pairs) for step in range(1, self.pairs)]

    def place(self, owner, first=0, rows=None):
        start = pl.multiple_of(owner * self.rows, self.rows)
        return self.full.at[pl.ds(start + first, self.rows if rows is None else rows)]

    def copy(self, src, dst, slot, device):
        return pltpu.make_async_remote_copy(
            src_ref=src, dst_ref=dst, send_sem=self.sems.at[0, slot], recv_sem=self.sems.at[1, slot],
            device_id=device, device_id_type=pl.DeviceIdType.MESH,
        )

    def mate(self, chip):
        return {"dp": 2 * chip + self.core}

    def start(self):
        reach = self.around[:2] if self.square else self.around
        self.sent = [self.copy(self.shard, self.place(self.dp), 1 + i, self.mate(c)) for i, c in enumerate(reach)]
        self.near = self.copy(self.shard, self.place(self.dp), 0, self.sibling)
        for copy in self.sent + [self.near]:
            copy.start()
        self.own.start()
        self.waiting = [self.near]

    def share(self, chip, slot):
        there = self.place(2 * chip + self.core)
        copy = self.copy(there, there, slot, self.sibling)
        copy.start()
        self.waiting.append(copy)
        self.sent.append(copy)

    def relay(self):
        for copy in self.sent:
            copy.wait_recv()
        if not self.square:
            for i, chip in enumerate(self.behind):
                self.share(chip, self.pairs + i)
            return
        across, along, _ = self.around
        half = self.rows // 2
        self.passed = []
        for i, (origin, target) in enumerate(((across, along), (along, across))):
            there = self.place(2 * origin + self.core, i * half, half)
            copy = self.copy(there, there, 3 + i, self.mate(target))
            copy.start()
            self.passed.append(copy)
        self.share(across, 5)
        self.share(along, 6)

    def relay_far(self):
        if not self.square:
            return
        for copy in self.passed:
            copy.wait_recv()
        self.share(self.around[2], 7)
        self.sent += self.passed

    def arrive(self):
        self.own.wait()
        for copy in self.waiting:
            copy.wait_recv()

    def finish(self):
        for copy in self.sent + [self.near]:
            copy.wait_send()


def layer_kernel(back, maxlen, *refs):
    (
        tokens_ref, cotangent_ref, deal_ref, lengths_ref, buckets_ref, *vector_refs, rel_ref,
        wqkv_s, wout_s, wup_s, wdown_s,
    ) = refs[:14]
    *sums, small_out, ret_out, ret_grad = refs[14:23]
    it = iter(refs[23:])
    sources = [next(it) for _ in range(6)]
    summers = [
        Summer(source, *[next(it) for _ in range(4)], out, next(it), halving)
        for source, out, halving in zip(sources, sums, (True, True, True, False, False, False))
    ]
    down, up, out_sum, *qkv_sums = summers
    small_ref, small_land, small_sems = next(it), next(it), next(it)
    slots, ret_sems, ret_own_sems, halo_send, halo_land, halo_sems = (next(it) for _ in range(6))
    dres_ref, do_ref, qaug, doaug, q_t, do_t = (next(it) for _ in range(6))
    bias, scores, kaug, vaug, dd, dq_acc, dkt, dvt, dkv, gkv = (next(it) for _ in range(10))
    dsum = scores.at[0]
    xwin, g_ref, wqkv_ref, wout_ref, wup_ref, wdown_ref = (next(it) for _ in range(6))
    gather_sems, own_sems, deal_sems, row_sems, piece_sems, few_land, few_sems = (next(it) for _ in range(7))
    gains_ref, base_ref, q_ref, k_ref, v_ref, att_ref, lse_ref = (next(it) for _ in range(7))
    few_mine, rel_all, hot_ref, qx_ref, kx_ref = (next(it) for _ in range(5))
    dp, groups = lax.axis_index("dp"), lax.axis_size("dp")
    seq, splits = lax.axis_index("seq"), lax.axis_size("seq")
    tokens, width = tokens_ref.shape
    length = tokens // groups
    per_chunk = tokens // QB
    tiles = base_ref.shape[-1] // QB - 1
    spans = phase_spans(back, per_chunk, tiles)
    mesh_ids = pl.DeviceIdType.MESH
    greet(others("dp") + others("seq"))

    def deal_out(which, source, target, first_row):
        for j in range(groups):
            piece = source[:length, :]
            for k in range(1, groups):
                piece = jnp.where(deal_ref[0, k] == j, source[k * length : (k + 1) * length, :], piece)
            slots[which, j] = piece
        copies = []
        rows_here = pl.ds(pl.multiple_of(first_row + dp * length, length), length)
        for step in range(1, groups):
            peer = lax.rem(dp + step, groups)
            copy = pltpu.make_async_remote_copy(
                src_ref=slots.at[which, peer], dst_ref=target.at[rows_here],
                send_sem=deal_sems.at[0, which, step - 1], recv_sem=deal_sems.at[1, which, step - 1],
                device_id={"dp": peer}, device_id_type=mesh_ids,
            )
            copy.start()
            copies.append(copy)
        target[rows_here, :] = slots[which, dp]
        return copies

    own_first = back * tokens
    own_rows = pl.ds(own_first, tokens)
    gathers = [
        Gather(shard, full, gather_sems.at[i], own_sems.at[i])
        for i, (shard, full) in enumerate(
            ((wqkv_s, wqkv_ref), (wout_s, wout_ref), (wup_s, wup_ref), (wdown_s, wdown_ref))
        )
    ]
    gathers[0].start()
    dealt = deal_out(0, tokens_ref, xwin, own_first)
    shard_rows, rel_rows = vector_refs[0].shape[0], rel_ref.shape[0]
    few_mine[...] = jnp.zeros_like(few_mine)
    for i, vector in enumerate(vector_refs):
        few_mine[i : i + 1, :shard_rows] = vector[...].astype(F32).reshape(1, shard_rows)
    few_mine[8 : 8 + rel_rows, :H] = rel_ref[...].astype(F32)
    few = []
    for step in range(1, groups):
        copy = pltpu.make_async_remote_copy(
            src_ref=few_mine, dst_ref=few_land.at[dp],
            send_sem=few_sems.at[0, step - 1], recv_sem=few_sems.at[1, step - 1],
            device_id={"dp": lax.rem(dp + step, groups)}, device_id_type=mesh_ids,
        )
        copy.start()
        few.append(copy)
    few_land[dp] = few_mine[...]
    gathers[1].start()

    seqs = lengths_ref.shape[1]

    def segments(rows, first_pos):
        place = lax.broadcasted_iota(jnp.int32, (rows, PAIR), 0) + first_pos
        found, end = jnp.zeros((rows, PAIR), jnp.int32), 0
        for c in range(seqs):
            end = end + lengths_ref[0, c]
            found = found + (place >= end).astype(jnp.int32)
        return jnp.where(place < 0, seqs, found)

    window = kx_ref.shape[0]
    lane_w = lax.rem(lax.broadcasted_iota(jnp.int32, (window, PAIR), 1), HD)
    key_seg = segments(window, (seq - back) * tokens)
    kx_ref[...] = jnp.where((lane_w == key_seg) | (lane_w >= HD - 3), 1.0, 0.0).astype(BF16)
    lane_q = lane_w[:tokens]
    qx_ref[...] = jnp.where((lane_q <= seqs) & (lane_q != segments(tokens, seq * tokens)), BIG, 0.0).astype(BF16)

    level = lax.broadcasted_iota(jnp.int32, (NBK, PAIR), 0)
    below, up_to = jnp.zeros((NBK, PAIR), F32), jnp.zeros((NBK, PAIR), F32)
    for r in range(buckets_ref.shape[0]):
        row = buckets_ref[r : r + 1, :]
        below = below + (row < level).astype(F32)
        up_to = up_to + (row <= level).astype(F32)
    below = jnp.sum(below, axis=1, keepdims=True)
    up_to = jnp.sum(up_to, axis=1, keepdims=True)
    far = (back * tokens + QB - lax.broadcasted_iota(jnp.int32, hot_ref.shape, 1)).astype(F32)
    hot_ref[...] = jnp.where((far >= below) & (far < up_to), 1.0, 0.0).astype(BF16)

    def row_copy(step):
        return pltpu.make_async_remote_copy(
            src_ref=xwin.at[pl.ds((back - step + 1) * tokens, tokens)],
            dst_ref=xwin.at[pl.ds((back - step) * tokens, tokens)],
            send_sem=row_sems.at[0, step - 1], recv_sem=row_sems.at[1, step - 1],
            device_id={"seq": lax.rem(seq + 1, splits)}, device_id_type=mesh_ids,
        )

    def piece_copy(step):
        first = lax.rem(dp + groups - step, groups) * length
        return pltpu.make_async_remote_copy(
            src_ref=xwin.at[pl.ds(pl.multiple_of(own_first + first, length), length)],
            dst_ref=xwin.at[pl.ds(pl.multiple_of(own_first - tokens + first, length), length)],
            send_sem=piece_sems.at[0, step], recv_sem=piece_sems.at[1, step],
            device_id={"seq": lax.rem(seq + 1, splits)}, device_id_type=mesh_ids,
        )

    def row_send(step):
        @pl.when((seq + 1 < splits) & (seq + 1 >= step))
        def _():
            row_copy(step).start()

    def row_wait(step):
        @pl.when(seq >= step)
        def _():
            if step > 1:
                row_copy(step).wait_recv()
                return
            for piece in range(groups):
                piece_copy(piece).wait_recv()

    for step in range(groups):
        if step > 0:
            dealt[step - 1].wait_recv()
        pl.when(seq + 1 < splits)(piece_copy(step).start)
    for copy in few:
        copy.wait_recv()
    per_tile = PAIR // shard_rows
    for i in range(width // PAIR):
        tile = few_land[i * per_tile, :8, :]
        for o in range(1, per_tile):
            tile = tile + pltpu.roll(few_land[i * per_tile + o, :8, :], o * shard_rows, 1)
        gains_ref[:, i * PAIR : (i + 1) * PAIR] = tile
    for o in range(groups):
        rel_all[o * rel_rows : (o + 1) * rel_rows, :] = few_land[o, 8 : 8 + rel_rows, :]
    table = dot_nn(flip(rel_all[...])[:H], hot_ref[...])
    far = back * tokens + QB - lax.broadcasted_iota(jnp.int32, table.shape, 1)
    base_ref[...] = jnp.where((far >= 0) & (far < maxlen), table, BIG).reshape(base_ref.shape)

    def first_norm(chunk):
        normal, _ = norm_stats(xwin[chunk * tokens : (chunk + 1) * tokens, :].astype(F32))
        return (normal * gains_ref[0:1, :] + gains_ref[1:2, :]).astype(BF16)

    own_normed = first_norm(back)
    gathers[0].relay()
    gathers[2].start()
    gathers[3].start()
    row_wait(1)
    if back > 1:
        row_send(2)
    gathers[0].relay_far()
    gathers[0].arrive()
    q_ref[...] = (dot_nn(own_normed, wqkv_ref[:, :width])).astype(BF16) * jnp.asarray(HD**-0.5, BF16)
    k_ref[own_rows, :] = dot_nn(own_normed, wqkv_ref[:, width : 2 * width]).astype(BF16)
    v_ref[own_rows, :] = dot_nn(own_normed, wqkv_ref[:, 2 * width :]).astype(BF16)

    low_tile = lax.broadcasted_iota(jnp.int32, (QB, PAIR), 1) < HD

    def look(low, high, started, last):
        jobs = [(kt, b, kt - b) for kt in range(low, high) for b in range(per_chunk) if 0 <= kt - b < tiles]
        first = min(j for _, _, j in jobs)
        span = (max(j for _, _, j in jobs) + 1 - first) * QB
        keys = pl.ds(low * QB, (high - low) * QB)
        jobs = [(kt - low, b, j) for kt, b, j in jobs]

        def body(pair, _):
            cols = pl.ds(pl.multiple_of(pair * PAIR, PAIR), PAIR)
            k_pair, v_pair, kx = k_ref[keys, cols], v_ref[keys, cols], kx_ref[keys, :]
            low_k = lax.broadcasted_iota(jnp.int32, k_pair.shape, 1) < HD
            for h in range(2):
                mine_k = low_k if h == 0 else jnp.logical_not(low_k)
                mine = low_tile if h == 0 else jnp.logical_not(low_tile)
                bias[:, :span] = toeplitz(base_ref[pair, h : h + 1, first * QB : first * QB + span + QB])
                kaug[: (high - low) * QB] = jnp.where(mine_k, k_pair, kx)
                vaug[: (high - low) * QB] = jnp.where(mine_k, v_pair, jnp.ones_like(v_pair))
                held = pl.ds(pl.multiple_of((2 * pair + h) * PAIR, PAIR), PAIR)
                for b in range(per_chunk):
                    here = pl.ds(b * QB, QB)
                    q_aug = jnp.where(mine, q_ref[here, cols], qx_ref[here, :])
                    work = [(pl.ds(kt * QB, QB), pl.ds((j - first) * QB, QB)) for kt, block, j in jobs if block == b]
                    top = None
                    for part, over in work:
                        score = dot_nt(q_aug, kaug[part, :]) + bias[:, over]
                        scores[b % scores.shape[0], :, over] = score
                        most = jnp.maximum(score[:, :128], score[:, 128:])
                        top = most if top is None else jnp.maximum(top, most)
                    top = jnp.max(top, axis=1, keepdims=True)
                    acc = None
                    if started:
                        lane_at = HD if h == 0 else 0
                        before = lse_ref[here, cols][:, lane_at : lane_at + 1]
                        top = jnp.maximum(top, before)
                        acc = gkv[here, held] * jnp.exp(before - top)
                    for part, over in work:
                        p = jnp.exp(scores[b % scores.shape[0], :, over] - top).astype(BF16)
                        more = dot_nn(p, vaug[part, :])
                        acc = more if acc is None else acc + more
                    if last:
                        value = (acc / pltpu.roll(acc, HD, 1)).astype(BF16)
                        att_ref[here, cols] = value if h == 0 else jnp.where(mine, value, att_ref[here, cols])
                        stat = top + jnp.log(acc)
                    else:
                        gkv[here, held] = acc
                        stat = jnp.broadcast_to(top, (QB, PAIR))
                    lse_ref[here, cols] = jnp.where(mine, lse_ref[here, cols], stat)
            return _

        lax.fori_loop(0, H // 2, body, 0)

    def keys_of(chunk):
        normed = jnp.where(seq >= back - chunk, first_norm(chunk).astype(F32), 0.0).astype(BF16)
        here = pl.ds(chunk * tokens, tokens)
        k_ref[here, :] = dot_nn(normed, wqkv_ref[:, width : 2 * width]).astype(BF16)
        v_ref[here, :] = dot_nn(normed, wqkv_ref[:, 2 * width :]).astype(BF16)

    for step in range(1, back):
        if step > 1:
            row_wait(step)
            row_send(step + 1)
        else:
            gathers[1].relay()
            gathers[2].relay()
            dealt_grad = deal_out(1, cotangent_ref, g_ref, 0)
        keys_of(back - step)
        if step % 2:
            high = (back - step + 2) * per_chunk
            look((back - step) * per_chunk, high, step > 1, False)
    gathers[3].relay()
    gathers[1].relay_far()
    gathers[2].relay_far()
    if back > 1:
        row_wait(back)
    keys_of(0)
    look(0, per_chunk, True, True)
    gathers[3].relay_far()
    for gather in gathers[1:]:
        gather.arrive()
    for copy in dealt_grad:
        copy.wait_recv()
    for copy in dealt + dealt_grad:
        copy.wait_send()

    def ret_copy(which, step):
        peer = lax.rem(dp + step, groups)
        return pltpu.make_async_remote_copy(
            src_ref=slots.at[which, peer], dst_ref=(ret_out, ret_grad)[which].at[dp],
            send_sem=ret_sems.at[0, which, step - 1], recv_sem=ret_sems.at[1, which, step - 1],
            device_id={"dp": peer}, device_id_type=mesh_ids,
        )

    def ret_own(which):
        return pltpu.make_async_copy(slots.at[which, dp], (ret_out, ret_grad)[which].at[dp], ret_own_sems.at[which])

    def send_back(which):
        for step in range(1, groups):
            ret_copy(which, step).start()
        ret_own(which).start()

    resid = xwin[own_rows, :].astype(F32) + dot_nn(att_ref[...], wout_ref[...])
    normal, scale = norm_stats(resid)
    gain_two = gains_ref[2:3, :]
    a2 = (normal * gain_two + gains_ref[3:4, :]).astype(BF16)
    a2_t = flip(a2)
    g = g_ref[...]
    y = resid
    da2 = jnp.zeros((tokens, width), F32)
    rows_up, rows_down = width // groups, wdown_ref.shape[0] // groups
    for c in range(wdown_ref.shape[0] // width):
        cols = pl.ds(c * width, width)
        upper = dot_nn(a2, wup_ref[:, cols])
        phi = 0.5 + 0.5 * lax.erf(upper * (0.5**0.5))
        act = (upper * phi).astype(BF16)
        y = y + dot_nn(act, wdown_ref[cols, :])
        slope = phi + upper * (jnp.exp(-0.5 * upper * upper) * 0.3989422804014327)
        dup = (dot_nt(g, wdown_ref[cols, :]) * slope).astype(BF16)
        da2 = da2 + dot_nt(dup, wup_ref[:, cols])
        grad_down = dot_nn(flip(act), g).astype(BF16)
        for o in range(width // rows_down):
            sources[0][c * (width // rows_down) + o] = grad_down[o * rows_down : (o + 1) * rows_down]
        per_step = width // rows_down // 2
        down.stage1(range(c * per_step, (c + 1) * per_step))
        grad_up = dot_nn(a2_t, dup).astype(BF16)
        for o in range(groups):
            sources[1][o, c * rows_up : (c + 1) * rows_up] = grad_up[o * rows_up : (o + 1) * rows_up]
    up.stage1()
    y = y.astype(BF16)
    for o in range(groups):
        slots[0, o] = y[o * length : (o + 1) * length]
    small_ref[0, 2:3, :] = jnp.sum(da2 * normal, axis=0, keepdims=True)
    small_ref[0, 3:4, :] = jnp.sum(da2, axis=0, keepdims=True)
    dres = g.astype(F32) + norm_back(da2 * gain_two, normal, scale)
    dres_ref[...] = dres
    dbr = dres.astype(BF16)
    grad_out = dot_nn(flip(att_ref[...]), dbr).astype(BF16)
    rows_out = width // groups
    for o in range(groups):
        sources[2][o] = grad_out[o * rows_out : (o + 1) * rows_out]
    out_sum.stage1()
    do_ref[...] = dot_nt(dbr, wout_ref[...]).astype(BF16)
    q_t[...] = flip(q_ref[...])
    do_t[...] = flip(do_ref[...])

    lane = lax.broadcasted_iota(jnp.int32, (tokens, PAIR), 1)
    extra = lax.rem(lane, HD)
    low_half = lane < HD
    swap = (
        (lax.broadcasted_iota(jnp.int32, (PAIR, PAIR), 0) < HD)
        != (lax.broadcasted_iota(jnp.int32, (PAIR, PAIR), 1) < HD)
    ).astype(BF16)

    def prepare(pair, _):
        cols = pl.ds(pl.multiple_of(pair * PAIR, PAIR), PAIR)
        prod = do_ref[:, cols].astype(F32) * att_ref[:, cols].astype(F32)
        prod_hi = prod.astype(BF16)
        prod_lo = (prod - prod_hi.astype(F32)).astype(BF16)
        delta = -(dot_nn(prod_hi, swap) + dot_nn(prod_lo, swap))
        delta_hi = delta.astype(BF16).astype(F32)
        lse = -lse_ref[:, cols]
        lse_hi = lse.astype(BF16).astype(F32)
        lse_mid = (lse - lse_hi).astype(BF16).astype(F32)
        lse_lo = lse - lse_hi - lse_mid
        q_extra = jnp.where(
            extra == HD - 3,
            lse_hi,
            jnp.where(extra == HD - 2, lse_mid, jnp.where(extra == HD - 1, lse_lo, qx_ref[...].astype(F32))),
        ).astype(BF16)
        do_extra = jnp.where(extra == 0, delta_hi, jnp.where(extra == 1, delta - delta_hi, 0.0)).astype(BF16)
        qaug[2 * pair] = jnp.where(low_half, q_ref[:, cols], q_extra)
        qaug[2 * pair + 1] = jnp.where(low_half, q_extra, q_ref[:, cols])
        doaug[2 * pair] = jnp.where(low_half, do_ref[:, cols], do_extra)
        doaug[2 * pair + 1] = jnp.where(low_half, do_extra, do_ref[:, cols])
        return _

    lax.fori_loop(0, H // 2, prepare, 0)
    down.stage2()
    up.stage2()
    out_sum.stage2()
    dd[...] = jnp.zeros_like(dd)
    dq_acc[...] = jnp.zeros_like(dq_acc)
    halo = []

    rounds = len(spans) * (H // 2)
    plan = {}
    for part, action in ((8, lambda: send_back(0)),):
        plan.setdefault(part * rounds // 12, []).append(action)

    def attend(index, chunk, first, count, jobs):
        span = count * QB
        keys = pl.ds(chunk * tokens, tokens)
        fresh = set()

        def body(pair, _):
            for spot in range(H // 2):
                for action in plan.get(index * (H // 2) + spot, ()):
                    pl.when(pair == spot)(action)
            cols = pl.ds(pl.multiple_of(pair * PAIR, PAIR), PAIR)
            k_pair, v_pair, kx = k_ref[keys, cols], v_ref[keys, cols], kx_ref[keys, :]
            for h in range(2):
                mine = low_half if h == 0 else jnp.logical_not(low_half)
                head = 2 * pair + h
                bias[:, :span] = toeplitz(base_ref[pair, h : h + 1, first * QB : (first + count + 1) * QB])
                k_aug = jnp.where(mine, k_pair, kx)
                v_aug = jnp.where(mine, v_pair, jnp.ones_like(v_pair))
                feat = pl.ds(pl.multiple_of(head * HD, HD), HD)
                spot = pl.ds(h * HD, HD)
                fresh.clear()
                dq = [None] * per_chunk
                for kt in range(per_chunk):
                    part = slice(kt * QB, (kt + 1) * QB)
                    dk_t = dv_t = None
                    for b in range(per_chunk):
                        if (kt, b, chunk * per_chunk + kt - b) not in jobs:
                            continue
                        j = chunk * per_chunk + kt - b - first
                        here = pl.ds(b * QB, QB)
                        over = pl.ds(j * QB, QB)
                        p = jnp.exp(dot_nt(qaug[head, here, :], k_aug[part]) + bias[:, over])
                        ds = p * dot_nt(doaug[head, here, :], v_aug[part])
                        ds_low = ds.astype(BF16)
                        more_v = dot_nn(do_t[feat, here], p.astype(BF16))
                        more_k = dot_nn(q_t[feat, here], ds_low)
                        more_q = dot_nn(ds_low, k_pair[part])
                        dv_t = more_v if dv_t is None else dv_t + more_v
                        dk_t = more_k if dk_t is None else dk_t + more_k
                        dq[b] = more_q if dq[b] is None else dq[b] + more_q
                        if j in fresh:
                            dsum[:, over] += ds
                        else:
                            fresh.add(j)
                            dsum[:, over] = ds
                    dkt[spot, part] = dk_t
                    dvt[spot, part] = dv_t
                for b in range(per_chunk):
                    if dq[b] is not None:
                        here = pl.ds(b * QB, QB)
                        dq_acc[here, cols] += jnp.where(mine[:QB], dq[b], 0.0)
                left = jnp.concatenate([jnp.zeros((QB, QB), F32), dsum[:, :span]], axis=1)
                half = QB // 2
                while half:
                    left = left[:half] + pltpu.roll(left[half:], span + QB - half, 1)
                    half //= 2
                dd[pair, h : h + 1, first * QB : (first + count + 1) * QB] += left
            dkv[:, cols] = dkt[...].astype(BF16).T
            dkv[:, pl.ds(pl.multiple_of(width + pair * PAIR, PAIR), PAIR)] = dvt[...].astype(BF16).T
            return _

        lax.fori_loop(0, H // 2, body, 0)

    def halo_copy(step):
        return pltpu.make_async_remote_copy(
            src_ref=halo_send.at[(step - 1) % 2], dst_ref=halo_land.at[step - 1],
            send_sem=halo_sems.at[0, step - 1], recv_sem=halo_sems.at[1, step - 1],
            device_id={"seq": lax.rem(seq + splits - 1, splits)}, device_id_type=pl.DeviceIdType.MESH,
        )

    grad_normed = None
    for index, (chunk, first, count, jobs) in enumerate(spans):
        attend(index, chunk, first, count, jobs)
        step = back - chunk
        part = dot_nt(dkv[...], wqkv_ref[:, width:])
        rows_t = first_norm(chunk)
        if step > 0:
            rows_t = jnp.where(seq >= step, rows_t.astype(F32), 0.0)
        rows_t = flip(rows_t)
        if index == 0:
            gkv[...] = dot_nn(rows_t, dkv[...])
        else:
            gkv[...] += dot_nn(rows_t, dkv[...])
        if step == 0:
            dq_low = (dq_acc[...] * (HD**-0.5)).astype(BF16)
            grad_normed = part + dot_nt(dq_low, wqkv_ref[:, :width])
            grads = (dot_nn(rows_t, dq_low).astype(BF16), gkv[:, :width].astype(BF16), gkv[:, width:].astype(BF16))
            for i, grad in enumerate(grads):
                for o in range(groups):
                    sources[3 + i][o] = grad[o * rows_up : (o + 1) * rows_up]
                qkv_sums[i].stage1()
        else:
            if step < back:

                @pl.when((seq + 1 < splits) & (seq >= step))
                def _(step=step):
                    halo_copy(step + 1).wait_recv()

                arrived = jnp.where((seq + 1 < splits) & (seq >= step), halo_land[step].astype(F32), 0.0)
                part = part + arrived
            if step + 2 <= back:

                @pl.when(seq >= step + 2)
                def _(step=step):
                    halo_copy(step + 2).wait_send()

            halo_send[(step - 1) % 2] = part.astype(BF16)

            @pl.when(seq >= step)
            def _(step=step):
                halo_copy(step).start()

            if index == back - 1:
                down.stage3()
    up.stage3()
    out_sum.stage3()
    for summer in qkv_sums:
        summer.stage2()
    wide = (down, up, out_sum)
    for summer in wide:
        summer.turn(1)

    @pl.when(seq + 1 < splits)
    def _():
        halo_copy(1).wait_recv()

    grad_normed = grad_normed + jnp.where(seq + 1 < splits, halo_land[0].astype(F32), 0.0)
    normal, scale = norm_stats(xwin[own_rows, :].astype(F32))
    small_ref[0, 0:1, :] = jnp.sum(grad_normed * normal, axis=0, keepdims=True)
    small_ref[0, 1:2, :] = jnp.sum(grad_normed, axis=0, keepdims=True)
    small_ref[0, 4:8, :] = jnp.zeros((4, width), F32)
    dd_all = dd[...].reshape(H, dd.shape[-1])
    dd_hi = dd_all.astype(BF16)
    dd_mid = (dd_all - dd_hi.astype(F32)).astype(BF16)
    small_ref[0, 8:16, :] = jnp.zeros((8, width), F32)
    small_ref[0, 8:16, :NBK] = dot_nt(dd_hi, hot_ref[...]) + dot_nt(dd_mid, hot_ref[...])
    small = SmallSummer(small_ref, small_land, small_sems)
    small.plane()
    dx = (dres_ref[...] + norm_back(grad_normed * gains_ref[0:1, :], normal, scale)).astype(BF16)
    for o in range(groups):
        slots[1, o] = dx[o * length : (o + 1) * length]
    send_back(1)
    for turn in range(2, down.rounds + 1):
        for summer in wide:
            summer.turn(turn)
    for summer in qkv_sums:
        summer.stage3()
    small.take()
    small.along()
    for turn in reversed(range(1, down.rounds)):
        for summer in wide:
            summer.turn_back(turn)
    for summer in summers:
        summer.stage4()
    for summer in wide:
        summer.turn_back(0)
    small.take()
    small_out[...] = small_ref[2]
    for summer in summers:
        summer.finish()
    small.finish()
    for which in range(2):
        ret_own(which).wait()
        for step in range(1, groups):
            ret_copy(which, step).wait()
    for gather in gathers:
        gather.finish()
    for copy in few:
        copy.wait_send()
    for step in range(groups):
        pl.when(seq + 1 < splits)(piece_copy(step).wait_send)
    for step in range(2, back + 1):

        @pl.when((seq + 1 < splits) & (seq + 1 >= step))
        def _(step=step):
            row_copy(step).wait_send()
    for step in range(1, min(back, 2) + 1):

        @pl.when(seq >= step)
        def _(step=step):
            halo_copy(step).wait_send()


def layer(back, tokens_in, cotangent, deal, lengths, buckets, vectors, rel, wqkv, wout, wup, wdown):
    splits, groups = lax.axis_size("seq"), lax.axis_size("dp")
    tokens, width = tokens_in.shape
    length = tokens // groups
    per_chunk = tokens // QB
    maxlen = buckets.shape[0]
    window, reach = (back + 1) * tokens, back * tokens + 2 * QB
    wide = min(2, back) * per_chunk
    span = min(wide + per_chunk - 1, reach // QB - 1) * QB
    grads = [wdown.shape[0], wup.shape[0] * wup.shape[1] // width, *[width // groups] * 4]
    out_shapes, more, sources = [], [], []
    for height in grads:
        shape = (groups, height, width)
        out, scratch = summer_shapes(shape, BF16, splits)
        sources.append(pltpu.VMEM(shape, BF16))
        out_shapes.append(out)
        more += scratch
    out_shapes.append(jax.ShapeDtypeStruct((16, width), F32))
    out_shapes += [jax.ShapeDtypeStruct((groups, length, width), BF16)] * 2
    small_copies = (groups - 1) + (splits - 1)
    scratch = sources + more + [
        pltpu.VMEM((4, 16, width), F32),
        pltpu.VMEM((small_copies, 16, width), F32),
        pltpu.SemaphoreType.DMA((2, small_copies)),
        pltpu.VMEM((2, groups, length, width), BF16),
        pltpu.SemaphoreType.DMA((2, 2, groups - 1)),
        pltpu.SemaphoreType.DMA((2,)),
        pltpu.VMEM((min(back, 2), tokens, width), BF16),
        pltpu.VMEM((back, tokens, width), BF16),
        pltpu.SemaphoreType.DMA((2, back)),
        pltpu.VMEM((tokens, width), F32),
        pltpu.VMEM((tokens, width), BF16),
        pltpu.VMEM((H, tokens, PAIR), BF16),
        pltpu.VMEM((H, tokens, PAIR), BF16),
        pltpu.VMEM((width, tokens), BF16),
        pltpu.VMEM((width, tokens), BF16),
        pltpu.VMEM((QB, span), F32),
        pltpu.VMEM((2 if span <= 1024 else 1, QB, span), F32),
        pltpu.VMEM((wide * QB, PAIR), BF16),
        pltpu.VMEM((wide * QB, PAIR), BF16),
        pltpu.VMEM((H // 2, 2, reach), F32),
        pltpu.VMEM((tokens, width), F32),
        pltpu.VMEM((PAIR, tokens), F32),
        pltpu.VMEM((PAIR, tokens), F32),
        pltpu.VMEM((tokens, 2 * width), BF16),
        pltpu.VMEM((width, 2 * width), F32),
        pltpu.VMEM((window, width), BF16),
        pltpu.VMEM((tokens, width), BF16),
        pltpu.VMEM((width, 3 * width), BF16),
        pltpu.VMEM((width, width), BF16),
        pltpu.VMEM((width, wup.shape[1]), BF16),
        pltpu.VMEM((wup.shape[1], width), BF16),
        pltpu.SemaphoreType.DMA((4, 2, max(8, groups - 1))),
        pltpu.SemaphoreType.DMA((4,)),
        pltpu.SemaphoreType.DMA((2, 2, groups - 1)),
        pltpu.SemaphoreType.DMA((2, back)),
        pltpu.SemaphoreType.DMA((2, groups)),
        pltpu.VMEM((groups, 16, PAIR), F32),
        pltpu.SemaphoreType.DMA((2, groups - 1)),
        pltpu.VMEM((8, width), F32),
        pltpu.VMEM((H // 2, 2, reach), F32),
        pltpu.VMEM((tokens, width), BF16),
        pltpu.VMEM((window, width), BF16),
        pltpu.VMEM((window, width), BF16),
        pltpu.VMEM((tokens, width), BF16),
        pltpu.VMEM((tokens, width), F32),
        pltpu.VMEM((16, PAIR), F32),
        pltpu.VMEM((NBK, PAIR), F32),
        pltpu.VMEM((NBK, reach), BF16),
        pltpu.VMEM((tokens, PAIR), BF16),
        pltpu.VMEM((window, PAIR), BF16),
    ]
    vmem, smem = pl.BlockSpec(memory_space=pltpu.VMEM), pl.BlockSpec(memory_space=pltpu.SMEM)
    return pl.pallas_call(
        functools.partial(layer_kernel, back, maxlen),
        in_specs=[vmem] * 2 + [smem] * 2 + [vmem] * (2 + len(vectors)) + [pl.BlockSpec(memory_space=pl.ANY)] * 4,
        out_specs=[vmem] * (len(out_shapes) - 2) + [pl.BlockSpec(memory_space=pl.ANY)] * 2,
        out_shape=out_shapes,
        scratch_shapes=scratch,
        compiler_params=pltpu.CompilerParams(collective_id=1, has_side_effects=True, vmem_limit_bytes=VMEM_LIMIT),
        name="layer",
    )(tokens_in, cotangent, deal, lengths, buckets.reshape(-1, PAIR), *vectors, rel, wqkv, wout, wup, wdown)


def finish_kernel(deal_ref, down, up, out, q, k, v, small, ret_out, ret_grad, *outs):
    o_out, o_grad, o_qkv, o_wout, o_up, o_down, *o_vectors, o_rel = outs
    length = ret_out.shape[1]
    for g in range(ret_out.shape[0]):
        piece = deal_ref[0, g]
        o_out[pl.ds(g * length, length), :] = ret_out[piece]
        o_grad[pl.ds(g * length, length), :] = ret_grad[piece]
    def collect(source, rows):
        parts, height, cols = source.shape
        if height == rows:
            return add_low(*[source[t] for t in range(parts)])
        return source[...].reshape(-1, cols).astype(F32)

    width = down.shape[2]
    for source, target in ((down, o_down), (up, o_up), (out, o_wout)):
        height, columns = target.shape[0], target.shape[1] // width
        value = collect(source, height * columns)
        for c in range(columns):
            target[:, c * width : (c + 1) * width] = value[c * height : (c + 1) * height]
    for c, source in enumerate((q, k, v)):
        o_qkv[:, c * width : (c + 1) * width] = collect(source, o_qkv.shape[0])
    dp, groups = lax.axis_index("dp"), lax.axis_size("dp")
    for i, target in enumerate(o_vectors):
        size = target.shape[0]
        value = small[i : i + 1, :size]
        for o in range(1, groups):
            value = jnp.where(dp == o, small[i : i + 1, o * size : (o + 1) * size], value)
        target[...] = value.reshape(size)
    levels = small[8 : 8 + H, :PAIR].T
    size = o_rel.shape[0]
    value = levels[:size, :H]
    for o in range(1, groups):
        value = jnp.where(dp == o, levels[o * size : (o + 1) * size, :H], value)
    o_rel[...] = value


def finish(deal, sums, returned, shapes):
    return pl.pallas_call(
        finish_kernel,
        in_specs=[pl.BlockSpec(memory_space=pltpu.SMEM)] + [pl.BlockSpec(memory_space=pltpu.VMEM)] * 9,
        out_specs=[pl.BlockSpec(memory_space=pltpu.VMEM)] * len(shapes),
        out_shape=shapes,
        compiler_params=pltpu.CompilerParams(vmem_limit_bytes=VMEM_LIMIT),
        name="finish",
    )(deal, *sums, *returned)


def shards(
    tokens,
    cotangent,
    deal,
    lengths,
    buckets,
    ln1_gain,
    ln1_bias,
    w_qkv,
    w_out,
    rel_bias,
    ln2_gain,
    ln2_bias,
    w_up,
    w_down,
):
    tok_dev = tokens.shape[0]
    back = -(-buckets.shape[0] // tok_dev)
    *sums, small_total, back_out, back_grad = layer(
        back, tokens, cotangent, deal, lengths, buckets, (ln1_gain, ln1_bias, ln2_gain, ln2_bias), rel_bias,
        w_qkv, w_out, w_up, w_down,
    )
    output, grad_tokens, total_qkv, total_out, total_up, total_down, g_one, b_one, g_two, b_two, total_rel = finish(
        deal,
        [*sums, small_total],
        [back_out, back_grad],
        [jax.ShapeDtypeStruct(tokens.shape, BF16)] * 2
        + [
            jax.ShapeDtypeStruct(a.shape, F32)
            for a in (w_qkv, w_out, w_up, w_down, ln1_gain, ln1_bias, ln2_gain, ln2_bias, rel_bias)
        ],
    )
    return (
        output, grad_tokens, g_one, b_one, total_qkv, total_out, total_rel, g_two, b_two, total_up, total_down,
    )


def solution(mesh):
    by_all, by_dp = P(("seq", "dp"), None), P("dp", None)
    return jax.shard_map(
        shards,
        mesh=mesh,
        in_specs=(
            by_all, by_all, by_all, by_dp, P(), P("dp"), P("dp"), by_dp, by_dp, by_dp, P("dp"), P("dp"), by_dp, by_dp,
        ),
        out_specs=(by_all, by_all, P("dp"), P("dp"), by_dp, by_dp, by_dp, P("dp"), P("dp"), by_dp, by_dp),
        check_vma=False,
    )
```
